32 devices in a mesh: region: 32 (over z, y, x, core).
Axes of the slice: x: 2, y: 2, z: 4, core: 2. Of those that a mesh axis runs over, the one named last changes fastest.
Arguments:
- edge_feat: bfloat16 [65536, 32], P('region'), may hold values from -6 to 6
- w_in: bfloat16 [32, 512], replicated, may hold values from -1 to 1
- b_in: float32 [512], replicated, may hold values from -3 to 3
- w_out: float32 [512], replicated, may hold values from -0.25 to 0.25
- targets: int32 [65536], P('region'), may hold values from 0 to 639, as said below
- edge_live: int32 [65536], P('region'), may hold values from 0 to 1, as said below
- boundary_rows: int32 [4096], P('region'), may hold values from 0 to 511
- dest_nodes: int32 [32], replicated, may hold values from 0 to 16383
- anchor_mass: float32 [32, 16384], P(None, 'region'), may hold values from 0.001 to 0.06
- prior_value: float32 [32, 16384], P(None, 'region'), may hold values from -353 to 3
- demo_counts: int32 [65536], P('region'), may hold values from 0 to 3
Outputs:
- value: float32 [32, 16384], P(None, 'region')
- visits: float32 [32, 16384], P(None, 'region')
- grad_w_in: float32 [32, 512], replicated
- grad_w_out: float32 [512], replicated
The draws below stay inside these ranges and needn't reach their ends.
Inputs may be any that keep to these rules, and one draw needn't show every extreme that they name: `targets`: values below 512 are the region's own nodes, the others its extended boundary slots. `edge_live`: the first slot (k = 0) of every node is live.
All inputs are finite; a program needn't handle non-finite values.
Results may differ from the reference program's by a relative error of at most 0.0003.
Values sent between devices are 32-bit elements; how exact they have to be, the bound alone decides.
No kernel may reach another device: no remote copies, remote signals or barrier semaphores. Data moves between devices by JAX's collectives and lax.ppermute only.
A program may use at most 64 MiB of HBM per device.

```python
import math
import jax
import jax.numpy as jnp
from jax import lax

NODE_DEV = 512
DEG = 4
BND = 64
DEST = 32
FEAT = 32
HID = 512
SWEEPS = 4
NODES = 16384
EDGES = 65536
N_REGION = 32


def draw_targets(key, part):
    key = jax.random.fold_in(key, 11)
    key_kind, key_inner, key_rim = jax.random.split(key, 3)
    choose = jax.random.randint(key_kind, (EDGES,), 0, 4)
    inner = jax.random.randint(key_inner, (EDGES,), 0, NODE_DEV)
    rim_slot = NODE_DEV + jax.random.randint(key_rim, (EDGES,), 0, 2 * BND)
    return jnp.where(choose < 3, inner, rim_slot).astype(jnp.int32)


def draw_edge_live(key, part):
    key = jax.random.fold_in(key, 23)
    degree_slot = jnp.arange(EDGES, dtype=jnp.int32) // NODE_DEV % DEG
    coin_flip = jax.random.randint(key, (EDGES,), 0, 4)
    return jnp.where((degree_slot == 0) | (coin_flip > 0), 1, 0).astype(jnp.int32)


def draw_prior_value(key, part):
    key = jax.random.fold_in(key, 37)
    key_offset, key_jitter = jax.random.split(key)
    offset = jax.random.uniform(key_offset, (DEST, 1), jnp.float32, -8.0, 0.0)
    jitter = jax.random.uniform(key_jitter, (DEST, NODES), jnp.float32, -3.0, 3.0)
    return (offset + jitter).astype(jnp.float32)


def set_ends(result, rng, least, largest):
    place = [jax.random.randint(jax.random.fold_in(rng, axis), (), 0, length) for axis, length in enumerate(result.shape)]
    widest = result.shape.index(max(result.shape))
    neighbour = place[:widest] + [(place[widest] + 1) % result.shape[widest]] + place[widest + 1:]
    return result.at[tuple(place)].set(least).at[tuple(neighbour)].set(largest)


def block_scale(key, dims, shards, low, top_value):
    level, own = 1.0, jax.random.fold_in(key, 6)
    for position, blocks in shards:
        draws = jnp.exp(jax.random.uniform(jax.random.fold_in(own, position), (blocks,), jnp.float32, low / len(shards), top_value / len(shards)))
        level = level * jnp.repeat(draws, dims[position] // blocks).reshape([-1 if axis == position else 1 for axis in range(len(dims))])
    return level


def bell_draw(own_key, dims, spread, most, shards=(), kind=jnp.bfloat16):
    values = jax.random.normal(own_key, dims, jnp.float32) * spread
    if len(shards) > 0:
        values = block_scale(own_key, dims, shards, -0.22, 0.18) * values
    return jnp.clip(values, min=-most, max=most).astype(kind)


def setup_inputs(seed: int = 0) -> dict:
    keys = jax.random.split(jax.random.key(seed), 12)
    edge_feat = bell_draw(keys[0], (EDGES, FEAT), 1.0, 6.0, ((0, 32),))
    w_in = bell_draw(keys[1], (FEAT, HID), FEAT ** -0.5, 1.0)
    b_in = bell_draw(keys[2], (HID,), 0.5, 3.0, (), jnp.float32)
    w_out = bell_draw(keys[3], (HID,), HID ** -0.5, 0.25, (), jnp.float32)
    targets = draw_targets(jax.random.fold_in(keys[11], 71), 0)
    edge_live = draw_edge_live(jax.random.fold_in(keys[11], 71), 0)
    boundary_rows = set_ends(jax.random.randint(keys[6], (2 * BND * N_REGION,), 0, NODE_DEV), jax.random.fold_in(keys[6], 1), 0, NODE_DEV - 1).astype(jnp.int32)
    dest_nodes = set_ends(jax.random.randint(keys[7], (DEST,), 0, NODES), jax.random.fold_in(keys[7], 1), 0, NODES - 1).astype(jnp.int32)
    anchor_mass = jnp.clip(jnp.exp(math.log(0.06) - 4.0943445 * jax.random.uniform(keys[8], (DEST, NODES), jnp.float32) ** block_scale(keys[8], (DEST, NODES), ((1, 32),), -0.2, 0.2)), 0.001, 0.06)
    prior_value = draw_prior_value(jax.random.fold_in(keys[11], 71), 0)
    demo_counts = set_ends(jax.random.randint(keys[10], (EDGES,), 0, 4), jax.random.fold_in(keys[10], 1), 0, 3).astype(jnp.int32)
    return {"edge_feat": edge_feat, "w_in": w_in, "b_in": b_in, "w_out": w_out, "targets": targets, "edge_live": edge_live, "boundary_rows": boundary_rows, "dest_nodes": dest_nodes, "anchor_mass": anchor_mass, "prior_value": prior_value, "demo_counts": demo_counts}


NEG_FILL = -1e+30

def edge_logits(feat_rows, w_in, b_in, w_out):
    pre_act = jnp.dot(feat_rows, w_in, preferred_element_type=jnp.float32) + b_in
    hidden = jnp.tanh(pre_act)
    logits = jnp.dot(hidden, w_out, precision=lax.Precision.HIGHEST)
    return (hidden, logits)

def masked_scores(extended, target_idx, live_mask, reward):
    scores = extended[:, target_idx] + reward[None]
    return jnp.where(live_mask[None], scores, NEG_FILL)

def soft_maximum(masked):
    row_top = lax.optimization_barrier(jnp.max(masked, axis=1))
    exp_total = lax.optimization_barrier(jnp.sum(jnp.exp(masked - row_top[:, None, :]), axis=1))
    return row_top + jnp.log(exp_total)

def policy_of(extended, target_idx, live_mask, reward, dest_mask):
    masked = masked_scores(extended, target_idx, live_mask, reward)
    log_total = soft_maximum(masked)
    keep_flow = jnp.where(dest_mask, 0.0, 1.0)
    return jnp.exp(masked - log_total[:, None, :]) * keep_flow[:, None, :]

def pick_rows(values, row_lists):
    value_dims = (values.shape[0], values.shape[1], row_lists.shape[1])
    return jnp.take_along_axis(values, jnp.broadcast_to(row_lists[:, None, :], value_dims), axis=2)

def extend_all(values, left_rows, right_rows):
    give_left = pick_rows(values, left_rows)
    give_right = pick_rows(values, right_rows)
    from_left = jnp.roll(give_right, 1, axis=0)
    from_right = jnp.roll(give_left, -1, axis=0)
    return jnp.concatenate([values, from_left, from_right], axis=2)

def add_rows(field, row_list, amounts):
    return field.at[:, row_list].add(amounts)

def reference(edge_feat, w_in, b_in, w_out, targets, edge_live, boundary_rows, dest_nodes, anchor_mass, prior_value, demo_counts):
    feat_blocks = edge_feat.reshape(N_REGION, DEG * NODE_DEV, FEAT)

    def reward_block(feat_rows):
        hidden, logits = edge_logits(feat_rows, w_in, b_in, w_out)
        return logits
    logits_all = lax.map(reward_block, feat_blocks)
    reward_all = (-jax.nn.softplus(logits_all)).reshape(N_REGION, DEG, NODE_DEV)
    target_all = targets.reshape(N_REGION, DEG, NODE_DEV)
    live_all = edge_live.reshape(N_REGION, DEG, NODE_DEV) > 0
    rim_all = boundary_rows.reshape(N_REGION, 2, BND)
    left_rows = rim_all[:, 0]
    right_rows = rim_all[:, 1]
    node_ids = jnp.arange(NODES, dtype=jnp.int32).reshape(N_REGION, NODE_DEV)
    at_dest = node_ids[:, None, :] == dest_nodes[None, :, None]
    values = prior_value.reshape(DEST, N_REGION, NODE_DEV).transpose(1, 0, 2)
    anchor = anchor_mass.reshape(DEST, N_REGION, NODE_DEV).transpose(1, 0, 2)

    def bellman_block(items):
        extended, target_idx, live_mask, reward, dest_mask = items
        masked = masked_scores(extended, target_idx, live_mask, reward)
        return jnp.where(dest_mask, 0.0, soft_maximum(masked))
    last_ext = values
    for sweep in range(SWEEPS):
        last_ext = extend_all(values, left_rows, right_rows)
        values = lax.map(bellman_block, (last_ext, target_all, live_all, reward_all, at_dest))

    def push_block(items):
        extended, target_idx, live_mask, reward, dest_mask, visits = items
        policy = policy_of(extended, target_idx, live_mask, reward, dest_mask)
        outflow = visits[:, None, :] * policy
        arrivals = jnp.zeros((DEST, NODE_DEV + 2 * BND), jnp.float32)
        return arrivals.at[:, target_idx.reshape(-1)].add(outflow.reshape(DEST, -1))
    visits = anchor
    for sweep in range(SWEEPS):
        arrivals = lax.map(push_block, (last_ext, target_all, live_all, reward_all, at_dest, visits))
        to_left = arrivals[:, :, NODE_DEV:NODE_DEV + BND]
        to_right = arrivals[:, :, NODE_DEV + BND:]
        from_left = jnp.roll(to_right, 1, axis=0)
        from_right = jnp.roll(to_left, -1, axis=0)
        visits = anchor + arrivals[:, :, :NODE_DEV]
        visits = jax.vmap(add_rows)(visits, left_rows, from_left)
        visits = jax.vmap(add_rows)(visits, right_rows, from_right)
    count_blocks = demo_counts.reshape(N_REGION, DEG * NODE_DEV)

    def grad_block(items):
        feat_rows, extended, target_idx, live_mask, dest_mask, visit_rows, counts = items
        hidden, logits = edge_logits(feat_rows, w_in, b_in, w_out)
        reward = (-jax.nn.softplus(logits)).reshape(DEG, NODE_DEV)
        policy = policy_of(extended, target_idx, live_mask, reward, dest_mask)
        expected = lax.optimization_barrier(jnp.sum(visit_rows[:, None, :] * policy, axis=0)).reshape(-1)
        residual_gap = counts.astype(jnp.float32) - expected
        logit_grad = -residual_gap * jax.nn.sigmoid(logits)
        out_grad = jnp.dot(logit_grad, hidden, precision=lax.Precision.HIGHEST)
        hidden_grad = (logit_grad[:, None] * w_out[None, :] * (1.0 - hidden * hidden)).astype(jnp.bfloat16)
        in_grad = lax.dot_general(feat_rows, hidden_grad, (((0,), (0,)), ((), ())), preferred_element_type=jnp.float32)
        return (in_grad, out_grad)
    in_all, out_all = lax.map(grad_block, (feat_blocks, last_ext, target_all, live_all, at_dest, visits, count_blocks))
    grad_scale = 1.0 / math.sqrt(EDGES)
    value_out = values.transpose(1, 0, 2).reshape(DEST, NODES)
    visit_out = visits.transpose(1, 0, 2).reshape(DEST, NODES)
    return (value_out, visit_out, lax.optimization_barrier(jnp.sum(in_all, axis=0)) * grad_scale, lax.optimization_barrier(jnp.sum(out_all, axis=0)) * grad_scale)
```

```python
import math

import jax
import jax.numpy as jnp
from jax import lax
from jax.sharding import PartitionSpec as P

SWEEPS = 4


NEG_FILL = -1e30


def with_halo(cells, sides, width):
    for axis, dim in sides:
        count = lax.axis_size(axis)
        head = lax.slice_in_dim(cells, 0, width, axis=dim)
        tail = lax.slice_in_dim(cells, cells.shape[dim] - width, cells.shape[dim], axis=dim)
        cells = jnp.concatenate(
            [
                lax.ppermute(tail, axis, [(i, (i + 1) % count) for i in range(count)]),
                cells,
                lax.ppermute(head, axis, [((i + 1) % count, i) for i in range(count)]),
            ],
            axis=dim,
        )
    return cells


def sum_over(cells, axis, count):
    if count & (count - 1):
        return lax.psum(cells, axis)

    def partner(block, step):
        return lax.ppermute(block, axis, [(i, i ^ step) for i in range(count)])

    stride = 1
    while stride < count:
        if stride > 1 and stride * 4 <= count:
            near = partner(cells, stride)
            far = partner(cells, 2 * stride)
            across = partner(cells, 3 * stride)
            cells = (cells + near) + (far + across)
            stride *= 4
        else:
            cells = cells + partner(cells, stride)
            stride *= 2
    return cells


def shards(
    edge_feat,
    w_in,
    b_in,
    w_out,
    targets,
    edge_live,
    boundary_rows,
    dest_nodes,
    anchor_mass,
    prior_value,
    demo_counts,
):
    node_count = prior_value.shape[1]
    dest_count = prior_value.shape[0]
    rim_width = boundary_rows.shape[0] // 2
    degree = targets.shape[0] // node_count
    region_pos = lax.axis_index("region")
    node_ids = region_pos * node_count + jnp.arange(node_count, dtype=jnp.int32)
    at_dest = node_ids[None, :] == dest_nodes[:, None]
    keep_flow = jnp.where(at_dest, 0.0, 1.0)
    target_idx = targets.reshape(degree, node_count)
    live_mask = edge_live.reshape(degree, node_count) > 0
    left_rows = boundary_rows[:rim_width]
    right_rows = boundary_rows[rim_width:]
    pre_act = jnp.dot(edge_feat, w_in, preferred_element_type=jnp.float32) + b_in
    hidden = jnp.tanh(pre_act)
    logits = jnp.dot(hidden, w_out, precision=lax.Precision.HIGHEST)
    reward = (-jax.nn.softplus(logits)).reshape(degree, node_count)
    values = prior_value
    masked = None
    log_total = None
    for sweep in range(SWEEPS):
        outgoing = jnp.concatenate([values[:, left_rows], values[:, right_rows]], axis=1)
        extend_padded = with_halo(outgoing, (("region", 1),), rim_width)
        extended = jnp.concatenate(
            [values, extend_padded[:, :rim_width], extend_padded[:, 3 * rim_width :]], axis=1
        )
        masked = jnp.where(live_mask[None], extended[:, target_idx] + reward[None], NEG_FILL)
        row_top = jnp.max(masked, axis=1)
        exp_total = jnp.sum(jnp.exp(masked - row_top[:, None, :]), axis=1)
        log_total = row_top + jnp.log(exp_total)
        values = jnp.where(at_dest, 0.0, log_total)
    policy = jnp.exp(masked - log_total[:, None, :]) * keep_flow[:, None, :]
    flat_targets = target_idx.reshape(-1)
    visits = anchor_mass
    for sweep in range(SWEEPS):
        outflow = (visits[:, None, :] * policy).reshape(dest_count, -1)
        arrivals = (
            jnp.zeros((dest_count, node_count + 2 * rim_width), jnp.float32)
            .at[:, flat_targets]
            .add(outflow)
        )
        padded = with_halo(arrivals[:, node_count:], (("region", 1),), rim_width)
        visits = anchor_mass + arrivals[:, :node_count]
        visits = visits.at[:, left_rows].add(padded[:, :rim_width])
        visits = visits.at[:, right_rows].add(padded[:, 3 * rim_width :])
    expected = jnp.sum(visits[:, None, :] * policy, axis=0).reshape(-1)
    residual_gap = demo_counts.astype(jnp.float32) - expected
    logit_grad = -residual_gap * jax.nn.sigmoid(logits)
    out_grad = jnp.dot(logit_grad, hidden, precision=lax.Precision.HIGHEST)
    hidden_grad = (logit_grad[:, None] * w_out[None, :] * (1.0 - hidden * hidden)).astype(
        jnp.bfloat16
    )
    in_grad = lax.dot_general(
        edge_feat, hidden_grad, (((0,), (0,)), ((), ())), preferred_element_type=jnp.float32
    )
    region_count = lax.axis_size("region")
    grad_scale = 1.0 / math.sqrt(targets.shape[0] * region_count)
    packed = jnp.concatenate([in_grad, out_grad[None]], axis=0)
    total = sum_over(packed, "region", region_count) * grad_scale
    return (values, visits, total[:-1], total[-1])


def solution(mesh):
    placed = (
        P("region", None),
        P(),
        P(),
        P(),
        P("region"),
        P("region"),
        P("region"),
        P(),
        P(None, "region"),
        P(None, "region"),
        P("region"),
    )
    return jax.shard_map(
        shards,
        mesh=mesh,
        in_specs=placed,
        out_specs=(P(None, "region"), P(None, "region"), P(), P()),
        check_vma=False,
    )
```

```python
import functools
import math

import jax
import jax.numpy as jnp
from jax import lax
from jax.experimental import pallas as pl
from jax.experimental.pallas import tpu as pltpu
from jax.sharding import PartitionSpec as P

SWEEPS = 4


NEG_FILL = -1e30


def with_halo(cells, sides, width):
    for axis, dim in sides:
        count = lax.axis_size(axis)
        head = lax.slice_in_dim(cells, 0, width, axis=dim)
        tail = lax.slice_in_dim(cells, cells.shape[dim] - width, cells.shape[dim], axis=dim)
        cells = jnp.concatenate(
            [
                lax.ppermute(tail, axis, [(i, (i + 1) % count) for i in range(count)]),
                cells,
                lax.ppermute(head, axis, [((i + 1) % count, i) for i in range(count)]),
            ],
            axis=dim,
        )
    return cells


def sum_over(cells, axis, count):
    if count & (count - 1):
        return lax.psum(cells, axis)

    def partner(block, step):
        return lax.ppermute(block, axis, [(i, i ^ step) for i in range(count)])

    stride = 1
    while stride < count:
        if stride > 1 and stride * 4 <= count:
            near = partner(cells, stride)
            far = partner(cells, 2 * stride)
            across = partner(cells, 3 * stride)
            cells = (cells + near) + (far + across)
            stride *= 4
        else:
            cells = cells + partner(cells, stride)
            stride *= 2
    return cells


def ring_sweeps(
    edge_feat,
    w_in,
    b_in,
    w_out,
    targets,
    edge_live,
    boundary_rows,
    dest_nodes,
    anchor_mass,
    prior_value,
    demo_counts,
):
    node_count = prior_value.shape[1]
    dest_count = prior_value.shape[0]
    rim_width = boundary_rows.shape[0] // 2
    degree = targets.shape[0] // node_count
    region_pos = lax.axis_index("region")
    node_ids = region_pos * node_count + jnp.arange(node_count, dtype=jnp.int32)
    at_dest = node_ids[None, :] == dest_nodes[:, None]
    keep_flow = jnp.where(at_dest, 0.0, 1.0)
    target_idx = targets.reshape(degree, node_count)
    live_mask = edge_live.reshape(degree, node_count) > 0
    left_rows = boundary_rows[:rim_width]
    right_rows = boundary_rows[rim_width:]
    pre_act = jnp.dot(edge_feat, w_in, preferred_element_type=jnp.float32) + b_in
    hidden = jnp.tanh(pre_act)
    logits = jnp.dot(hidden, w_out, precision=lax.Precision.HIGHEST)
    reward = (-jax.nn.softplus(logits)).reshape(degree, node_count)
    values = prior_value
    masked = None
    log_total = None
    for sweep in range(SWEEPS):
        outgoing = jnp.concatenate([values[:, left_rows], values[:, right_rows]], axis=1)
        extend_padded = with_halo(outgoing, (("region", 1),), rim_width)
        extended = jnp.concatenate(
            [values, extend_padded[:, :rim_width], extend_padded[:, 3 * rim_width :]], axis=1
        )
        masked = jnp.where(live_mask[None], extended[:, target_idx] + reward[None], NEG_FILL)
        row_top = jnp.max(masked, axis=1)
        exp_total = jnp.sum(jnp.exp(masked - row_top[:, None, :]), axis=1)
        log_total = row_top + jnp.log(exp_total)
        values = jnp.where(at_dest, 0.0, log_total)
    policy = jnp.exp(masked - log_total[:, None, :]) * keep_flow[:, None, :]
    flat_targets = target_idx.reshape(-1)
    visits = anchor_mass
    for sweep in range(SWEEPS):
        outflow = (visits[:, None, :] * policy).reshape(dest_count, -1)
        arrivals = (
            jnp.zeros((dest_count, node_count + 2 * rim_width), jnp.float32)
            .at[:, flat_targets]
            .add(outflow)
        )
        padded = with_halo(arrivals[:, node_count:], (("region", 1),), rim_width)
        visits = anchor_mass + arrivals[:, :node_count]
        visits = visits.at[:, left_rows].add(padded[:, :rim_width])
        visits = visits.at[:, right_rows].add(padded[:, 3 * rim_width :])
    expected = jnp.sum(visits[:, None, :] * policy, axis=0).reshape(-1)
    residual_gap = demo_counts.astype(jnp.float32) - expected
    logit_grad = -residual_gap * jax.nn.sigmoid(logits)
    out_grad = jnp.dot(logit_grad, hidden, precision=lax.Precision.HIGHEST)
    hidden_grad = (logit_grad[:, None] * w_out[None, :] * (1.0 - hidden * hidden)).astype(
        jnp.bfloat16
    )
    in_grad = lax.dot_general(
        edge_feat, hidden_grad, (((0,), (0,)), ((), ())), preferred_element_type=jnp.float32
    )
    region_count = lax.axis_size("region")
    grad_scale = 1.0 / math.sqrt(targets.shape[0] * region_count)
    packed = jnp.concatenate([in_grad, out_grad[None]], axis=0)
    total = sum_over(packed, "region", region_count) * grad_scale
    return (values, visits, total[:-1], total[-1])


LANES = 128
MIB = 1024 * 1024


def along(table, index):
    return jnp.take_along_axis(table, index, axis=1, mode="promise_in_bounds")


def spread(row, count):
    return jnp.broadcast_to(row, (count, row.shape[1]))


def lane_iota(rows):
    return lax.broadcasted_iota(jnp.int32, (rows, LANES), 1)


def row_iota(rows):
    return lax.broadcasted_iota(jnp.int32, (rows, LANES), 0)


def contract_lanes(left, right):
    return lax.dot_general(
        left.astype(jnp.bfloat16),
        right.astype(jnp.bfloat16),
        (((1,), (1,)), ((), ())),
        preferred_element_type=jnp.float32,
    )


def three_parts(cells):
    high = cells.astype(jnp.bfloat16)
    rest = cells - high.astype(jnp.float32)
    middle = rest.astype(jnp.bfloat16)
    low = (rest - middle.astype(jnp.float32)).astype(jnp.bfloat16)
    return high, middle, low


def prefix_and_total(cells, steps):
    rows = cells.shape[0]
    parts = jnp.concatenate(three_parts(cells), axis=0)
    sums = jnp.dot(parts, steps, preferred_element_type=jnp.float32)
    sums = (sums[:rows] + sums[rows : 2 * rows]) + sums[2 * rows :]
    return sums[:, :LANES], sums[:, LANES:]


def step_matrix():
    src = lax.broadcasted_iota(jnp.int32, (LANES, 2 * LANES), 0)
    dst = lax.broadcasted_iota(jnp.int32, (LANES, 2 * LANES), 1)
    return jnp.where(dst > src, 1.0, 0.0).astype(jnp.bfloat16)


def earlier_equal(keys):
    lane = lane_iota(keys.shape[0])
    found = jnp.zeros(keys.shape, jnp.float32)
    for shift in range(1, LANES):
        same = (pltpu.roll(keys, shift, 1) == keys) & (lane >= shift)
        found = found + jnp.where(same, 1.0, 0.0)
    return found


def sort_plan(keys, earlier, steps):
    rows = keys.shape[0]
    low, high = keys & (LANES - 1), keys >> 7
    column = row_iota(LANES)
    band = row_iota(8)
    hists = []
    for c in range(rows):
        in_band = jnp.where(spread(high[c : c + 1], 8) == band, 1.0, 0.0)
        in_lane = jnp.where(spread(low[c : c + 1], LANES) == column, 1.0, 0.0)
        hists.append(contract_lanes(in_band, in_lane))
    total = hists[0]
    for c in range(1, rows):
        total = total + hists[c]
    inside, sums = prefix_and_total(total, steps)
    before = jnp.zeros((1, LANES), jnp.float32)
    starts = []
    for band_row in range(8):
        starts.append(inside[band_row : band_row + 1] + before)
        before = before + sums[band_row : band_row + 1]
    start = jnp.concatenate(starts, axis=0)
    ends = start + total
    ranks = []
    for c in range(rows):
        found = along(start, spread(low[c : c + 1], 8))
        found = jnp.where(spread(high[c : c + 1], 8) == band, found, 0.0)
        ranks.append(jnp.sum(found, axis=0, keepdims=True) + earlier[c : c + 1])
        start = start + hists[c]
    rank = jnp.concatenate(ranks, axis=0).astype(jnp.int32) if rows > 1 else ranks[0].astype(jnp.int32)
    rank_low, rank_high = rank & (LANES - 1), rank >> 7
    out_rows = max(rows, 8)
    out_band = row_iota(out_rows)
    lane = lane_iota(out_rows).astype(jnp.float32)
    order = jnp.zeros((out_rows, LANES), jnp.float32)
    for c in range(rows):
        in_band = spread(rank_high[c : c + 1], out_rows) == out_band
        in_lane = jnp.where(spread(rank_low[c : c + 1], LANES) == column, 1.0, 0.0)
        both = jnp.concatenate(
            [jnp.where(in_band, lane, 0.0), jnp.where(in_band, 1.0, 0.0)], axis=0
        )
        got = contract_lanes(both, in_lane)
        order = order + got[:out_rows] + got[out_rows:] * float(c * LANES)
    return order, ends


def prepare_kernel(
    feat_ref,
    w_in_ref,
    b_in_ref,
    w_out_ref,
    targets_ref,
    live_ref,
    rows_ref,
    prior_ref,
    anchor_ref,
    graph_ref,
    field_ref,
    logits_ref,
    hidden_ref,
    column_ref,
):
    hid = w_in_ref.shape[1]
    edges = feat_ref.shape[0]
    dests, nodes = prior_ref.shape
    chunks = edges // LANES
    node_chunks = nodes // LANES
    for c in range(node_chunks):
        span = pl.ds(c * LANES, LANES)
        field_ref[pl.ds(c, dests, stride=8), :] = prior_ref[:, span]
        field_ref[pl.ds(4 + c, dests, stride=8), :] = anchor_ref[:, span]
    b_col = spread(b_in_ref[...], LANES).T
    w_col = spread(w_out_ref[...], LANES).T
    column_ref[...] = w_col
    w_rows = w_in_ref[...].astype(jnp.float32).T.astype(jnp.bfloat16)
    logit_rows = []
    for c in range(chunks):
        span = pl.ds(c * LANES, LANES)
        pre = lax.dot_general(
            w_rows,
            feat_ref[span, :],
            (((1,), (1,)), ((), ())),
            preferred_element_type=jnp.float32,
        )
        hidden = jnp.tanh(pre + b_col)
        hidden_ref[:, span] = hidden
        logit_rows.append(jnp.sum(hidden * w_col, axis=0, keepdims=True))
    logits = jnp.concatenate(logit_rows, axis=0)
    logits_ref[...] = logits
    reward = -(jnp.maximum(logits, 0.0) + jnp.log1p(jnp.exp(-jnp.abs(logits))))
    reward = jnp.where(live_ref[...] > 0, reward, NEG_FILL)
    steps = step_matrix()
    targets = targets_ref[...]
    rows = rows_ref[...]
    earlier = earlier_equal(jnp.concatenate([targets, spread(rows, 8)], axis=0))
    order, ends = sort_plan(targets, earlier[:chunks], steps)
    rim_order, rim_ends = sort_plan(rows, earlier[chunks : chunks + 1], steps)
    graph_ref[0:16, :] = targets.astype(jnp.float32)
    graph_ref[16:32, :] = reward
    graph_ref[32:48, :] = order
    graph_ref[48:56, :] = ends
    graph_ref[56:60, :] = rim_ends[0:4]
    graph_ref[60:61, :] = rows.astype(jnp.float32)
    graph_ref[61:62, :] = rim_order[0:1]
    graph_ref[62:64, :] = jnp.zeros((2, LANES), jnp.float32)


def sweep_kernel(
    offsets,
    place_ref,
    own_ref,
    other_ref,
    field_ref,
    out_ref,
    graph_ref,
    ext_ref,
    rim_ref,
    policy_ref,
    sorted_ref,
    flow_ref,
    part_ref,
    total_ref,
    copy_sem,
):
    me, dest = place_ref[0], place_ref[1]
    regions = len(offsets)
    half = own_ref.shape[0]
    copies = []
    for spot, offset in enumerate(offsets):
        src = own_ref.at[spot] if spot < half else other_ref.at[spot - half]
        copies.append(
            pltpu.make_async_copy(src, graph_ref.at[me ^ offset], copy_sem.at[spot])
        )
    for copy in copies:
        copy.start()
    for copy in copies:
        copy.wait()
    dest_region, dest_node = dest // 512, dest % 512
    position = (row_iota(8) & 3) * LANES + lane_iota(8)
    band = row_iota(8)
    left_lanes = lane_iota(regions) < LANES // 2
    steps = step_matrix()

    def at_dest(region):
        return position == jnp.where(region == dest_region, dest_node, -1)

    def give_rim(region, values):
        rows = graph_ref[region, 60:61, :].astype(jnp.int32)
        got = along(values, spread(rows & (LANES - 1), 8))
        got = jnp.where(spread(rows >> 7, 8) == band, got, 0.0)
        rim_ref[pl.ds(region, 1), :] = jnp.sum(got, axis=0, keepdims=True)

    def swap_rims(rims):
        turned = pltpu.roll(rims, LANES // 2, 1)
        return jnp.where(
            left_lanes, pltpu.roll(turned, 1, 0), pltpu.roll(turned, regions - 1, 0)
        )

    def take_rims():
        ext_ref[:, 4:5, :] = swap_rims(rim_ref[...]).reshape(regions, 1, LANES)

    def first(region, carry):
        values = field_ref[region][0:4]
        ext_ref[region, 0:4, :] = values
        give_rim(region, jnp.concatenate([values, values], axis=0))
        return carry

    def bellman(last, region, carry):
        target = graph_ref[region, 0:16, :].astype(jnp.int32)
        low, high = target & (LANES - 1), target >> 7
        scores = jnp.zeros((16, LANES), jnp.float32)
        for c in range(5):
            got = along(spread(ext_ref[region, c : c + 1, :], 16), low)
            scores = jnp.where(high == c, got, scores)
        scores = scores + graph_ref[region, 16:32, :]
        near, far = scores[0:8], scores[8:16]
        top = jnp.maximum(near, far)
        top = jnp.maximum(top, pltpu.roll(top, 4, 0))
        total = jnp.exp(near - top) + jnp.exp(far - top)
        total = total + pltpu.roll(total, 4, 0)
        log_total = top + jnp.log(total)
        mask = at_dest(region)
        values = jnp.where(mask, 0.0, log_total)
        if last:
            policy_ref[region, 0:8, :] = jnp.where(mask, 0.0, jnp.exp(near - log_total))
            policy_ref[region, 8:16, :] = jnp.where(mask, 0.0, jnp.exp(far - log_total))
            out_ref[region, 16:20, :] = values[0:4]
        else:
            ext_ref[region, 0:4, :] = values[0:4]
            give_rim(region, values)
        return carry

    def arrange(region, carry):
        order = graph_ref[region, 32:48, :].astype(jnp.int32)
        low, high = order & (LANES - 1), order >> 7
        moved = jnp.zeros((16, LANES), jnp.float32)
        for c in range(16):
            got = along(spread(policy_ref[region, c : c + 1, :], 16), low)
            moved = jnp.where(high == c, got, moved)
        sorted_ref[region] = moved
        anchor = field_ref[region][4:8]
        ext_ref[region, 0:4, :] = anchor
        return carry

    def leave(region, carry):
        order = graph_ref[region, 32:48, :].astype(jnp.int32)
        low, high = order & (LANES - 1), (order >> 7) & 3
        mass = jnp.zeros((16, LANES), jnp.float32)
        for c in range(4):
            got = along(spread(ext_ref[region, c : c + 1, :], 16), low)
            mass = jnp.where(high == c, got, mass)
        flow_ref[pl.ds(pl.multiple_of(region * 16, 16), 16), :] = mass * sorted_ref[region]
        return carry

    first_lane = lane_iota(8) == 0
    first_slot = first_lane & (band == 0)

    def previous(sums):
        shifted = pltpu.roll(sums, 1, 1)
        shifted = jnp.where(first_lane, pltpu.roll(shifted, 1, 0), shifted)
        return jnp.where(first_slot, 0.0, shifted)

    def arrive(region, carry):
        ends = graph_ref[region, 48:56, :].astype(jnp.int32)
        low, high = ends & (LANES - 1), ends >> 7
        part = jnp.zeros((8, LANES), jnp.float32)
        whole = jnp.zeros((8, LANES), jnp.float32)
        before = jnp.zeros((8, LANES), jnp.float32)
        for c in range(16):
            row = pl.ds(region * 16 + c, 1)
            got = along(spread(part_ref[row, :], 8), low)
            here = high == c
            part = jnp.where(here, got, part)
            whole = jnp.where(here, before, whole)
            before = before + spread(total_ref[row, :], 8)
        whole = jnp.where(high == 16, before, whole)
        arrivals = (part - previous(part)) + (whole - previous(whole))
        ext_ref[region, 4:8, :] = field_ref[region][4:8] + arrivals[0:4]
        rim_ref[pl.ds(region, 1), :] = arrivals[4:5]
        return carry

    def settle(sums, region_totals, region, carry):
        tile = graph_ref[region, 56:64, :].astype(jnp.int32)
        low, high = tile & (LANES - 1), tile >> 7
        row = pl.ds(region, 1)
        got = along(spread(sums[row, :], 8), low)
        got = jnp.where(high == 1, spread(region_totals[row, :], 8), got)
        ext_ref[region, 0:4, :] = ext_ref[region, 4:8, :] + (got - previous(got))[0:4]
        return carry

    def each(body, unroll=8):
        lax.fori_loop(0, regions, body, 0, unroll=unroll)

    each(first)
    for sweep in range(SWEEPS):
        take_rims()
        each(functools.partial(bellman, sweep == SWEEPS - 1))
    each(arrange)
    rim_order = graph_ref[:, 61:62, :].reshape(regions, LANES).astype(jnp.int32)
    for sweep in range(SWEEPS):
        each(leave)
        part, total = prefix_and_total(flow_ref[...], steps)
        part_ref[...] = part
        total_ref[...] = total
        each(arrive)
        arrived = along(swap_rims(rim_ref[...]), rim_order)
        part, total = prefix_and_total(arrived, steps)
        part_ref[pl.ds(0, regions), :] = part
        total_ref[pl.ds(0, regions), :] = total
        each(functools.partial(settle, part_ref, total_ref))

    def finish(region, carry):
        visits = ext_ref[region, 0:4, :]
        out_ref[region, 20:24, :] = visits
        twice = jnp.concatenate([visits, visits], axis=0)
        out_ref[region, 0:8, :] = policy_ref[region, 0:8, :] * twice
        out_ref[region, 8:16, :] = policy_ref[region, 8:16, :] * twice
        return carry

    each(finish)


def gradient_kernel(
    scale,
    back_ref,
    counts_ref,
    logits_ref,
    hidden_ref,
    column_ref,
    feat_ref,
    value_ref,
    visit_ref,
    grad_ref,
    hidden_grad_ref,
):
    dests, nodes = value_ref.shape
    chunks = counts_ref.shape[0]
    hid = hidden_ref.shape[0]
    feats = feat_ref.shape[1]
    expected = jnp.sum(back_ref[:, 0:16, :], axis=0)
    for c in range(nodes // LANES):
        span = pl.ds(c * LANES, LANES)
        value_ref[:, span] = back_ref[:, 16 + c : 17 + c, :].reshape(dests, LANES)
        visit_ref[:, span] = back_ref[:, 20 + c : 21 + c, :].reshape(dests, LANES)
    logits = logits_ref[...]
    gap = counts_ref[...].astype(jnp.float32) - expected
    logit_grad = -gap * (1.0 / (1.0 + jnp.exp(-logits)))
    column = column_ref[...]
    out_sum = jnp.zeros((hid, LANES), jnp.float32)
    for c in range(chunks):
        span = pl.ds(c * LANES, LANES)
        hidden = hidden_ref[:, span]
        grad_row = logit_grad[c : c + 1]
        out_sum = out_sum + hidden * grad_row
        hidden_grad = grad_row * column * (1.0 - hidden * hidden)
        hidden_grad_ref[:, span] = hidden_grad.astype(jnp.bfloat16)
    in_grad = jnp.dot(hidden_grad_ref[...], feat_ref[...], preferred_element_type=jnp.float32)
    grad_ref[0:feats, :] = in_grad.T
    out_grad = jnp.sum(out_sum.T, axis=0, keepdims=True)
    grad_ref[feats : feats + 8, :] = spread(out_grad, 8)


def stage_steps(count):
    bits = []
    step = count // 2
    while step:
        bits.append(step)
        step //= 2
    stages = []
    while bits:
        if len(bits) > 1:
            stages.append((bits[1], bits[0], bits[0] + bits[1]))
            bits = bits[2:]
        else:
            stages.append((bits[0],))
            bits = bits[1:]
    return stages


def by_destination(
    edge_feat,
    w_in,
    b_in,
    w_out,
    targets,
    edge_live,
    boundary_rows,
    dest_nodes,
    anchor_mass,
    prior_value,
    demo_counts,
):
    regions = lax.axis_size("region")
    dests, nodes = prior_value.shape
    edges, feats = edge_feat.shape
    hid = w_in.shape[1]
    chunks = edges // LANES
    me = lax.axis_index("region")
    f32 = jnp.float32
    graph, field, logits, hidden, column = pl.pallas_call(
        prepare_kernel,
        out_shape=(
            jax.ShapeDtypeStruct((64, LANES), f32),
            jax.ShapeDtypeStruct((dests * 8, LANES), f32),
            jax.ShapeDtypeStruct((chunks, LANES), f32),
            jax.ShapeDtypeStruct((hid, edges), f32),
            jax.ShapeDtypeStruct((hid, LANES), f32),
        ),
        compiler_params=pltpu.CompilerParams(vmem_limit_bytes=32 * MIB),
        name="prepare",
    )(
        edge_feat,
        w_in,
        b_in.reshape(1, hid),
        w_out.reshape(1, hid),
        targets.reshape(chunks, LANES),
        edge_live.reshape(chunks, LANES),
        boundary_rows.reshape(1, LANES),
        prior_value,
        anchor_mass,
    )
    field = lax.all_to_all(field.reshape(dests, 8, LANES), "region", 0, 0, tiled=True)

    def partner(block, step):
        return lax.ppermute(block, "region", [(i, i ^ step) for i in range(regions)])

    blocks = graph[None]
    offsets = [0]
    stages = stage_steps(regions)
    for stage in stages[:-1]:
        blocks = jnp.concatenate([blocks] + [partner(blocks, step) for step in stage], axis=0)
        offsets = [spot ^ step for step in (0,) + stage for spot in offsets]
    other = partner(blocks, stages[-1][0])
    offsets = offsets + [spot ^ stages[-1][0] for spot in offsets]
    place = jnp.stack([me.astype(jnp.int32), dest_nodes[me]])
    back = pl.pallas_call(
        functools.partial(sweep_kernel, tuple(offsets)),
        out_shape=jax.ShapeDtypeStruct((regions, 24, LANES), f32),
        in_specs=[
            pl.BlockSpec(memory_space=pltpu.SMEM),
            pl.BlockSpec(memory_space=pl.ANY),
            pl.BlockSpec(memory_space=pl.ANY),
            pl.BlockSpec(memory_space=pltpu.VMEM),
        ],
        out_specs=pl.BlockSpec(memory_space=pltpu.VMEM),
        scratch_shapes=[
            pltpu.VMEM((regions, 64, LANES), f32),
            pltpu.VMEM((regions, 8, LANES), f32),
            pltpu.VMEM((regions, LANES), f32),
            pltpu.VMEM((regions, 16, LANES), f32),
            pltpu.VMEM((regions, 16, LANES), f32),
            pltpu.VMEM((regions * 16, LANES), f32),
            pltpu.VMEM((regions * 16, LANES), f32),
            pltpu.VMEM((regions * 16, LANES), f32),
            pltpu.SemaphoreType.DMA((regions,)),
        ],
        compiler_params=pltpu.CompilerParams(vmem_limit_bytes=32 * MIB),
        name="sweeps",
    )(place, blocks, other, field)
    back = lax.all_to_all(back, "region", 0, 0, tiled=True)
    values, visits, packed = pl.pallas_call(
        functools.partial(gradient_kernel, 1.0),
        out_shape=(
            jax.ShapeDtypeStruct((dests, nodes), f32),
            jax.ShapeDtypeStruct((dests, nodes), f32),
            jax.ShapeDtypeStruct((feats + 8, hid), f32),
        ),
        scratch_shapes=[pltpu.VMEM((hid, edges), jnp.bfloat16)],
        compiler_params=pltpu.CompilerParams(vmem_limit_bytes=32 * MIB),
        name="gradient",
    )(back, demo_counts.reshape(chunks, LANES), logits, hidden, column, edge_feat)
    grad_scale = 1.0 / math.sqrt(edges * regions)
    total = sum_over(packed, "region", regions) * grad_scale
    return (values, visits, total[:feats], total[feats])


def shards(*arrays):
    boundary_rows, prior_value, targets = arrays[6], arrays[9], arrays[4]
    regions = lax.axis_size("region")
    dests, nodes = prior_value.shape
    fits = (nodes, targets.shape[0], boundary_rows.shape[0]) == (512, 2048, LANES)
    if fits and dests == regions and regions & (regions - 1) == 0:
        return by_destination(*arrays)
    return ring_sweeps(*arrays)


def solution(mesh):
    placed = (
        P("region", None),
        P(),
        P(),
        P(),
        P("region"),
        P("region"),
        P("region"),
        P(),
        P(None, "region"),
        P(None, "region"),
        P("region"),
    )
    return jax.shard_map(
        shards,
        mesh=mesh,
        in_specs=placed,
        out_specs=(P(None, "region"), P(None, "region"), P(), P()),
        check_vma=False,
    )
```

```python
import functools
import math

import jax
import jax.numpy as jnp
from jax import lax
from jax.experimental import pallas as pl
from jax.experimental.pallas import tpu as pltpu
from jax.sharding import PartitionSpec as P

SWEEPS = 4


NEG_FILL = -1e30


def with_halo(cells, sides, width):
    for axis, dim in sides:
        count = lax.axis_size(axis)
        head = lax.slice_in_dim(cells, 0, width, axis=dim)
        tail = lax.slice_in_dim(cells, cells.shape[dim] - width, cells.shape[dim], axis=dim)
        cells = jnp.concatenate(
            [
                lax.ppermute(tail, axis, [(i, (i + 1) % count) for i in range(count)]),
                cells,
                lax.ppermute(head, axis, [((i + 1) % count, i) for i in range(count)]),
            ],
            axis=dim,
        )
    return cells


def sum_over(cells, axis, count):
    if count & (count - 1):
        return lax.psum(cells, axis)

    def partner(block, step):
        return lax.ppermute(block, axis, [(i, i ^ step) for i in range(count)])

    stride = 1
    while stride < count:
        if stride > 1 and stride * 4 <= count:
            near = partner(cells, stride)
            far = partner(cells, 2 * stride)
            across = partner(cells, 3 * stride)
            cells = (cells + near) + (far + across)
            stride *= 4
        else:
            cells = cells + partner(cells, stride)
            stride *= 2
    return cells


def ring_sweeps(
    edge_feat,
    w_in,
    b_in,
    w_out,
    targets,
    edge_live,
    boundary_rows,
    dest_nodes,
    anchor_mass,
    prior_value,
    demo_counts,
):
    node_count = prior_value.shape[1]
    dest_count = prior_value.shape[0]
    rim_width = boundary_rows.shape[0] // 2
    degree = targets.shape[0] // node_count
    region_pos = lax.axis_index("region")
    node_ids = region_pos * node_count + jnp.arange(node_count, dtype=jnp.int32)
    at_dest = node_ids[None, :] == dest_nodes[:, None]
    keep_flow = jnp.where(at_dest, 0.0, 1.0)
    target_idx = targets.reshape(degree, node_count)
    live_mask = edge_live.reshape(degree, node_count) > 0
    left_rows = boundary_rows[:rim_width]
    right_rows = boundary_rows[rim_width:]
    pre_act = jnp.dot(edge_feat, w_in, preferred_element_type=jnp.float32) + b_in
    hidden = jnp.tanh(pre_act)
    logits = jnp.dot(hidden, w_out, precision=lax.Precision.HIGHEST)
    reward = (-jax.nn.softplus(logits)).reshape(degree, node_count)
    values = prior_value
    masked = None
    log_total = None
    for sweep in range(SWEEPS):
        outgoing = jnp.concatenate([values[:, left_rows], values[:, right_rows]], axis=1)
        extend_padded = with_halo(outgoing, (("region", 1),), rim_width)
        extended = jnp.concatenate(
            [values, extend_padded[:, :rim_width], extend_padded[:, 3 * rim_width :]], axis=1
        )
        masked = jnp.where(live_mask[None], extended[:, target_idx] + reward[None], NEG_FILL)
        row_top = jnp.max(masked, axis=1)
        exp_total = jnp.sum(jnp.exp(masked - row_top[:, None, :]), axis=1)
        log_total = row_top + jnp.log(exp_total)
        values = jnp.where(at_dest, 0.0, log_total)
    policy = jnp.exp(masked - log_total[:, None, :]) * keep_flow[:, None, :]
    flat_targets = target_idx.reshape(-1)
    visits = anchor_mass
    for sweep in range(SWEEPS):
        outflow = (visits[:, None, :] * policy).reshape(dest_count, -1)
        arrivals = (
            jnp.zeros((dest_count, node_count + 2 * rim_width), jnp.float32)
            .at[:, flat_targets]
            .add(outflow)
        )
        padded = with_halo(arrivals[:, node_count:], (("region", 1),), rim_width)
        visits = anchor_mass + arrivals[:, :node_count]
        visits = visits.at[:, left_rows].add(padded[:, :rim_width])
        visits = visits.at[:, right_rows].add(padded[:, 3 * rim_width :])
    expected = jnp.sum(visits[:, None, :] * policy, axis=0).reshape(-1)
    residual_gap = demo_counts.astype(jnp.float32) - expected
    logit_grad = -residual_gap * jax.nn.sigmoid(logits)
    out_grad = jnp.dot(logit_grad, hidden, precision=lax.Precision.HIGHEST)
    hidden_grad = (logit_grad[:, None] * w_out[None, :] * (1.0 - hidden * hidden)).astype(
        jnp.bfloat16
    )
    in_grad = lax.dot_general(
        edge_feat, hidden_grad, (((0,), (0,)), ((), ())), preferred_element_type=jnp.float32
    )
    region_count = lax.axis_size("region")
    grad_scale = 1.0 / math.sqrt(targets.shape[0] * region_count)
    packed = jnp.concatenate([in_grad, out_grad[None]], axis=0)
    total = sum_over(packed, "region", region_count) * grad_scale
    return (values, visits, total[:-1], total[-1])


LANES = 128
BLOCK = 80
MIB = 1024 * 1024


def along(table, index):
    return jnp.take_along_axis(table, index, axis=1, mode="promise_in_bounds")


def spread(row, count):
    return jnp.broadcast_to(row, (count, row.shape[1]))


def lane_iota(rows):
    return lax.broadcasted_iota(jnp.int32, (rows, LANES), 1)


def row_iota(rows):
    return lax.broadcasted_iota(jnp.int32, (rows, LANES), 0)


def contract_lanes(left, right):
    return lax.dot_general(
        left.astype(jnp.bfloat16),
        right.astype(jnp.bfloat16),
        (((1,), (1,)), ((), ())),
        preferred_element_type=jnp.float32,
    )


def three_parts(cells):
    high = cells.astype(jnp.bfloat16)
    rest = cells - high.astype(jnp.float32)
    middle = rest.astype(jnp.bfloat16)
    low = (rest - middle.astype(jnp.float32)).astype(jnp.bfloat16)
    return high, middle, low


def prefix_and_total(cells, steps):
    rows = cells.shape[0]
    parts = jnp.concatenate(three_parts(cells), axis=0)
    sums = jnp.dot(parts, steps, preferred_element_type=jnp.float32)
    sums = (sums[:rows] + sums[rows : 2 * rows]) + sums[2 * rows :]
    return sums[:, :LANES], sums[:, LANES:]


def step_matrix():
    src = lax.broadcasted_iota(jnp.int32, (LANES, 2 * LANES), 0)
    dst = lax.broadcasted_iota(jnp.int32, (LANES, 2 * LANES), 1)
    return jnp.where(dst > src, 1.0, 0.0).astype(jnp.bfloat16)


def earlier_equal(keys):
    lane = lane_iota(keys.shape[0])
    found = jnp.zeros(keys.shape, jnp.float32)
    for shift in range(1, LANES):
        same = (pltpu.roll(keys, shift, 1) == keys) & (lane >= shift)
        found = found + jnp.where(same, 1.0, 0.0)
    return found


def sort_plan(keys, earlier, steps):
    rows = keys.shape[0]
    low, high = keys & (LANES - 1), keys >> 7
    column = row_iota(LANES)
    band = row_iota(8)
    hists = []
    for c in range(rows):
        in_band = jnp.where(spread(high[c : c + 1], 8) == band, 1.0, 0.0)
        in_lane = jnp.where(spread(low[c : c + 1], LANES) == column, 1.0, 0.0)
        hists.append(contract_lanes(in_band, in_lane))
    total = hists[0]
    for c in range(1, rows):
        total = total + hists[c]
    inside, sums = prefix_and_total(total, steps)
    before = jnp.zeros((1, LANES), jnp.float32)
    starts = []
    for band_row in range(8):
        starts.append(inside[band_row : band_row + 1] + before)
        before = before + sums[band_row : band_row + 1]
    start = jnp.concatenate(starts, axis=0)
    ends = start + total
    ranks = []
    for c in range(rows):
        found = along(start, spread(low[c : c + 1], 8))
        found = jnp.where(spread(high[c : c + 1], 8) == band, found, 0.0)
        ranks.append(jnp.sum(found, axis=0, keepdims=True) + earlier[c : c + 1])
        start = start + hists[c]
    rank = jnp.concatenate(ranks, axis=0).astype(jnp.int32) if rows > 1 else ranks[0].astype(jnp.int32)
    rank_low, rank_high = rank & (LANES - 1), rank >> 7
    out_rows = max(rows, 8)
    out_band = row_iota(out_rows)
    lane = lane_iota(out_rows).astype(jnp.float32)
    order = jnp.zeros((out_rows, LANES), jnp.float32)
    for c in range(rows):
        in_band = spread(rank_high[c : c + 1], out_rows) == out_band
        in_lane = jnp.where(spread(rank_low[c : c + 1], LANES) == column, 1.0, 0.0)
        both = jnp.concatenate(
            [jnp.where(in_band, lane, 0.0), jnp.where(in_band, 1.0, 0.0)], axis=0
        )
        got = contract_lanes(both, in_lane)
        order = order + got[:out_rows] + got[out_rows:] * float(c * LANES)
    return order, ends


def columns_of(w_in_ref, b_in_ref, w_out_ref):
    b_col = spread(b_in_ref[...], LANES).T
    w_col = spread(w_out_ref[...], LANES).T
    w_rows = w_in_ref[...].astype(jnp.float32).T.astype(jnp.bfloat16)
    return w_rows, b_col, w_col


def hidden_chunk(w_rows, b_col, feat):
    return jnp.tanh(jnp.dot(w_rows, feat, preferred_element_type=jnp.float32) + b_col)


def prepare_kernel(
    feat_hbm,
    w_in_hbm,
    b_in_hbm,
    w_out_hbm,
    targets_hbm,
    live_hbm,
    rows_hbm,
    prior_hbm,
    anchor_hbm,
    send_ref,
    logits_ref,
    feat_ref,
    w_in_ref,
    b_in_ref,
    w_out_ref,
    targets_ref,
    live_ref,
    rows_ref,
    prior_ref,
    anchor_ref,
    copy_sem,
):
    chunks = targets_ref.shape[0]
    pairs = (
        (w_in_hbm, w_in_ref),
        (b_in_hbm, b_in_ref),
        (w_out_hbm, w_out_ref),
        (feat_hbm, feat_ref),
        (targets_hbm, targets_ref),
        (live_hbm, live_ref),
        (rows_hbm, rows_ref),
        (prior_hbm, prior_ref),
        (anchor_hbm, anchor_ref),
    )
    copies = [
        pltpu.make_async_copy(src, dst, copy_sem.at[k]) for k, (src, dst) in enumerate(pairs)
    ]
    for copy in copies:
        copy.start()
    for copy in copies:
        copy.wait()
    w_rows, b_col, w_col = columns_of(w_in_ref, b_in_ref, w_out_ref)
    logit_rows = []
    for c in range(chunks):
        hidden = hidden_chunk(w_rows, b_col, feat_ref[:, pl.ds(c * LANES, LANES)])
        logit_rows.append(jnp.sum(hidden * w_col, axis=0, keepdims=True))
    logits = jnp.concatenate(logit_rows, axis=0)
    logits_ref[...] = logits
    reward = -(jnp.maximum(logits, 0.0) + jnp.log1p(jnp.exp(-jnp.abs(logits))))
    reward = jnp.where(live_ref[...] > 0, reward, NEG_FILL)
    steps = step_matrix()
    targets = targets_ref[...]
    rows = rows_ref[...]
    earlier = earlier_equal(jnp.concatenate([targets, spread(rows, 8)], axis=0))
    order, ends = sort_plan(targets, earlier[:chunks], steps)
    rim_order, rim_ends = sort_plan(rows, earlier[chunks : chunks + 1], steps)
    graph = jnp.concatenate(
        [
            targets.astype(jnp.float32),
            reward,
            order,
            ends,
            rim_ends[0:4],
            rows.astype(jnp.float32),
            rim_order[0:1],
            jnp.zeros((2, LANES), jnp.float32),
        ],
        axis=0,
    )
    layer = lax.axis_index("region") >> 3
    for k in range(4):
        send_ref[pl.ds(k * 128, 64), :] = graph
        dests = pl.ds(pl.multiple_of((layer ^ k) * 8, 8), 8)
        for c in range(4):
            span = pl.ds(c * LANES, LANES)
            send_ref[pl.ds(k * 128 + 64 + 8 * c, 8), :] = prior_ref[dests, span]
            send_ref[pl.ds(k * 128 + 96 + 8 * c, 8), :] = anchor_ref[dests, span]


def sweep_kernel(
    offsets,
    dest_nodes_ref,
    own_ref,
    other_ref,
    out_ref,
    graph_ref,
    index_ref,
    reward_ref,
    ext_ref,
    anchor_ref,
    policy_ref,
    sorted_ref,
    flow_ref,
    part_ref,
    total_ref,
    copy_sem,
):
    me = lax.axis_index("region")
    dest = dest_nodes_ref[me]
    regions = len(offsets)
    half = own_ref.shape[0]
    copies = []
    for spot, offset in enumerate(offsets):
        src = own_ref.at[spot] if spot < half else other_ref.at[spot - half]
        place = pl.ds(pl.multiple_of((me ^ offset) * BLOCK, BLOCK), BLOCK)
        copies.append(pltpu.make_async_copy(src, graph_ref.at[place], copy_sem.at[spot]))
    for copy in copies:
        copy.start()
    for copy in copies:
        copy.wait()
    dest_region, dest_node = dest // 512, dest % 512
    bands = range(0, regions, 8)
    region = lax.broadcasted_iota(jnp.int32, (8, LANES), 0)
    lane = lane_iota(8)
    first_lane = lane == 0
    left_lanes = lane_iota(regions) < LANES // 2
    steps = step_matrix()

    def block(k, band=None):
        if band is None:
            return pl.ds(k * regions, regions)
        return pl.ds(k * regions + band, 8)

    def split(k, band):
        cells = index_ref[block(k, band), :]
        return cells & (LANES - 1), cells >> 7

    def pick(tables, low, high):
        found = along(tables[0], low)
        for c, table in enumerate(tables[1:], 1):
            found = jnp.where(high == c, along(table, low), found)
        return found

    def swap_rims(rims):
        turned = pltpu.roll(rims, LANES // 2, 1)
        return jnp.where(
            left_lanes, pltpu.roll(turned, 1, 0), pltpu.roll(turned, regions - 1, 0)
        )

    def graph_rows(row):
        return graph_ref[pl.ds(row, regions, stride=BLOCK), :]

    def field_rows(row):
        return graph_rows(64 + 2 * row + (me & 1))

    sources = list(range(16)) + list(range(32, 48)) + list(range(48, 53))
    sources = sources + list(range(56, 60)) + [60, 61]
    for k, row in enumerate(sources):
        index_ref[block(k), :] = graph_rows(row).astype(jnp.int32)
    order_at, ends_at, rim_ends_at, rows_at, rim_order_at = 16, 32, 37, 41, 42
    for k in range(16):
        reward_ref[block(k), :] = graph_rows(16 + k)

    def give_rims():
        rims = []
        for band in bands:
            values = [ext_ref[block(c, band), :] for c in range(4)]
            rims.append(pick(values, *split(rows_at, band)))
        ext_ref[block(4), :] = swap_rims(jnp.concatenate(rims, axis=0))

    def bellman(last):
        for band in bands:
            ext = [ext_ref[block(c, band), :] for c in range(5)]
            values = []
            for c in range(4):
                scores = [
                    pick(ext, *split(4 * k + c, band)) + reward_ref[block(4 * k + c, band), :]
                    for k in range(4)
                ]
                top = jnp.maximum(
                    jnp.maximum(scores[0], scores[1]), jnp.maximum(scores[2], scores[3])
                )
                grown = [jnp.exp(score - top) for score in scores]
                log_total = top + jnp.log((grown[0] + grown[1]) + (grown[2] + grown[3]))
                mask = (region == dest_region - band) & (lane == dest_node - c * LANES)
                values.append(jnp.where(mask, 0.0, log_total))
                if last:
                    for k in range(4):
                        policy_ref[block(4 * k + c, band), :] = jnp.where(
                            mask, 0.0, jnp.exp(scores[k] - log_total)
                        )
            for c in range(4):
                ext_ref[block(c, band), :] = values[c]

    def arrange():
        for band in bands:
            tables = [policy_ref[block(c, band), :] for c in range(16)]
            for k in range(16):
                sorted_ref[block(k, band), :] = pick(tables, *split(order_at + k, band))

    def previous(sums):
        rolled = [pltpu.roll(cells, 1, 1) for cells in sums]
        return [
            jnp.where(first_lane, before, cells)
            for before, cells in zip([jnp.zeros((8, LANES), jnp.float32)] + rolled[:-1], rolled)
        ]

    def push():
        for band in bands:
            visits = [ext_ref[block(c, band), :] for c in range(4)]
            for k in range(16):
                low, high = split(order_at + k, band)
                flow = pick(visits, low, high & 3) * sorted_ref[block(k, band), :]
                flow_ref[block(k, band), :] = flow
        part, total = prefix_and_total(flow_ref[...], steps)
        part_ref[...] = part
        total_ref[...] = total
        rims = []
        for band in bands:
            part = [part_ref[block(c, band), :] for c in range(16)]
            before = [jnp.zeros((8, LANES), jnp.float32)]
            for c in range(16):
                before.append(before[c] + total_ref[block(c, band), :])
            parts, wholes = [], []
            for o in range(5):
                low, high = split(ends_at + o, band)
                inside = jnp.zeros((8, LANES), jnp.float32)
                whole = before[16]
                for c in range(16):
                    here = high == c
                    inside = jnp.where(here, along(part[c], low), inside)
                    whole = jnp.where(here, before[c], whole)
                parts.append(inside)
                wholes.append(whole)
            arrivals = [
                (inside - inside_back) + (whole - whole_back)
                for inside, inside_back, whole, whole_back in zip(
                    parts, previous(parts), wholes, previous(wholes)
                )
            ]
            for c in range(4):
                ext_ref[block(c, band), :] = anchor_ref[block(c, band), :] + arrivals[c]
            rims.append(arrivals[4])
        arrived = swap_rims(jnp.concatenate(rims, axis=0))
        arrived = [
            along(arrived[band : band + 8], split(rim_order_at, band)[0]) for band in bands
        ]
        part, total = prefix_and_total(jnp.concatenate(arrived, axis=0), steps)
        for band in bands:
            sums = []
            for c in range(4):
                low, high = split(rim_ends_at + c, band)
                inside = along(part[band : band + 8], low)
                sums.append(jnp.where(high == 1, total[band : band + 8], inside))
            for c, (here, back) in enumerate(zip(sums, previous(sums))):
                ext_ref[block(c, band), :] = ext_ref[block(c, band), :] + (here - back)

    for c in range(4):
        ext_ref[block(c), :] = field_rows(c)
        anchor_ref[block(c), :] = field_rows(4 + c)
    for sweep in range(SWEEPS):
        give_rims()
        bellman(sweep == SWEEPS - 1)
    for c in range(4):
        out_ref[pl.ds(16 + c, regions, stride=24), :] = ext_ref[block(c), :]
        ext_ref[block(c), :] = anchor_ref[block(c), :]
    arrange()
    for sweep in range(SWEEPS):
        push()
    for c in range(4):
        visits = ext_ref[block(c), :]
        out_ref[pl.ds(20 + c, regions, stride=24), :] = visits
        for k in range(4):
            row = 4 * k + c
            out_ref[pl.ds(row, regions, stride=24), :] = policy_ref[block(row), :] * visits


def gradient_kernel(
    back_ref,
    counts_ref,
    logits_ref,
    feat_ref,
    w_in_ref,
    b_in_ref,
    w_out_ref,
    value_ref,
    visit_ref,
    grad_ref,
    hidden_grad_ref,
):
    dests, nodes = value_ref.shape
    chunks = counts_ref.shape[0]
    hid = w_in_ref.shape[1]
    feats = feat_ref.shape[0]
    expected = jnp.sum(back_ref[:, 0:16, :], axis=0)
    for c in range(nodes // LANES):
        span = pl.ds(c * LANES, LANES)
        value_ref[:, span] = back_ref[:, 16 + c : 17 + c, :].reshape(dests, LANES)
        visit_ref[:, span] = back_ref[:, 20 + c : 21 + c, :].reshape(dests, LANES)
    gap = counts_ref[...].astype(jnp.float32) - expected
    logit_grad = -gap * (1.0 / (1.0 + jnp.exp(-logits_ref[...])))
    w_rows, b_col, w_col = columns_of(w_in_ref, b_in_ref, w_out_ref)
    out_sum = jnp.zeros((hid, LANES), jnp.float32)
    for c in range(chunks):
        span = pl.ds(c * LANES, LANES)
        hidden = hidden_chunk(w_rows, b_col, feat_ref[:, span])
        grad_row = logit_grad[c : c + 1]
        out_sum = out_sum + hidden * grad_row
        hidden_grad = grad_row * w_col * (1.0 - hidden * hidden)
        hidden_grad_ref[:, span] = hidden_grad.astype(jnp.bfloat16)
    grad_ref[0:feats, :] = contract_lanes(feat_ref[...], hidden_grad_ref[...])
    out_grad = jnp.sum(out_sum.T, axis=0, keepdims=True)
    grad_ref[feats : feats + 8, :] = spread(out_grad, 8)


def close_kernel(scale, own_ref, near_ref, far_ref, across_ref, in_grad_ref, out_grad_ref):
    total = (own_ref[...] + near_ref[...]) + (far_ref[...] + across_ref[...])
    feats = in_grad_ref.shape[0]
    in_grad_ref[...] = total[0:feats] * scale
    out_grad_ref[...] = total[feats : feats + 1] * scale


def by_destination(
    edge_feat,
    w_in,
    b_in,
    w_out,
    targets,
    edge_live,
    boundary_rows,
    dest_nodes,
    anchor_mass,
    prior_value,
    demo_counts,
):
    regions = lax.axis_size("region")
    dests, nodes = prior_value.shape
    edges, feats = edge_feat.shape
    hid = w_in.shape[1]
    chunks = edges // LANES
    f32 = jnp.float32

    def partners(block, *steps):
        return [
            lax.ppermute(block[k], "region", [(i, i ^ step) for i in range(regions)])
            for k, step in enumerate(steps)
        ]

    layer_steps, chip_steps, core_step = (8, 16, 24), (2, 4, 6), 1
    feat_rows = edge_feat.T
    weights = (w_in, b_in.reshape(1, hid), w_out.reshape(1, hid))
    inputs = (
        feat_rows,
        *weights,
        targets.reshape(chunks, LANES),
        edge_live.reshape(chunks, LANES),
        boundary_rows.reshape(1, LANES),
        prior_value,
        anchor_mass,
    )
    send, logits = pl.pallas_call(
        prepare_kernel,
        out_shape=(
            jax.ShapeDtypeStruct((4 * 128, LANES), f32),
            jax.ShapeDtypeStruct((chunks, LANES), f32),
        ),
        in_specs=[pl.BlockSpec(memory_space=pl.ANY)] * len(inputs),
        scratch_shapes=[pltpu.VMEM(cells.shape, cells.dtype) for cells in inputs]
        + [pltpu.SemaphoreType.DMA((len(inputs),))],
        compiler_params=pltpu.CompilerParams(vmem_limit_bytes=62 * MIB),
        name="prepare",
    )(*inputs)
    send = send.reshape(4, 128, LANES)
    layers = jnp.stack([send[0]] + partners(send[1:], *layer_steps))
    graphs = layers[:, :64]
    fields = layers[:, 64:].reshape(4, 8, 8, LANES)
    chip = (lax.axis_index("region") >> 1) & 3

    def for_chip(step):
        part = lax.dynamic_slice_in_dim(fields, (chip ^ step) * 2, 2, axis=2)
        return jnp.concatenate([graphs, part.reshape(4, 16, LANES)], axis=1)

    sends = [for_chip(k) for k in range(4)]
    blocks = jnp.concatenate([sends[0]] + partners(sends[1:], *chip_steps), axis=0)
    (other,) = partners([blocks], core_step)
    offsets = [layer ^ spot for spot in (0,) + chip_steps for layer in (0,) + layer_steps]
    offsets = offsets + [spot ^ core_step for spot in offsets]
    back = pl.pallas_call(
        functools.partial(sweep_kernel, tuple(offsets)),
        out_shape=jax.ShapeDtypeStruct((regions * 24, LANES), f32),
        in_specs=[
            pl.BlockSpec(memory_space=pltpu.SMEM),
            pl.BlockSpec(memory_space=pl.ANY),
            pl.BlockSpec(memory_space=pl.ANY),
        ],
        out_specs=pl.BlockSpec(memory_space=pltpu.VMEM),
        scratch_shapes=[
            pltpu.VMEM((regions * BLOCK, LANES), f32),
            pltpu.VMEM((regions * 43, LANES), jnp.int32),
            pltpu.VMEM((regions * 16, LANES), f32),
            pltpu.VMEM((regions * 5, LANES), f32),
            pltpu.VMEM((regions * 4, LANES), f32),
            pltpu.VMEM((regions * 16, LANES), f32),
            pltpu.VMEM((regions * 16, LANES), f32),
            pltpu.VMEM((regions * 16, LANES), f32),
            pltpu.VMEM((regions * 16, LANES), f32),
            pltpu.VMEM((regions * 16, LANES), f32),
            pltpu.SemaphoreType.DMA((regions,)),
        ],
        compiler_params=pltpu.CompilerParams(vmem_limit_bytes=16 * MIB),
        name="sweeps",
    )(dest_nodes, blocks, other)
    back = lax.all_to_all(back.reshape(regions, 24, LANES), "region", 0, 0, tiled=True)
    values, visits, packed = pl.pallas_call(
        gradient_kernel,
        out_shape=(
            jax.ShapeDtypeStruct((dests, nodes), f32),
            jax.ShapeDtypeStruct((dests, nodes), f32),
            jax.ShapeDtypeStruct((feats + 8, hid), f32),
        ),
        scratch_shapes=[pltpu.VMEM((hid, edges), jnp.bfloat16)],
        compiler_params=pltpu.CompilerParams(vmem_limit_bytes=16 * MIB),
        name="gradient",
    )(back, demo_counts.reshape(chunks, LANES), logits, feat_rows, *weights)
    (twin,) = partners([packed], core_step)
    packed = packed + twin
    near, far, across = partners([packed] * 3, *chip_steps)
    packed = (packed + near) + (far + across)
    in_grad, out_grad = pl.pallas_call(
        functools.partial(close_kernel, 1.0 / math.sqrt(edges * regions)),
        out_shape=(
            jax.ShapeDtypeStruct((feats, hid), f32),
            jax.ShapeDtypeStruct((1, hid), f32),
        ),
        compiler_params=pltpu.CompilerParams(vmem_limit_bytes=16 * MIB),
        name="close",
    )(packed, *partners([packed] * 3, *layer_steps))
    return (values, visits, in_grad, out_grad.reshape(hid))


def shards(*arrays):
    boundary_rows, prior_value, targets = arrays[6], arrays[9], arrays[4]
    regions = lax.axis_size("region")
    dests, nodes = prior_value.shape
    fits = (nodes, targets.shape[0], boundary_rows.shape[0]) == (512, 2048, LANES)
    if fits and dests == regions == 32:
        return by_destination(*arrays)
    return ring_sweeps(*arrays)


def solution(mesh):
    placed = (
        P("region", None),
        P(),
        P(),
        P(),
        P("region"),
        P("region"),
        P("region"),
        P(),
        P(None, "region"),
        P(None, "region"),
        P("region"),
    )
    return jax.shard_map(
        shards,
        mesh=mesh,
        in_specs=placed,
        out_specs=(P(None, "region"), P(None, "region"), P(), P()),
        check_vma=False,
    )
```

```python
import functools
import math

import jax
import jax.numpy as jnp
from jax import lax
from jax.experimental import pallas as pl
from jax.experimental.pallas import tpu as pltpu
from jax.sharding import PartitionSpec as P

SWEEPS = 4


NEG_FILL = -1e30


def with_halo(cells, sides, width):
    for axis, dim in sides:
        count = lax.axis_size(axis)
        head = lax.slice_in_dim(cells, 0, width, axis=dim)
        tail = lax.slice_in_dim(cells, cells.shape[dim] - width, cells.shape[dim], axis=dim)
        cells = jnp.concatenate(
            [
                lax.ppermute(tail, axis, [(i, (i + 1) % count) for i in range(count)]),
                cells,
                lax.ppermute(head, axis, [((i + 1) % count, i) for i in range(count)]),
            ],
            axis=dim,
        )
    return cells


def sum_over(cells, axis, count):
    if count & (count - 1):
        return lax.psum(cells, axis)

    def partner(block, step):
        return lax.ppermute(block, axis, [(i, i ^ step) for i in range(count)])

    stride = 1
    while stride < count:
        if stride > 1 and stride * 4 <= count:
            near = partner(cells, stride)
            far = partner(cells, 2 * stride)
            across = partner(cells, 3 * stride)
            cells = (cells + near) + (far + across)
            stride *= 4
        else:
            cells = cells + partner(cells, stride)
            stride *= 2
    return cells


def ring_sweeps(
    edge_feat,
    w_in,
    b_in,
    w_out,
    targets,
    edge_live,
    boundary_rows,
    dest_nodes,
    anchor_mass,
    prior_value,
    demo_counts,
):
    node_count = prior_value.shape[1]
    dest_count = prior_value.shape[0]
    rim_width = boundary_rows.shape[0] // 2
    degree = targets.shape[0] // node_count
    region_pos = lax.axis_index("region")
    node_ids = region_pos * node_count + jnp.arange(node_count, dtype=jnp.int32)
    at_dest = node_ids[None, :] == dest_nodes[:, None]
    keep_flow = jnp.where(at_dest, 0.0, 1.0)
    target_idx = targets.reshape(degree, node_count)
    live_mask = edge_live.reshape(degree, node_count) > 0
    left_rows = boundary_rows[:rim_width]
    right_rows = boundary_rows[rim_width:]
    pre_act = jnp.dot(edge_feat, w_in, preferred_element_type=jnp.float32) + b_in
    hidden = jnp.tanh(pre_act)
    logits = jnp.dot(hidden, w_out, precision=lax.Precision.HIGHEST)
    reward = (-jax.nn.softplus(logits)).reshape(degree, node_count)
    values = prior_value
    masked = None
    log_total = None
    for sweep in range(SWEEPS):
        outgoing = jnp.concatenate([values[:, left_rows], values[:, right_rows]], axis=1)
        extend_padded = with_halo(outgoing, (("region", 1),), rim_width)
        extended = jnp.concatenate(
            [values, extend_padded[:, :rim_width], extend_padded[:, 3 * rim_width :]], axis=1
        )
        masked = jnp.where(live_mask[None], extended[:, target_idx] + reward[None], NEG_FILL)
        row_top = jnp.max(masked, axis=1)
        exp_total = jnp.sum(jnp.exp(masked - row_top[:, None, :]), axis=1)
        log_total = row_top + jnp.log(exp_total)
        values = jnp.where(at_dest, 0.0, log_total)
    policy = jnp.exp(masked - log_total[:, None, :]) * keep_flow[:, None, :]
    flat_targets = target_idx.reshape(-1)
    visits = anchor_mass
    for sweep in range(SWEEPS):
        outflow = (visits[:, None, :] * policy).reshape(dest_count, -1)
        arrivals = (
            jnp.zeros((dest_count, node_count + 2 * rim_width), jnp.float32)
            .at[:, flat_targets]
            .add(outflow)
        )
        padded = with_halo(arrivals[:, node_count:], (("region", 1),), rim_width)
        visits = anchor_mass + arrivals[:, :node_count]
        visits = visits.at[:, left_rows].add(padded[:, :rim_width])
        visits = visits.at[:, right_rows].add(padded[:, 3 * rim_width :])
    expected = jnp.sum(visits[:, None, :] * policy, axis=0).reshape(-1)
    residual_gap = demo_counts.astype(jnp.float32) - expected
    logit_grad = -residual_gap * jax.nn.sigmoid(logits)
    out_grad = jnp.dot(logit_grad, hidden, precision=lax.Precision.HIGHEST)
    hidden_grad = (logit_grad[:, None] * w_out[None, :] * (1.0 - hidden * hidden)).astype(
        jnp.bfloat16
    )
    in_grad = lax.dot_general(
        edge_feat, hidden_grad, (((0,), (0,)), ((), ())), preferred_element_type=jnp.float32
    )
    region_count = lax.axis_size("region")
    grad_scale = 1.0 / math.sqrt(targets.shape[0] * region_count)
    packed = jnp.concatenate([in_grad, out_grad[None]], axis=0)
    total = sum_over(packed, "region", region_count) * grad_scale
    return (values, visits, total[:-1], total[-1])


LANES = 128
BLOCK = 80
MIB = 1024 * 1024


def along(table, index):
    return jnp.take_along_axis(table, index, axis=1, mode="promise_in_bounds")


def spread(row, count):
    return jnp.broadcast_to(row, (count, row.shape[1]))


def lane_iota(rows):
    return lax.broadcasted_iota(jnp.int32, (rows, LANES), 1)


def row_iota(rows):
    return lax.broadcasted_iota(jnp.int32, (rows, LANES), 0)


def contract_lanes(left, right):
    return lax.dot_general(
        left.astype(jnp.bfloat16),
        right.astype(jnp.bfloat16),
        (((1,), (1,)), ((), ())),
        preferred_element_type=jnp.float32,
    )


def three_parts(cells):
    high = cells.astype(jnp.bfloat16)
    rest = cells - high.astype(jnp.float32)
    middle = rest.astype(jnp.bfloat16)
    low = (rest - middle.astype(jnp.float32)).astype(jnp.bfloat16)
    return high, middle, low


def prefix_and_total(cells, steps):
    parts = jnp.concatenate(three_parts(cells), axis=1)
    sums = jnp.dot(parts, steps, preferred_element_type=jnp.float32)
    return sums[:, :LANES], sums[:, LANES:]


def step_matrix():
    src = lax.broadcasted_iota(jnp.int32, (3 * LANES, 2 * LANES), 0) & (LANES - 1)
    dst = lax.broadcasted_iota(jnp.int32, (3 * LANES, 2 * LANES), 1)
    return jnp.where(dst > src, 1.0, 0.0).astype(jnp.bfloat16)


def earlier_equal(keys):
    lane = lane_iota(keys.shape[0])
    found = jnp.zeros(keys.shape, jnp.float32)
    for shift in range(1, LANES):
        same = (pltpu.roll(keys, shift, 1) == keys) & (lane >= shift)
        found = found + jnp.where(same, 1.0, 0.0)
    return found


def sort_plan(keys, earlier, steps):
    rows = keys.shape[0]
    low, high = keys & (LANES - 1), keys >> 7
    column = row_iota(LANES)
    band = row_iota(8)
    hists = []
    for c in range(rows):
        in_band = jnp.where(spread(high[c : c + 1], 8) == band, 1.0, 0.0)
        in_lane = jnp.where(spread(low[c : c + 1], LANES) == column, 1.0, 0.0)
        hists.append(contract_lanes(in_band, in_lane))
    total = hists[0]
    for c in range(1, rows):
        total = total + hists[c]
    inside, sums = prefix_and_total(total, steps)
    before = jnp.zeros((1, LANES), jnp.float32)
    starts = []
    for band_row in range(8):
        starts.append(inside[band_row : band_row + 1] + before)
        before = before + sums[band_row : band_row + 1]
    start = jnp.concatenate(starts, axis=0)
    ends = start + total
    ranks = []
    for c in range(rows):
        found = along(start, spread(low[c : c + 1], 8))
        found = jnp.where(spread(high[c : c + 1], 8) == band, found, 0.0)
        ranks.append(jnp.sum(found, axis=0, keepdims=True) + earlier[c : c + 1])
        start = start + hists[c]
    rank = jnp.concatenate(ranks, axis=0).astype(jnp.int32) if rows > 1 else ranks[0].astype(jnp.int32)
    rank_low, rank_high = rank & (LANES - 1), rank >> 7
    out_rows = max(rows, 8)
    out_band = row_iota(out_rows)
    lane = lane_iota(out_rows).astype(jnp.float32)
    order = jnp.zeros((out_rows, LANES), jnp.float32)
    for c in range(rows):
        in_band = spread(rank_high[c : c + 1], out_rows) == out_band
        in_lane = jnp.where(spread(rank_low[c : c + 1], LANES) == column, 1.0, 0.0)
        both = jnp.concatenate(
            [jnp.where(in_band, lane, 0.0), jnp.where(in_band, 1.0, 0.0)], axis=0
        )
        got = contract_lanes(both, in_lane)
        order = order + got[:out_rows] + got[out_rows:] * float(c * LANES)
    return order, ends


def columns_of(w_in_ref, b_in_ref, w_out_ref):
    b_col = spread(b_in_ref[...], LANES).T
    w_col = spread(w_out_ref[...], LANES).T
    w_rows = w_in_ref[...].astype(jnp.float32).T.astype(jnp.bfloat16)
    return w_rows, b_col, w_col


def hidden_chunk(w_rows, b_col, feat):
    return jnp.tanh(jnp.dot(w_rows, feat, preferred_element_type=jnp.float32) + b_col)


def prepare_kernel(
    feat_hbm,
    w_in_hbm,
    b_in_hbm,
    w_out_hbm,
    targets_hbm,
    live_hbm,
    rows_hbm,
    prior_hbm,
    anchor_hbm,
    send_0_ref,
    send_1_ref,
    send_2_ref,
    send_3_ref,
    logits_ref,
    feat_ref,
    w_in_ref,
    b_in_ref,
    w_out_ref,
    targets_ref,
    live_ref,
    rows_ref,
    prior_ref,
    anchor_ref,
    copy_sem,
):
    chunks = targets_ref.shape[0]
    pairs = (
        (targets_hbm, targets_ref),
        (rows_hbm, rows_ref),
        (w_in_hbm, w_in_ref),
        (b_in_hbm, b_in_ref),
        (w_out_hbm, w_out_ref),
        (feat_hbm, feat_ref),
        (live_hbm, live_ref),
        (prior_hbm, prior_ref),
        (anchor_hbm, anchor_ref),
    )
    copies = [
        pltpu.make_async_copy(src, dst, copy_sem.at[k]) for k, (src, dst) in enumerate(pairs)
    ]
    for copy in copies:
        copy.start()
    for copy in copies[:2]:
        copy.wait()
    steps = step_matrix()
    targets = targets_ref[...]
    rows = rows_ref[...]
    earlier = earlier_equal(jnp.concatenate([targets, spread(rows, 8)], axis=0))
    order, ends = sort_plan(targets, earlier[:chunks], steps)
    rim_order, rim_ends = sort_plan(rows, earlier[chunks : chunks + 1], steps)
    for copy in copies[2:]:
        copy.wait()
    w_rows, b_col, w_col = columns_of(w_in_ref, b_in_ref, w_out_ref)
    logit_rows = []
    for c in range(chunks):
        hidden = hidden_chunk(w_rows, b_col, feat_ref[:, pl.ds(c * LANES, LANES)])
        logit_rows.append(jnp.sum(hidden * w_col, axis=0, keepdims=True))
    logits = jnp.concatenate(logit_rows, axis=0)
    logits_ref[...] = logits
    reward = -(jnp.maximum(logits, 0.0) + jnp.log1p(jnp.exp(-jnp.abs(logits))))
    reward = jnp.where(live_ref[...] > 0, reward, NEG_FILL)
    graph = jnp.concatenate(
        [
            targets.astype(jnp.float32),
            reward,
            order,
            ends,
            rim_ends[0:4],
            rows.astype(jnp.float32),
            rim_order[0:1],
            jnp.zeros((2, LANES), jnp.float32),
        ],
        axis=0,
    )
    layer = lax.axis_index("region") >> 3
    for k, send_ref in enumerate((send_0_ref, send_1_ref, send_2_ref, send_3_ref)):
        send_ref[0:64, :] = graph
        dests = pl.ds(pl.multiple_of((layer ^ k) * 8, 8), 8)
        for c in range(4):
            span = pl.ds(c * LANES, LANES)
            send_ref[pl.ds(64 + 8 * c, 8), :] = prior_ref[dests, span]
            send_ref[pl.ds(96 + 8 * c, 8), :] = anchor_ref[dests, span]


def sweep_kernel(
    offsets,
    dest_nodes_ref,
    own_ref,
    other_ref,
    out_ref,
    graph_ref,
    index_ref,
    reward_ref,
    ext_ref,
    anchor_ref,
    policy_ref,
    sorted_ref,
    flow_ref,
    part_ref,
    total_ref,
    copy_sem,
):
    me = lax.axis_index("region")
    dest = dest_nodes_ref[me]
    regions = len(offsets)
    half = own_ref.shape[0]
    copies = []
    for spot, offset in enumerate(offsets):
        src = own_ref.at[spot] if spot < half else other_ref.at[spot - half]
        place = pl.ds(pl.multiple_of((me ^ offset) * BLOCK, BLOCK), BLOCK)
        copies.append(pltpu.make_async_copy(src, graph_ref.at[place], copy_sem.at[spot]))
    for copy in copies:
        copy.start()
    for copy in copies:
        copy.wait()
    dest_region, dest_node = dest // 512, dest % 512
    bands = range(0, regions, 8)
    region = lax.broadcasted_iota(jnp.int32, (8, LANES), 0)
    lane = lane_iota(8)
    first_lane = lane == 0
    left_lanes = lane_iota(regions) < LANES // 2
    steps = step_matrix()

    def block(k, band=None):
        if band is None:
            return pl.ds(k * regions, regions)
        return pl.ds(k * regions + band, 8)

    def split(k, band):
        cells = index_ref[block(k, band), :]
        return cells & (LANES - 1), cells >> 7

    def pick(tables, low, high):
        found = along(tables[0], low)
        for c, table in enumerate(tables[1:], 1):
            found = jnp.where(high == c, along(table, low), found)
        return found

    def swap_rims(rims):
        turned = pltpu.roll(rims, LANES // 2, 1)
        return jnp.where(
            left_lanes, pltpu.roll(turned, 1, 0), pltpu.roll(turned, regions - 1, 0)
        )

    def graph_rows(row):
        return graph_ref[pl.ds(row, regions, stride=BLOCK), :]

    def field_rows(row):
        return graph_rows(64 + 2 * row + (me & 1))

    sources = list(range(16)) + list(range(32, 48)) + list(range(48, 53))
    sources = sources + list(range(56, 60)) + [60, 61]
    for k, row in enumerate(sources):
        index_ref[block(k), :] = graph_rows(row).astype(jnp.int32)
    order_at, ends_at, rim_ends_at, rows_at, rim_order_at = 16, 32, 37, 41, 42
    for k in range(16):
        reward_ref[block(k), :] = graph_rows(16 + k)

    def give_rims():
        rims = []
        for band in bands:
            values = [ext_ref[block(c, band), :] for c in range(4)]
            rims.append(pick(values, *split(rows_at, band)))
        ext_ref[block(4), :] = swap_rims(jnp.concatenate(rims, axis=0))

    def bellman(last):
        for band in bands:
            ext = [ext_ref[block(c, band), :] for c in range(5)]
            values = []
            for c in range(4):
                scores = [
                    pick(ext, *split(4 * k + c, band)) + reward_ref[block(4 * k + c, band), :]
                    for k in range(4)
                ]
                top = jnp.maximum(
                    jnp.maximum(scores[0], scores[1]), jnp.maximum(scores[2], scores[3])
                )
                grown = [jnp.exp(score - top) for score in scores]
                log_total = top + jnp.log((grown[0] + grown[1]) + (grown[2] + grown[3]))
                mask = (region == dest_region - band) & (lane == dest_node - c * LANES)
                values.append(jnp.where(mask, 0.0, log_total))
                if last:
                    for k in range(4):
                        policy_ref[block(4 * k + c, band), :] = jnp.where(
                            mask, 0.0, jnp.exp(scores[k] - log_total)
                        )
            for c in range(4):
                ext_ref[block(c, band), :] = values[c]

    def arrange():
        for band in bands:
            tables = [policy_ref[block(c, band), :] for c in range(16)]
            for k in range(16):
                sorted_ref[block(k, band), :] = pick(tables, *split(order_at + k, band))

    def previous(sums):
        rolled = [pltpu.roll(cells, 1, 1) for cells in sums]
        return [
            jnp.where(first_lane, before, cells)
            for before, cells in zip([jnp.zeros((8, LANES), jnp.float32)] + rolled[:-1], rolled)
        ]

    def push():
        for band in bands:
            visits = [ext_ref[block(c, band), :] for c in range(4)]
            for k in range(16):
                low, high = split(order_at + k, band)
                flow = pick(visits, low, high & 3) * sorted_ref[block(k, band), :]
                flow_ref[block(k, band), :] = flow
        for h in range(1):
            sp = pl.ds(h * 512, 512)
            part, total = prefix_and_total(flow_ref[sp, :], steps)
            part_ref[sp, :] = part
            total_ref[sp, :] = total
        def sums_at(band, o):
            low, high = split(ends_at + o, band)
            inside = jnp.zeros((8, LANES), jnp.float32)
            before = jnp.zeros((8, LANES), jnp.float32)
            whole = jnp.zeros((8, LANES), jnp.float32)
            for c in range(16):
                here = high == c
                inside = jnp.where(here, along(part_ref[block(c, band), :], low), inside)
                whole = jnp.where(here, before, whole)
                before = before + total_ref[block(c, band), :]
            return inside, jnp.where(high == 16, before, whole)

        def between(here, back):
            rolled = [pltpu.roll(cells, 1, 1) for cells in here]
            if back is None:
                earlier = [jnp.zeros((8, LANES), jnp.float32)] * 2
            else:
                earlier = [pltpu.roll(cells, 1, 1) for cells in back]
            shifted = [jnp.where(first_lane, a, b) for a, b in zip(earlier, rolled)]
            return (here[0] - shifted[0]) + (here[1] - shifted[1])

        rims, lasts = [], []
        for band in bands:
            lasts.append(sums_at(band, 3))
            rims.append(between(sums_at(band, 4), lasts[-1]))
        arrived = swap_rims(jnp.concatenate(rims, axis=0))
        arrived = [
            along(arrived[band : band + 8], split(rim_order_at, band)[0]) for band in bands
        ]
        part, total = prefix_and_total(jnp.concatenate(arrived, axis=0), steps)
        for k, band in enumerate(bands):
            marks = [None] + [sums_at(band, o) for o in range(3)] + [lasts[k]]
            for c in range(4):
                arrivals = between(marks[c + 1], marks[c])
                ext_ref[block(c, band), :] = anchor_ref[block(c, band), :] + arrivals
        for band in bands:
            sums = []
            for c in range(4):
                low, high = split(rim_ends_at + c, band)
                inside = along(part[band : band + 8], low)
                sums.append(jnp.where(high == 1, total[band : band + 8], inside))
            for c, (here, back) in enumerate(zip(sums, previous(sums))):
                ext_ref[block(c, band), :] = ext_ref[block(c, band), :] + (here - back)

    for c in range(4):
        ext_ref[block(c), :] = field_rows(c)
        anchor_ref[block(c), :] = field_rows(4 + c)
    for sweep in range(SWEEPS):
        give_rims()
        bellman(sweep == SWEEPS - 1)
    for c in range(4):
        out_ref[pl.ds(16 + c, regions, stride=24), :] = ext_ref[block(c), :]
        ext_ref[block(c), :] = anchor_ref[block(c), :]
    arrange()
    lax.fori_loop(0, SWEEPS, lambda sweep, carry: (push(), carry)[1], 0)
    for c in range(4):
        visits = ext_ref[block(c), :]
        out_ref[pl.ds(20 + c, regions, stride=24), :] = visits
        for k in range(4):
            row = 4 * k + c
            out_ref[pl.ds(row, regions, stride=24), :] = policy_ref[block(row), :] * visits


def gradient_kernel(
    back_ref,
    counts_ref,
    logits_ref,
    feat_ref,
    w_in_ref,
    b_in_ref,
    w_out_ref,
    keep_ref,
    send_ref,
    grad_ref,
    hidden_grad_ref,
):
    chunks = counts_ref.shape[0]
    hid = w_in_ref.shape[1]
    feats = feat_ref.shape[0]
    expected = jnp.sum(back_ref[:, 0:16, :], axis=0)
    gap = counts_ref[...].astype(jnp.float32) - expected
    logit_grad = -gap * (1.0 / (1.0 + jnp.exp(-logits_ref[...])))
    w_rows, b_col, w_col = columns_of(w_in_ref, b_in_ref, w_out_ref)
    out_sum = jnp.zeros((hid, LANES), jnp.float32)
    for c in range(chunks):
        span = pl.ds(c * LANES, LANES)
        hidden = hidden_chunk(w_rows, b_col, feat_ref[:, span])
        grad_row = logit_grad[c : c + 1]
        out_sum = out_sum + hidden * grad_row
        hidden_grad = grad_row * w_col * (1.0 - hidden * hidden)
        hidden_grad_ref[:, span] = hidden_grad.astype(jnp.bfloat16)
    grad_ref[0:feats, :] = contract_lanes(feat_ref[...], hidden_grad_ref[...])
    out_grad = jnp.sum(out_sum.T, axis=0, keepdims=True)
    grad_ref[feats : feats + 8, :] = spread(out_grad, 8)
    first_core = (lax.axis_index("region") & 1) == 0
    left, right = grad_ref[:, 0 : hid // 2], grad_ref[:, hid // 2 : hid]
    keep_ref[...] = jnp.where(first_core, left, right)
    send_ref[...] = jnp.where(first_core, right, left)


def close_kernel(
    scale, half_ref, twin_ref, back_ref, value_ref, visit_ref, in_grad_ref, out_grad_ref
):
    dests, nodes = value_ref.shape
    feats, hid = in_grad_ref.shape
    for c in range(nodes // LANES):
        span = pl.ds(c * LANES, LANES)
        value_ref[:, span] = back_ref[pl.ds(16 + c, dests, stride=24), :]
        visit_ref[:, span] = back_ref[pl.ds(20 + c, dests, stride=24), :]
    first_core = (lax.axis_index("region") & 1) == 0
    half, twin = half_ref[...] * scale, twin_ref[...] * scale
    left = jnp.where(first_core, half, twin)
    right = jnp.where(first_core, twin, half)
    in_grad_ref[:, 0 : hid // 2] = left[0:feats]
    in_grad_ref[:, hid // 2 : hid] = right[0:feats]
    out_grad_ref[:, 0 : hid // 2] = left[feats : feats + 1]
    out_grad_ref[:, hid // 2 : hid] = right[feats : feats + 1]


def by_destination(
    edge_feat,
    w_in,
    b_in,
    w_out,
    targets,
    edge_live,
    boundary_rows,
    dest_nodes,
    anchor_mass,
    prior_value,
    demo_counts,
):
    regions = lax.axis_size("region")
    dests, nodes = prior_value.shape
    edges, feats = edge_feat.shape
    hid = w_in.shape[1]
    chunks = edges // LANES
    f32 = jnp.float32

    def partners(block, *steps):
        return [
            lax.ppermute(block[k], "region", [(i, i ^ step) for i in range(regions)])
            for k, step in enumerate(steps)
        ]

    layer_steps, chip_steps, core_step = (8, 16, 24), (2, 4, 6), 1
    feat_rows = edge_feat.T
    weights = (w_in, b_in.reshape(1, hid), w_out.reshape(1, hid))
    inputs = (
        feat_rows,
        *weights,
        targets.reshape(chunks, LANES),
        edge_live.reshape(chunks, LANES),
        boundary_rows.reshape(1, LANES),
        prior_value,
        anchor_mass,
    )
    *send, logits = pl.pallas_call(
        prepare_kernel,
        out_shape=(jax.ShapeDtypeStruct((128, LANES), f32),) * 4
        + (jax.ShapeDtypeStruct((chunks, LANES), f32),),
        in_specs=[pl.BlockSpec(memory_space=pl.ANY)] * len(inputs),
        scratch_shapes=[pltpu.VMEM(cells.shape, cells.dtype) for cells in inputs]
        + [pltpu.SemaphoreType.DMA((len(inputs),))],
        compiler_params=pltpu.CompilerParams(vmem_limit_bytes=62 * MIB),
        name="prepare",
    )(*inputs)
    layers = jnp.stack([send[0]] + partners(send[1:], *layer_steps))
    graphs = layers[:, :64]
    fields = layers[:, 64:].reshape(4, 8, 8, LANES)
    chip = (lax.axis_index("region") >> 1) & 3

    def for_chip(step):
        part = lax.dynamic_slice_in_dim(fields, (chip ^ step) * 2, 2, axis=2)
        return jnp.concatenate([graphs, part.reshape(4, 16, LANES)], axis=1)

    sends = [for_chip(k) for k in range(4)]
    blocks = jnp.concatenate([sends[0]] + partners(sends[1:], *chip_steps), axis=0)
    (other,) = partners([blocks], core_step)
    offsets = [layer ^ spot for spot in (0,) + chip_steps for layer in (0,) + layer_steps]
    offsets = offsets + [spot ^ core_step for spot in offsets]
    back = pl.pallas_call(
        functools.partial(sweep_kernel, tuple(offsets)),
        out_shape=jax.ShapeDtypeStruct((regions * 24, LANES), f32),
        in_specs=[
            pl.BlockSpec(memory_space=pltpu.SMEM),
            pl.BlockSpec(memory_space=pl.ANY),
            pl.BlockSpec(memory_space=pl.ANY),
        ],
        scratch_shapes=[
            pltpu.VMEM((regions * BLOCK, LANES), f32),
            pltpu.VMEM((regions * 43, LANES), jnp.int32),
            pltpu.VMEM((regions * 16, LANES), f32),
            pltpu.VMEM((regions * 5, LANES), f32),
            pltpu.VMEM((regions * 4, LANES), f32),
            pltpu.VMEM((regions * 16, LANES), f32),
            pltpu.VMEM((regions * 16, LANES), f32),
            pltpu.VMEM((regions * 16, LANES), f32),
            pltpu.VMEM((regions * 16, LANES), f32),
            pltpu.VMEM((regions * 16, LANES), f32),
            pltpu.SemaphoreType.DMA((regions,)),
        ],
        compiler_params=pltpu.CompilerParams(vmem_limit_bytes=16 * MIB),
        name="sweeps",
    )(dest_nodes, blocks, other)
    back = lax.all_to_all(back.reshape(regions, 24, LANES), "region", 0, 0, tiled=True)
    keep, send = pl.pallas_call(
        gradient_kernel,
        out_shape=(jax.ShapeDtypeStruct((feats + 8, hid // 2), f32),) * 2,
        scratch_shapes=[
            pltpu.VMEM((feats + 8, hid), f32),
            pltpu.VMEM((hid, edges), jnp.bfloat16),
        ],
        compiler_params=pltpu.CompilerParams(vmem_limit_bytes=16 * MIB),
        name="gradient",
    )(back, demo_counts.reshape(chunks, LANES), logits, feat_rows, *weights)
    half = keep + partners([send], core_step)[0]
    for steps in (chip_steps, layer_steps):
        near, far, across = partners([half] * 3, *steps)
        half = (half + near) + (far + across)
    (twin,) = partners([half], core_step)
    values, visits, in_grad, out_grad = pl.pallas_call(
        functools.partial(close_kernel, 1.0 / math.sqrt(edges * regions)),
        out_shape=(
            jax.ShapeDtypeStruct((dests, nodes), f32),
            jax.ShapeDtypeStruct((dests, nodes), f32),
            jax.ShapeDtypeStruct((feats, hid), f32),
            jax.ShapeDtypeStruct((1, hid), f32),
        ),
        compiler_params=pltpu.CompilerParams(vmem_limit_bytes=16 * MIB),
        name="close",
    )(half, twin, back.reshape(dests * 24, LANES))
    return (values, visits, in_grad, out_grad.reshape(hid))


def shards(*arrays):
    boundary_rows, prior_value, targets = arrays[6], arrays[9], arrays[4]
    regions = lax.axis_size("region")
    dests, nodes = prior_value.shape
    fits = (nodes, targets.shape[0], boundary_rows.shape[0]) == (512, 2048, LANES)
    if fits and dests == regions == 32:
        return by_destination(*arrays)
    return ring_sweeps(*arrays)


def solution(mesh):
    placed = (
        P("region", None),
        P(),
        P(),
        P(),
        P("region"),
        P("region"),
        P("region"),
        P(),
        P(None, "region"),
        P(None, "region"),
        P("region"),
    )
    return jax.shard_map(
        shards,
        mesh=mesh,
        in_specs=placed,
        out_specs=(P(None, "region"), P(None, "region"), P(), P()),
        check_vma=False,
    )
```

```python
import functools
import math

import jax
import jax.numpy as jnp
from jax import lax
from jax.experimental import pallas as pl
from jax.experimental.pallas import tpu as pltpu
from jax.sharding import PartitionSpec as P

SWEEPS = 4


NEG_FILL = -1e30


def with_halo(cells, sides, width):
    for axis, dim in sides:
        count = lax.axis_size(axis)
        head = lax.slice_in_dim(cells, 0, width, axis=dim)
        tail = lax.slice_in_dim(cells, cells.shape[dim] - width, cells.shape[dim], axis=dim)
        cells = jnp.concatenate(
            [
                lax.ppermute(tail, axis, [(i, (i + 1) % count) for i in range(count)]),
                cells,
                lax.ppermute(head, axis, [((i + 1) % count, i) for i in range(count)]),
            ],
            axis=dim,
        )
    return cells


def sum_over(cells, axis, count):
    if count & (count - 1):
        return lax.psum(cells, axis)

    def partner(block, step):
        return lax.ppermute(block, axis, [(i, i ^ step) for i in range(count)])

    stride = 1
    while stride < count:
        if stride > 1 and stride * 4 <= count:
            near = partner(cells, stride)
            far = partner(cells, 2 * stride)
            across = partner(cells, 3 * stride)
            cells = (cells + near) + (far + across)
            stride *= 4
        else:
            cells = cells + partner(cells, stride)
            stride *= 2
    return cells


def ring_sweeps(
    edge_feat,
    w_in,
    b_in,
    w_out,
    targets,
    edge_live,
    boundary_rows,
    dest_nodes,
    anchor_mass,
    prior_value,
    demo_counts,
):
    node_count = prior_value.shape[1]
    dest_count = prior_value.shape[0]
    rim_width = boundary_rows.shape[0] // 2
    degree = targets.shape[0] // node_count
    region_pos = lax.axis_index("region")
    node_ids = region_pos * node_count + jnp.arange(node_count, dtype=jnp.int32)
    at_dest = node_ids[None, :] == dest_nodes[:, None]
    keep_flow = jnp.where(at_dest, 0.0, 1.0)
    target_idx = targets.reshape(degree, node_count)
    live_mask = edge_live.reshape(degree, node_count) > 0
    left_rows = boundary_rows[:rim_width]
    right_rows = boundary_rows[rim_width:]
    pre_act = jnp.dot(edge_feat, w_in, preferred_element_type=jnp.float32) + b_in
    hidden = jnp.tanh(pre_act)
    logits = jnp.dot(hidden, w_out, precision=lax.Precision.HIGHEST)
    reward = (-jax.nn.softplus(logits)).reshape(degree, node_count)
    values = prior_value
    masked = None
    log_total = None
    for sweep in range(SWEEPS):
        outgoing = jnp.concatenate([values[:, left_rows], values[:, right_rows]], axis=1)
        extend_padded = with_halo(outgoing, (("region", 1),), rim_width)
        extended = jnp.concatenate(
            [values, extend_padded[:, :rim_width], extend_padded[:, 3 * rim_width :]], axis=1
        )
        masked = jnp.where(live_mask[None], extended[:, target_idx] + reward[None], NEG_FILL)
        row_top = jnp.max(masked, axis=1)
        exp_total = jnp.sum(jnp.exp(masked - row_top[:, None, :]), axis=1)
        log_total = row_top + jnp.log(exp_total)
        values = jnp.where(at_dest, 0.0, log_total)
    policy = jnp.exp(masked - log_total[:, None, :]) * keep_flow[:, None, :]
    flat_targets = target_idx.reshape(-1)
    visits = anchor_mass
    for sweep in range(SWEEPS):
        outflow = (visits[:, None, :] * policy).reshape(dest_count, -1)
        arrivals = (
            jnp.zeros((dest_count, node_count + 2 * rim_width), jnp.float32)
            .at[:, flat_targets]
            .add(outflow)
        )
        padded = with_halo(arrivals[:, node_count:], (("region", 1),), rim_width)
        visits = anchor_mass + arrivals[:, :node_count]
        visits = visits.at[:, left_rows].add(padded[:, :rim_width])
        visits = visits.at[:, right_rows].add(padded[:, 3 * rim_width :])
    expected = jnp.sum(visits[:, None, :] * policy, axis=0).reshape(-1)
    residual_gap = demo_counts.astype(jnp.float32) - expected
    logit_grad = -residual_gap * jax.nn.sigmoid(logits)
    out_grad = jnp.dot(logit_grad, hidden, precision=lax.Precision.HIGHEST)
    hidden_grad = (logit_grad[:, None] * w_out[None, :] * (1.0 - hidden * hidden)).astype(
        jnp.bfloat16
    )
    in_grad = lax.dot_general(
        edge_feat, hidden_grad, (((0,), (0,)), ((), ())), preferred_element_type=jnp.float32
    )
    region_count = lax.axis_size("region")
    grad_scale = 1.0 / math.sqrt(targets.shape[0] * region_count)
    packed = jnp.concatenate([in_grad, out_grad[None]], axis=0)
    total = sum_over(packed, "region", region_count) * grad_scale
    return (values, visits, total[:-1], total[-1])


LANES = 128
BLOCK = 80
MIB = 1024 * 1024


def along(table, index):
    return jnp.take_along_axis(table, index, axis=1, mode="promise_in_bounds")


def spread(row, count):
    return jnp.broadcast_to(row, (count, row.shape[1]))


def lane_iota(rows):
    return lax.broadcasted_iota(jnp.int32, (rows, LANES), 1)


def row_iota(rows):
    return lax.broadcasted_iota(jnp.int32, (rows, LANES), 0)


def contract_lanes(left, right):
    return lax.dot_general(
        left.astype(jnp.bfloat16),
        right.astype(jnp.bfloat16),
        (((1,), (1,)), ((), ())),
        preferred_element_type=jnp.float32,
    )


def three_parts(cells):
    high = cells.astype(jnp.bfloat16)
    rest = cells - high.astype(jnp.float32)
    middle = rest.astype(jnp.bfloat16)
    low = (rest - middle.astype(jnp.float32)).astype(jnp.bfloat16)
    return high, middle, low


def prefix_and_total(cells, steps):
    parts = jnp.concatenate(three_parts(cells), axis=1)
    sums = jnp.dot(parts, steps, preferred_element_type=jnp.float32)
    return sums[:, :LANES], sums[:, LANES:]


def step_matrix():
    src = lax.broadcasted_iota(jnp.int32, (3 * LANES, 2 * LANES), 0) & (LANES - 1)
    dst = lax.broadcasted_iota(jnp.int32, (3 * LANES, 2 * LANES), 1)
    return jnp.where(dst > src, 1.0, 0.0).astype(jnp.bfloat16)


def earlier_equal(keys):
    lane = lane_iota(keys.shape[0])
    found = jnp.zeros(keys.shape, jnp.float32)
    for shift in range(1, LANES):
        same = (pltpu.roll(keys, shift, 1) == keys) & (lane >= shift)
        found = found + jnp.where(same, 1.0, 0.0)
    return found


def sort_plan(keys, earlier, steps):
    rows = keys.shape[0]
    low, high = keys & (LANES - 1), keys >> 7
    column = row_iota(LANES)
    band = row_iota(8)
    hists = []
    for c in range(rows):
        in_band = jnp.where(spread(high[c : c + 1], 8) == band, 1.0, 0.0)
        in_lane = jnp.where(spread(low[c : c + 1], LANES) == column, 1.0, 0.0)
        hists.append(contract_lanes(in_band, in_lane))
    total = hists[0]
    for c in range(1, rows):
        total = total + hists[c]
    inside, sums = prefix_and_total(total, steps)
    before = jnp.zeros((1, LANES), jnp.float32)
    starts = []
    for band_row in range(8):
        starts.append(inside[band_row : band_row + 1] + before)
        before = before + sums[band_row : band_row + 1]
    start = jnp.concatenate(starts, axis=0)
    ends = start + total
    ranks = []
    for c in range(rows):
        found = along(start, spread(low[c : c + 1], 8))
        found = jnp.where(spread(high[c : c + 1], 8) == band, found, 0.0)
        ranks.append(jnp.sum(found, axis=0, keepdims=True) + earlier[c : c + 1])
        start = start + hists[c]
    rank = jnp.concatenate(ranks, axis=0).astype(jnp.int32) if rows > 1 else ranks[0].astype(jnp.int32)
    rank_low, rank_high = rank & (LANES - 1), rank >> 7
    out_rows = max(rows, 8)
    out_band = row_iota(out_rows)
    lane = lane_iota(out_rows).astype(jnp.float32)
    order = jnp.zeros((out_rows, LANES), jnp.float32)
    for c in range(rows):
        in_band = spread(rank_high[c : c + 1], out_rows) == out_band
        in_lane = jnp.where(spread(rank_low[c : c + 1], LANES) == column, 1.0, 0.0)
        both = jnp.concatenate(
            [jnp.where(in_band, lane, 0.0), jnp.where(in_band, 1.0, 0.0)], axis=0
        )
        got = contract_lanes(both, in_lane)
        order = order + got[:out_rows] + got[out_rows:] * float(c * LANES)
    return order, ends


def columns_of(w_in_ref, b_in_ref, w_out_ref):
    b_col = spread(b_in_ref[...], LANES).T
    w_col = spread(w_out_ref[...], LANES).T
    w_rows = w_in_ref[...].astype(jnp.float32).T.astype(jnp.bfloat16)
    return w_rows, b_col, w_col


def hidden_chunk(w_rows, b_col, feat):
    return jnp.tanh(jnp.dot(w_rows, feat, preferred_element_type=jnp.float32) + b_col)


def prepare_kernel(
    feat_hbm,
    w_in_hbm,
    b_in_hbm,
    w_out_hbm,
    targets_hbm,
    live_hbm,
    rows_hbm,
    prior_hbm,
    anchor_hbm,
    counts_hbm,
    send_0_ref,
    send_1_ref,
    send_2_ref,
    send_3_ref,
    logits_ref,
    feat_ref,
    w_in_ref,
    b_in_ref,
    w_out_ref,
    targets_ref,
    live_ref,
    rows_ref,
    prior_ref,
    anchor_ref,
    counts_ref,
    copy_sem,
):
    chunks = targets_ref.shape[0]
    pairs = (
        (targets_hbm, targets_ref),
        (rows_hbm, rows_ref),
        (w_in_hbm, w_in_ref),
        (b_in_hbm, b_in_ref),
        (w_out_hbm, w_out_ref),
        (feat_hbm, feat_ref),
        (live_hbm, live_ref),
        (prior_hbm, prior_ref),
        (anchor_hbm, anchor_ref),
        (counts_hbm, counts_ref),
    )
    copies = [
        pltpu.make_async_copy(src, dst, copy_sem.at[k]) for k, (src, dst) in enumerate(pairs)
    ]
    for copy in copies:
        copy.start()
    for copy in copies[:2]:
        copy.wait()
    steps = step_matrix()
    targets = targets_ref[...]
    rows = rows_ref[...]
    earlier = earlier_equal(jnp.concatenate([targets, spread(rows, 8)], axis=0))
    order, ends = sort_plan(targets, earlier[:chunks], steps)
    rim_order, rim_ends = sort_plan(rows, earlier[chunks : chunks + 1], steps)
    for copy in copies[2:]:
        copy.wait()
    w_rows, b_col, w_col = columns_of(w_in_ref, b_in_ref, w_out_ref)
    logit_rows = []
    for c in range(chunks):
        hidden = hidden_chunk(w_rows, b_col, feat_ref[:, pl.ds(c * LANES, LANES)])
        logit_rows.append(jnp.sum(hidden * w_col, axis=0, keepdims=True))
    logits = jnp.concatenate(logit_rows, axis=0)
    logits_ref[0:chunks, :] = logits
    logits_ref[chunks : 2 * chunks, :] = counts_ref[...].astype(jnp.float32)
    reward = -(jnp.maximum(logits, 0.0) + jnp.log1p(jnp.exp(-jnp.abs(logits))))
    reward = jnp.where(live_ref[...] > 0, reward, NEG_FILL)
    graph = jnp.concatenate(
        [
            targets.astype(jnp.float32),
            reward,
            order,
            ends,
            rim_ends[0:4],
            rows.astype(jnp.float32),
            rim_order[0:1],
            jnp.zeros((2, LANES), jnp.float32),
        ],
        axis=0,
    )
    layer = lax.axis_index("region") >> 3
    for k, send_ref in enumerate((send_0_ref, send_1_ref, send_2_ref, send_3_ref)):
        send_ref[0:64, :] = graph
        dests = pl.ds(pl.multiple_of((layer ^ k) * 8, 8), 8)
        for c in range(4):
            span = pl.ds(c * LANES, LANES)
            send_ref[pl.ds(64 + 8 * c, 8), :] = prior_ref[dests, span]
            send_ref[pl.ds(96 + 8 * c, 8), :] = anchor_ref[dests, span]


def keep_kernel(src_ref, dst_ref):
    dst_ref[...] = src_ref[...]


def pack_kernel(*refs):
    layer_refs, send_refs = refs[:4], refs[4:]
    chip = (lax.axis_index("region") >> 1) & 3
    for k, send_ref in enumerate(send_refs):
        start = (chip ^ k) * 2
        for z, layer_ref in enumerate(layer_refs):
            send_ref[z, 0:64, :] = layer_ref[0:64, :]
            for c in range(8):
                row = pl.ds(64 + 8 * c + start, 2)
                send_ref[z, pl.ds(64 + 2 * c, 2), :] = layer_ref[row, :]


def sweep_kernel(
    offsets,
    dest_nodes_ref,
    own_ref,
    other_ref,
    out_ref,
    graph_ref,
    index_ref,
    reward_ref,
    ext_ref,
    anchor_ref,
    policy_ref,
    sorted_ref,
    flow_ref,
    part_ref,
    total_ref,
):
    me = lax.axis_index("region")
    dest = dest_nodes_ref[me]
    regions = len(offsets)
    half = own_ref.shape[0]
    for spot, offset in enumerate(offsets):
        place = pl.ds(pl.multiple_of((me ^ offset) * BLOCK, BLOCK), BLOCK)
        graph_ref[place, :] = own_ref[spot] if spot < half else other_ref[spot - half]
    dest_region, dest_node = dest // 512, dest % 512
    bands = range(0, regions, 8)
    region = lax.broadcasted_iota(jnp.int32, (8, LANES), 0)
    lane = lane_iota(8)
    first_lane = lane == 0
    left_lanes = lane_iota(regions) < LANES // 2
    steps = step_matrix()

    def block(k, band=None):
        if band is None:
            return pl.ds(k * regions, regions)
        return pl.ds(k * regions + band, 8)

    def split(k, band):
        cells = index_ref[block(k, band), :]
        return cells & (LANES - 1), cells >> 7

    def pick(tables, low, high):
        found = along(tables[0], low)
        for c, table in enumerate(tables[1:], 1):
            found = jnp.where(high == c, along(table, low), found)
        return found

    def swap_rims(rims):
        turned = pltpu.roll(rims, LANES // 2, 1)
        return jnp.where(
            left_lanes, pltpu.roll(turned, 1, 0), pltpu.roll(turned, regions - 1, 0)
        )

    def graph_rows(row):
        return graph_ref[pl.ds(row, regions, stride=BLOCK), :]

    def field_rows(row):
        return graph_rows(64 + 2 * row + (me & 1))

    sources = list(range(16)) + list(range(32, 48)) + list(range(48, 53))
    sources = sources + list(range(56, 60)) + [60, 61]
    for k, row in enumerate(sources):
        index_ref[block(k), :] = graph_rows(row).astype(jnp.int32)
    order_at, ends_at, rim_ends_at, rows_at, rim_order_at = 16, 32, 37, 41, 42
    for k in range(16):
        reward_ref[block(k), :] = graph_rows(16 + k)

    def give_rims():
        rims = []
        for band in bands:
            values = [ext_ref[block(c, band), :] for c in range(4)]
            rims.append(pick(values, *split(rows_at, band)))
        ext_ref[block(4), :] = swap_rims(jnp.concatenate(rims, axis=0))

    def bellman(last):
        for band in bands:
            ext = [ext_ref[block(c, band), :] for c in range(5)]
            values = []
            for c in range(4):
                scores = [
                    pick(ext, *split(4 * k + c, band)) + reward_ref[block(4 * k + c, band), :]
                    for k in range(4)
                ]
                top = jnp.maximum(
                    jnp.maximum(scores[0], scores[1]), jnp.maximum(scores[2], scores[3])
                )
                grown = [jnp.exp(score - top) for score in scores]
                log_total = top + jnp.log((grown[0] + grown[1]) + (grown[2] + grown[3]))
                mask = (region == dest_region - band) & (lane == dest_node - c * LANES)
                values.append(jnp.where(mask, 0.0, log_total))
                if last:
                    for k in range(4):
                        policy_ref[block(4 * k + c, band), :] = jnp.where(
                            mask, 0.0, jnp.exp(scores[k] - log_total)
                        )
            for c in range(4):
                ext_ref[block(c, band), :] = values[c]

    def arrange():
        for band in bands:
            tables = [policy_ref[block(c, band), :] for c in range(16)]
            for k in range(16):
                sorted_ref[block(k, band), :] = pick(tables, *split(order_at + k, band))

    def previous(sums):
        rolled = [pltpu.roll(cells, 1, 1) for cells in sums]
        return [
            jnp.where(first_lane, before, cells)
            for before, cells in zip([jnp.zeros((8, LANES), jnp.float32)] + rolled[:-1], rolled)
        ]

    def push():
        for band in bands:
            visits = [ext_ref[block(c, band), :] for c in range(4)]
            for k in range(16):
                low, high = split(order_at + k, band)
                flow = pick(visits, low, high & 3) * sorted_ref[block(k, band), :]
                flow_ref[block(k, band), :] = flow
        for h in range(1):
            sp = pl.ds(h * 512, 512)
            part, total = prefix_and_total(flow_ref[sp, :], steps)
            part_ref[sp, :] = part
            total_ref[sp, :] = total
        def sums_at(band, o):
            low, high = split(ends_at + o, band)
            inside = jnp.zeros((8, LANES), jnp.float32)
            before = jnp.zeros((8, LANES), jnp.float32)
            whole = jnp.zeros((8, LANES), jnp.float32)
            for c in range(16):
                here = high == c
                inside = jnp.where(here, along(part_ref[block(c, band), :], low), inside)
                whole = jnp.where(here, before, whole)
                before = before + total_ref[block(c, band), :]
            return inside, jnp.where(high == 16, before, whole)

        def between(here, back):
            rolled = [pltpu.roll(cells, 1, 1) for cells in here]
            if back is None:
                earlier = [jnp.zeros((8, LANES), jnp.float32)] * 2
            else:
                earlier = [pltpu.roll(cells, 1, 1) for cells in back]
            shifted = [jnp.where(first_lane, a, b) for a, b in zip(earlier, rolled)]
            return (here[0] - shifted[0]) + (here[1] - shifted[1])

        rims, lasts = [], []
        for band in bands:
            lasts.append(sums_at(band, 3))
            rims.append(between(sums_at(band, 4), lasts[-1]))
        arrived = swap_rims(jnp.concatenate(rims, axis=0))
        arrived = [
            along(arrived[band : band + 8], split(rim_order_at, band)[0]) for band in bands
        ]
        part, total = prefix_and_total(jnp.concatenate(arrived, axis=0), steps)
        for k, band in enumerate(bands):
            marks = [None] + [sums_at(band, o) for o in range(3)] + [lasts[k]]
            for c in range(4):
                arrivals = between(marks[c + 1], marks[c])
                ext_ref[block(c, band), :] = anchor_ref[block(c, band), :] + arrivals
        for band in bands:
            sums = []
            for c in range(4):
                low, high = split(rim_ends_at + c, band)
                inside = along(part[band : band + 8], low)
                sums.append(jnp.where(high == 1, total[band : band + 8], inside))
            for c, (here, back) in enumerate(zip(sums, previous(sums))):
                ext_ref[block(c, band), :] = ext_ref[block(c, band), :] + (here - back)

    for c in range(4):
        ext_ref[block(c), :] = field_rows(c)
        anchor_ref[block(c), :] = field_rows(4 + c)
    for sweep in range(SWEEPS):
        give_rims()
        bellman(sweep == SWEEPS - 1)
    for c in range(4):
        out_ref[pl.ds(16 + c, regions, stride=24), :] = ext_ref[block(c), :]
        ext_ref[block(c), :] = anchor_ref[block(c), :]
    arrange()
    lax.fori_loop(0, SWEEPS, lambda sweep, carry: (push(), carry)[1], 0)
    for c in range(4):
        visits = ext_ref[block(c), :]
        out_ref[pl.ds(20 + c, regions, stride=24), :] = visits
        for k in range(4):
            row = 4 * k + c
            out_ref[pl.ds(row, regions, stride=24), :] = policy_ref[block(row), :] * visits


def gradient_kernel(
    back_ref,
    logits_ref,
    feat_ref,
    w_in_ref,
    b_in_ref,
    w_out_ref,
    keep_ref,
    send_ref,
    grad_ref,
    hidden_grad_ref,
):
    chunks = logits_ref.shape[0] // 2
    hid = w_in_ref.shape[1]
    feats = feat_ref.shape[0]
    expected = jnp.sum(back_ref[:, 0:16, :], axis=0)
    gap = logits_ref[chunks : 2 * chunks, :] - expected
    logit_grad = -gap * (1.0 / (1.0 + jnp.exp(-logits_ref[0:chunks, :])))
    w_rows, b_col, w_col = columns_of(w_in_ref, b_in_ref, w_out_ref)
    out_sum = jnp.zeros((hid, LANES), jnp.float32)
    for c in range(chunks):
        span = pl.ds(c * LANES, LANES)
        hidden = hidden_chunk(w_rows, b_col, feat_ref[:, span])
        grad_row = logit_grad[c : c + 1]
        out_sum = out_sum + hidden * grad_row
        hidden_grad = grad_row * w_col * (1.0 - hidden * hidden)
        hidden_grad_ref[:, span] = hidden_grad.astype(jnp.bfloat16)
    grad_ref[0:feats, :] = contract_lanes(feat_ref[...], hidden_grad_ref[...])
    out_grad = jnp.sum(out_sum.T, axis=0, keepdims=True)
    grad_ref[feats : feats + 8, :] = spread(out_grad, 8)
    first_core = (lax.axis_index("region") & 1) == 0
    left, right = grad_ref[:, 0 : hid // 2], grad_ref[:, hid // 2 : hid]
    keep_ref[...] = jnp.where(first_core, left, right)
    send_ref[...] = jnp.where(first_core, right, left)


def close_kernel(
    scale, half_ref, twin_ref, back_ref, value_ref, visit_ref, in_grad_ref, out_grad_ref
):
    dests, nodes = value_ref.shape
    feats, hid = in_grad_ref.shape
    for c in range(nodes // LANES):
        span = pl.ds(c * LANES, LANES)
        value_ref[:, span] = back_ref[pl.ds(16 + c, dests, stride=24), :]
        visit_ref[:, span] = back_ref[pl.ds(20 + c, dests, stride=24), :]
    first_core = (lax.axis_index("region") & 1) == 0
    half, twin = half_ref[...] * scale, twin_ref[...] * scale
    left = jnp.where(first_core, half, twin)
    right = jnp.where(first_core, twin, half)
    in_grad_ref[:, 0 : hid // 2] = left[0:feats]
    in_grad_ref[:, hid // 2 : hid] = right[0:feats]
    out_grad_ref[:, 0 : hid // 2] = left[feats : feats + 1]
    out_grad_ref[:, hid // 2 : hid] = right[feats : feats + 1]


def by_destination(
    edge_feat,
    w_in,
    b_in,
    w_out,
    targets,
    edge_live,
    boundary_rows,
    dest_nodes,
    anchor_mass,
    prior_value,
    demo_counts,
):
    regions = lax.axis_size("region")
    dests, nodes = prior_value.shape
    edges, feats = edge_feat.shape
    hid = w_in.shape[1]
    chunks = edges // LANES
    f32 = jnp.float32

    def partners(block, *steps):
        return [
            lax.ppermute(block[k], "region", [(i, i ^ step) for i in range(regions)])
            for k, step in enumerate(steps)
        ]

    layer_steps, chip_steps, core_step = (8, 16, 24), (2, 4, 6), 1
    feat_rows = edge_feat.T
    weights = (w_in, b_in.reshape(1, hid), w_out.reshape(1, hid))
    inputs = (
        feat_rows,
        *weights,
        targets.reshape(chunks, LANES),
        edge_live.reshape(chunks, LANES),
        boundary_rows.reshape(1, LANES),
        prior_value,
        anchor_mass,
        demo_counts.reshape(chunks, LANES),
    )
    *send, logits = pl.pallas_call(
        prepare_kernel,
        out_shape=(jax.ShapeDtypeStruct((128, LANES), f32),) * 4
        + (jax.ShapeDtypeStruct((2 * chunks, LANES), f32),),
        in_specs=[pl.BlockSpec(memory_space=pl.ANY)] * len(inputs),
        scratch_shapes=[pltpu.VMEM(cells.shape, cells.dtype) for cells in inputs]
        + [pltpu.SemaphoreType.DMA((len(inputs),))],
        compiler_params=pltpu.CompilerParams(vmem_limit_bytes=62 * MIB),
        name="prepare",
    )(*inputs)
    kept = pl.pallas_call(
        keep_kernel,
        out_shape=jax.ShapeDtypeStruct((128, LANES), f32),
        compiler_params=pltpu.CompilerParams(vmem_limit_bytes=16 * MIB),
        name="keep",
    )(send[0])
    layers = [kept] + partners(send[1:], *layer_steps)
    sends = pl.pallas_call(
        pack_kernel,
        out_shape=(jax.ShapeDtypeStruct((4, 80, LANES), f32),) * 4,
        compiler_params=pltpu.CompilerParams(vmem_limit_bytes=16 * MIB),
        name="pack",
    )(*layers)
    blocks = jnp.concatenate([sends[0]] + partners(sends[1:], *chip_steps), axis=0)
    (other,) = partners([blocks], core_step)
    offsets = [layer ^ spot for spot in (0,) + chip_steps for layer in (0,) + layer_steps]
    offsets = offsets + [spot ^ core_step for spot in offsets]
    back = pl.pallas_call(
        functools.partial(sweep_kernel, tuple(offsets)),
        out_shape=jax.ShapeDtypeStruct((regions * 24, LANES), f32),
        in_specs=[
            pl.BlockSpec(memory_space=pltpu.SMEM),
            pl.BlockSpec(memory_space=pltpu.VMEM),
            pl.BlockSpec(memory_space=pltpu.VMEM),
        ],
        scratch_shapes=[
            pltpu.VMEM((regions * BLOCK, LANES), f32),
            pltpu.VMEM((regions * 43, LANES), jnp.int32),
            pltpu.VMEM((regions * 16, LANES), f32),
            pltpu.VMEM((regions * 5, LANES), f32),
            pltpu.VMEM((regions * 4, LANES), f32),
            pltpu.VMEM((regions * 16, LANES), f32),
            pltpu.VMEM((regions * 16, LANES), f32),
            pltpu.VMEM((regions * 16, LANES), f32),
            pltpu.VMEM((regions * 16, LANES), f32),
            pltpu.VMEM((regions * 16, LANES), f32),
        ],
        compiler_params=pltpu.CompilerParams(vmem_limit_bytes=16 * MIB),
        name="sweeps",
    )(dest_nodes, blocks, other)
    back = lax.all_to_all(back.reshape(regions, 24, LANES), "region", 0, 0, tiled=True)
    keep, send = pl.pallas_call(
        gradient_kernel,
        out_shape=(jax.ShapeDtypeStruct((feats + 8, hid // 2), f32),) * 2,
        scratch_shapes=[
            pltpu.VMEM((feats + 8, hid), f32),
            pltpu.VMEM((hid, edges), jnp.bfloat16),
        ],
        compiler_params=pltpu.CompilerParams(vmem_limit_bytes=16 * MIB),
        name="gradient",
    )(back, logits, feat_rows, *weights)
    half = keep + partners([send], core_step)[0]
    for steps in (chip_steps, layer_steps):
        near, far, across = partners([half] * 3, *steps)
        half = (half + near) + (far + across)
    (twin,) = partners([half], core_step)
    values, visits, in_grad, out_grad = pl.pallas_call(
        functools.partial(close_kernel, 1.0 / math.sqrt(edges * regions)),
        out_shape=(
            jax.ShapeDtypeStruct((dests, nodes), f32),
            jax.ShapeDtypeStruct((dests, nodes), f32),
            jax.ShapeDtypeStruct((feats, hid), f32),
            jax.ShapeDtypeStruct((1, hid), f32),
        ),
        compiler_params=pltpu.CompilerParams(vmem_limit_bytes=16 * MIB),
        name="close",
    )(half, twin, back.reshape(dests * 24, LANES))
    return (values, visits, in_grad, out_grad.reshape(hid))


def shards(*arrays):
    boundary_rows, prior_value, targets = arrays[6], arrays[9], arrays[4]
    regions = lax.axis_size("region")
    dests, nodes = prior_value.shape
    fits = (nodes, targets.shape[0], boundary_rows.shape[0]) == (512, 2048, LANES)
    if fits and dests == regions == 32:
        return by_destination(*arrays)
    return ring_sweeps(*arrays)


def solution(mesh):
    placed = (
        P("region", None),
        P(),
        P(),
        P(),
        P("region"),
        P("region"),
        P("region"),
        P(),
        P(None, "region"),
        P(None, "region"),
        P("region"),
    )
    return jax.shard_map(
        shards,
        mesh=mesh,
        in_specs=placed,
        out_specs=(P(None, "region"), P(None, "region"), P(), P()),
        check_vma=False,
    )
```

```python
import functools
import math

import jax
import jax.numpy as jnp
from jax import lax
from jax.experimental import pallas as pl
from jax.experimental.pallas import tpu as pltpu
from jax.sharding import PartitionSpec as P

SWEEPS = 4


NEG_FILL = -1e30


def with_halo(cells, sides, width):
    for axis, dim in sides:
        count = lax.axis_size(axis)
        head = lax.slice_in_dim(cells, 0, width, axis=dim)
        tail = lax.slice_in_dim(cells, cells.shape[dim] - width, cells.shape[dim], axis=dim)
        cells = jnp.concatenate(
            [
                lax.ppermute(tail, axis, [(i, (i + 1) % count) for i in range(count)]),
                cells,
                lax.ppermute(head, axis, [((i + 1) % count, i) for i in range(count)]),
            ],
            axis=dim,
        )
    return cells


def sum_over(cells, axis, count):
    if count & (count - 1):
        return lax.psum(cells, axis)

    def partner(block, step):
        return lax.ppermute(block, axis, [(i, i ^ step) for i in range(count)])

    stride = 1
    while stride < count:
        if stride > 1 and stride * 4 <= count:
            near = partner(cells, stride)
            far = partner(cells, 2 * stride)
            across = partner(cells, 3 * stride)
            cells = (cells + near) + (far + across)
            stride *= 4
        else:
            cells = cells + partner(cells, stride)
            stride *= 2
    return cells


def ring_sweeps(
    edge_feat,
    w_in,
    b_in,
    w_out,
    targets,
    edge_live,
    boundary_rows,
    dest_nodes,
    anchor_mass,
    prior_value,
    demo_counts,
):
    node_count = prior_value.shape[1]
    dest_count = prior_value.shape[0]
    rim_width = boundary_rows.shape[0] // 2
    degree = targets.shape[0] // node_count
    region_pos = lax.axis_index("region")
    node_ids = region_pos * node_count + jnp.arange(node_count, dtype=jnp.int32)
    at_dest = node_ids[None, :] == dest_nodes[:, None]
    keep_flow = jnp.where(at_dest, 0.0, 1.0)
    target_idx = targets.reshape(degree, node_count)
    live_mask = edge_live.reshape(degree, node_count) > 0
    left_rows = boundary_rows[:rim_width]
    right_rows = boundary_rows[rim_width:]
    pre_act = jnp.dot(edge_feat, w_in, preferred_element_type=jnp.float32) + b_in
    hidden = jnp.tanh(pre_act)
    logits = jnp.dot(hidden, w_out, precision=lax.Precision.HIGHEST)
    reward = (-jax.nn.softplus(logits)).reshape(degree, node_count)
    values = prior_value
    masked = None
    log_total = None
    for sweep in range(SWEEPS):
        outgoing = jnp.concatenate([values[:, left_rows], values[:, right_rows]], axis=1)
        extend_padded = with_halo(outgoing, (("region", 1),), rim_width)
        extended = jnp.concatenate(
            [values, extend_padded[:, :rim_width], extend_padded[:, 3 * rim_width :]], axis=1
        )
        masked = jnp.where(live_mask[None], extended[:, target_idx] + reward[None], NEG_FILL)
        row_top = jnp.max(masked, axis=1)
        exp_total = jnp.sum(jnp.exp(masked - row_top[:, None, :]), axis=1)
        log_total = row_top + jnp.log(exp_total)
        values = jnp.where(at_dest, 0.0, log_total)
    policy = jnp.exp(masked - log_total[:, None, :]) * keep_flow[:, None, :]
    flat_targets = target_idx.reshape(-1)
    visits = anchor_mass
    for sweep in range(SWEEPS):
        outflow = (visits[:, None, :] * policy).reshape(dest_count, -1)
        arrivals = (
            jnp.zeros((dest_count, node_count + 2 * rim_width), jnp.float32)
            .at[:, flat_targets]
            .add(outflow)
        )
        padded = with_halo(arrivals[:, node_count:], (("region", 1),), rim_width)
        visits = anchor_mass + arrivals[:, :node_count]
        visits = visits.at[:, left_rows].add(padded[:, :rim_width])
        visits = visits.at[:, right_rows].add(padded[:, 3 * rim_width :])
    expected = jnp.sum(visits[:, None, :] * policy, axis=0).reshape(-1)
    residual_gap = demo_counts.astype(jnp.float32) - expected
    logit_grad = -residual_gap * jax.nn.sigmoid(logits)
    out_grad = jnp.dot(logit_grad, hidden, precision=lax.Precision.HIGHEST)
    hidden_grad = (logit_grad[:, None] * w_out[None, :] * (1.0 - hidden * hidden)).astype(
        jnp.bfloat16
    )
    in_grad = lax.dot_general(
        edge_feat, hidden_grad, (((0,), (0,)), ((), ())), preferred_element_type=jnp.float32
    )
    region_count = lax.axis_size("region")
    grad_scale = 1.0 / math.sqrt(targets.shape[0] * region_count)
    packed = jnp.concatenate([in_grad, out_grad[None]], axis=0)
    total = sum_over(packed, "region", region_count) * grad_scale
    return (values, visits, total[:-1], total[-1])


LANES = 128
BLOCK = 80
MIB = 1024 * 1024


def along(table, index):
    return jnp.take_along_axis(table, index, axis=1, mode="promise_in_bounds")


def spread(row, count):
    return jnp.broadcast_to(row, (count, row.shape[1]))


def lane_iota(rows):
    return lax.broadcasted_iota(jnp.int32, (rows, LANES), 1)


def row_iota(rows):
    return lax.broadcasted_iota(jnp.int32, (rows, LANES), 0)


def contract_lanes(left, right):
    return lax.dot_general(
        left.astype(jnp.bfloat16),
        right.astype(jnp.bfloat16),
        (((1,), (1,)), ((), ())),
        preferred_element_type=jnp.float32,
    )


def three_parts(cells):
    high = cells.astype(jnp.bfloat16)
    rest = cells - high.astype(jnp.float32)
    middle = rest.astype(jnp.bfloat16)
    low = (rest - middle.astype(jnp.float32)).astype(jnp.bfloat16)
    return high, middle, low


def prefix_and_total(cells, steps):
    parts = jnp.concatenate(three_parts(cells), axis=1)
    sums = jnp.dot(parts, steps, preferred_element_type=jnp.float32)
    return sums[:, :LANES], sums[:, LANES:]


def step_matrix():
    src = lax.broadcasted_iota(jnp.int32, (3 * LANES, 2 * LANES), 0) & (LANES - 1)
    dst = lax.broadcasted_iota(jnp.int32, (3 * LANES, 2 * LANES), 1)
    return jnp.where(dst > src, 1.0, 0.0).astype(jnp.bfloat16)


def earlier_equal(keys):
    lane = lane_iota(keys.shape[0])
    found = jnp.zeros(keys.shape, jnp.float32)
    for shift in range(1, LANES):
        same = (pltpu.roll(keys, shift, 1) == keys) & (lane >= shift)
        found = found + jnp.where(same, 1.0, 0.0)
    return found


def one_hot_lanes(row):
    return jnp.where(spread(row, LANES) == row_iota(LANES), 1.0, 0.0)


def histograms(keys):
    low, high = keys & (LANES - 1), keys >> 7
    found = []
    for c in range(keys.shape[0]):
        in_band = jnp.where(spread(high[c : c + 1], 8) == row_iota(8), 1.0, 0.0)
        found.append(contract_lanes(in_band, one_hot_lanes(low[c : c + 1])))
    return found


def order_of(keys, earlier, hists, start):
    rows = keys.shape[0]
    low, high = keys & (LANES - 1), keys >> 7
    ranks = []
    for c in range(rows):
        found = along(start, spread(low[c : c + 1], 8))
        found = jnp.where(spread(high[c : c + 1], 8) == row_iota(8), found, 0.0)
        ranks.append(jnp.sum(found, axis=0, keepdims=True) + earlier[c : c + 1])
        start = start + hists[c]
    lane = lane_iota(8).astype(jnp.float32)
    order = jnp.zeros((8, LANES), jnp.float32)
    for c in range(rows):
        rank = ranks[c].astype(jnp.int32)
        in_band = spread(rank >> 7, 8) == row_iota(8)
        both = jnp.concatenate(
            [jnp.where(in_band, lane, 0.0), jnp.where(in_band, 1.0, 0.0)], axis=0
        )
        got = contract_lanes(both, one_hot_lanes(rank & (LANES - 1)))
        order = order + got[:8] + got[8:] * float(c * LANES)
    return order


def sort_plans(groups, steps):
    hists = [histograms(keys) for keys, _ in groups]
    totals = [functools.reduce(jnp.add, found) for found in hists]
    inside, sums = prefix_and_total(jnp.concatenate(totals, axis=0), steps)
    plans = []
    for k, (keys, earlier) in enumerate(groups):
        before = jnp.zeros((1, LANES), jnp.float32)
        starts = []
        for row in range(8 * k, 8 * k + 8):
            starts.append(inside[row : row + 1] + before)
            before = before + sums[row : row + 1]
        start = jnp.concatenate(starts, axis=0)
        plans.append((order_of(keys, earlier, hists[k], start), start + totals[k]))
    return plans


def columns_of(w_in_ref, b_in_ref, w_out_ref):
    b_col = spread(b_in_ref[...], LANES).T
    w_col = spread(w_out_ref[...], LANES).T
    w_rows = w_in_ref[...].astype(jnp.float32).T.astype(jnp.bfloat16)
    return w_rows, b_col, w_col


def hidden_chunk(w_rows, b_col, feat):
    return jnp.tanh(jnp.dot(w_rows, feat, preferred_element_type=jnp.float32) + b_col)


def prepare_kernel(
    feat_hbm,
    w_in_hbm,
    b_in_hbm,
    w_out_hbm,
    targets_hbm,
    live_hbm,
    rows_hbm,
    prior_hbm,
    anchor_hbm,
    counts_hbm,
    send_0_ref,
    send_1_ref,
    send_2_ref,
    send_3_ref,
    logits_ref,
    feat_ref,
    w_in_ref,
    b_in_ref,
    w_out_ref,
    targets_ref,
    live_ref,
    rows_ref,
    prior_ref,
    anchor_ref,
    counts_ref,
    copy_sem,
):
    chunks = targets_ref.shape[0]
    pairs = (
        (targets_hbm, targets_ref),
        (rows_hbm, rows_ref),
        (w_in_hbm, w_in_ref),
        (b_in_hbm, b_in_ref),
        (w_out_hbm, w_out_ref),
        (feat_hbm, feat_ref),
        (live_hbm, live_ref),
        (prior_hbm, prior_ref),
        (anchor_hbm, anchor_ref),
        (counts_hbm, counts_ref),
    )
    copies = [
        pltpu.make_async_copy(src, dst, copy_sem.at[k]) for k, (src, dst) in enumerate(pairs)
    ]
    for copy in copies:
        copy.start()
    for copy in copies[:2]:
        copy.wait()
    steps = step_matrix()
    targets = targets_ref[...]
    rows = rows_ref[...]
    earlier = earlier_equal(jnp.concatenate([targets, spread(rows, 8)], axis=0))
    groups = []
    for half in range(2):
        picked = [4 * k + 2 * half + c for k in range(chunks // 4) for c in range(2)]
        groups.append(
            [
                jnp.concatenate([cells[j : j + 1] for j in picked], axis=0)
                for cells in (targets, earlier)
            ]
        )
    groups.append((rows, earlier[chunks : chunks + 1]))
    plans = sort_plans(groups, steps)
    rim_order, rim_ends = plans[2]
    for copy in copies[2:]:
        copy.wait()
    w_rows, b_col, w_col = columns_of(w_in_ref, b_in_ref, w_out_ref)
    logit_rows = []
    for c in range(chunks):
        hidden = hidden_chunk(w_rows, b_col, feat_ref[:, pl.ds(c * LANES, LANES)])
        logit_rows.append(jnp.sum(hidden * w_col, axis=0, keepdims=True))
    logits = jnp.concatenate(logit_rows, axis=0)
    logits_ref[0:chunks, :] = logits
    logits_ref[chunks : 2 * chunks, :] = counts_ref[...].astype(jnp.float32)
    reward = -(jnp.maximum(logits, 0.0) + jnp.log1p(jnp.exp(-jnp.abs(logits))))
    reward = jnp.where(live_ref[...] > 0, reward, NEG_FILL)
    graph = jnp.concatenate(
        [
            targets.astype(jnp.float32),
            reward,
            plans[0][0],
            plans[1][0],
            plans[0][1][0:5],
            plans[1][1][0:5],
            rim_ends[0:4],
            rows.astype(jnp.float32),
            rim_order[0:1],
        ],
        axis=0,
    )
    layer = lax.axis_index("region") >> 3
    for k, send_ref in enumerate((send_0_ref, send_1_ref, send_2_ref, send_3_ref)):
        send_ref[0:64, :] = graph
        dests = pl.ds(pl.multiple_of((layer ^ k) * 8, 8), 8)
        for c in range(4):
            span = pl.ds(c * LANES, LANES)
            send_ref[pl.ds(64 + 8 * c, 8), :] = prior_ref[dests, span]
            send_ref[pl.ds(96 + 8 * c, 8), :] = anchor_ref[dests, span]


def keep_kernel(src_ref, dst_ref):
    dst_ref[...] = src_ref[...]


def pack_kernel(*refs):
    layer_refs, send_refs = refs[:4], refs[4:]
    chip = (lax.axis_index("region") >> 1) & 3
    for k, send_ref in enumerate(send_refs):
        start = (chip ^ k) * 2
        for z, layer_ref in enumerate(layer_refs):
            send_ref[z, 0:64, :] = layer_ref[0:64, :]
            for c in range(8):
                row = pl.ds(64 + 8 * c + start, 2)
                send_ref[z, pl.ds(64 + 2 * c, 2), :] = layer_ref[row, :]


def sweep_kernel(
    offsets,
    dest_nodes_ref,
    *refs,
):
    block_refs, refs = refs[:8], refs[8:]
    (
        out_ref,
        graph_ref,
    index_ref,
    reward_ref,
    ext_ref,
    anchor_ref,
    policy_ref,
    sorted_ref,
    flow_ref,
    part_ref,
    total_ref,
    ) = refs
    me = lax.axis_index("region")
    dest = dest_nodes_ref[me]
    regions = len(offsets)
    for spot, offset in enumerate(offsets):
        place = pl.ds(pl.multiple_of((me ^ offset) * BLOCK, BLOCK), BLOCK)
        graph_ref[place, :] = block_refs[spot // 4][spot % 4]
    dest_region, dest_node = dest // 512, dest % 512
    bands = range(0, regions, 8)
    region = lax.broadcasted_iota(jnp.int32, (8, LANES), 0)
    lane = lane_iota(8)
    first_lane = lane == 0
    left_lanes = lane_iota(regions) < LANES // 2
    steps = step_matrix()

    def block(k, band=None):
        if band is None:
            return pl.ds(k * regions, regions)
        return pl.ds(k * regions + band, 8)

    def split(k, band):
        cells = index_ref[block(k, band), :]
        return cells & (LANES - 1), cells >> 7

    def pick(tables, low, high):
        found = along(tables[0], low)
        for c, table in enumerate(tables[1:], 1):
            found = jnp.where(high == c, along(table, low), found)
        return found

    def swap_rims(rims):
        turned = pltpu.roll(rims, LANES // 2, 1)
        return jnp.where(
            left_lanes, pltpu.roll(turned, 1, 0), pltpu.roll(turned, regions - 1, 0)
        )

    def graph_rows(row):
        return graph_ref[pl.ds(row, regions, stride=BLOCK), :]

    def field_rows(row):
        return graph_rows(64 + 2 * row + (me & 1))

    for k, row in enumerate(list(range(16)) + list(range(32, 64))):
        index_ref[block(k), :] = graph_rows(row).astype(jnp.int32)
    order_at, ends_at, rim_ends_at, rows_at, rim_order_at = 16, 32, 42, 46, 47
    for k in range(16):
        reward_ref[block(k), :] = graph_rows(16 + k)

    def give_rims():
        rims = []
        for band in bands:
            values = [ext_ref[block(c, band), :] for c in range(4)]
            rims.append(pick(values, *split(rows_at, band)))
        ext_ref[block(4), :] = swap_rims(jnp.concatenate(rims, axis=0))

    def bellman(last):
        for band in bands:
            ext = [ext_ref[block(c, band), :] for c in range(5)]
            values = []
            for c in range(4):
                scores = [
                    pick(ext, *split(4 * k + c, band)) + reward_ref[block(4 * k + c, band), :]
                    for k in range(4)
                ]
                top = jnp.maximum(
                    jnp.maximum(scores[0], scores[1]), jnp.maximum(scores[2], scores[3])
                )
                grown = [jnp.exp(score - top) for score in scores]
                log_total = top + jnp.log((grown[0] + grown[1]) + (grown[2] + grown[3]))
                mask = (region == dest_region - band) & (lane == dest_node - c * LANES)
                values.append(jnp.where(mask, 0.0, log_total))
                if last:
                    for k in range(4):
                        policy_ref[block(4 * k + c, band), :] = jnp.where(
                            mask, 0.0, jnp.exp(scores[k] - log_total)
                        )
            for c in range(4):
                ext_ref[block(c, band), :] = values[c]

    def arrange():
        for band in bands:
            for half in range(2):
                tables = [
                    policy_ref[block(4 * (i >> 1) + 2 * half + (i & 1), band), :]
                    for i in range(8)
                ]
                for k in range(8 * half, 8 * half + 8):
                    sorted_ref[block(k, band), :] = pick(tables, *split(order_at + k, band))

    def previous(sums):
        rolled = [pltpu.roll(cells, 1, 1) for cells in sums]
        return [
            jnp.where(first_lane, before, cells)
            for before, cells in zip([jnp.zeros((8, LANES), jnp.float32)] + rolled[:-1], rolled)
        ]

    def push():
        for band in bands:
            visits = [ext_ref[block(c, band), :] for c in range(4)]
            for k in range(16):
                low, high = split(order_at + k, band)
                near = visits[2 * (k // 8) : 2 * (k // 8) + 2]
                flow = pick(near, low, high & 1) * sorted_ref[block(k, band), :]
                flow_ref[block(k, band), :] = flow
        for h in range(1):
            sp = pl.ds(h * 512, 512)
            part, total = prefix_and_total(flow_ref[sp, :], steps)
            part_ref[sp, :] = part
            total_ref[sp, :] = total
        def half_sums(band, half, o):
            low, high = split(ends_at + 5 * half + o, band)
            inside = jnp.zeros((8, LANES), jnp.float32)
            before = jnp.zeros((8, LANES), jnp.float32)
            whole = jnp.zeros((8, LANES), jnp.float32)
            for c in range(8):
                row = block(8 * half + c, band)
                here = high == c
                inside = jnp.where(here, along(part_ref[row, :], low), inside)
                whole = jnp.where(here, before, whole)
                before = before + total_ref[row, :]
            return inside, jnp.where(high == 8, before, whole)

        def sums_at(band, o):
            first, second = half_sums(band, 0, o), half_sums(band, 1, o)
            return first[0] + second[0], first[1] + second[1]

        def between(here, back):
            rolled = [pltpu.roll(cells, 1, 1) for cells in here]
            if back is None:
                earlier = [jnp.zeros((8, LANES), jnp.float32)] * 2
            else:
                earlier = [pltpu.roll(cells, 1, 1) for cells in back]
            shifted = [jnp.where(first_lane, a, b) for a, b in zip(earlier, rolled)]
            return (here[0] - shifted[0]) + (here[1] - shifted[1])

        rims, lasts = [], []
        for band in bands:
            lasts.append(sums_at(band, 3))
            rims.append(between(sums_at(band, 4), lasts[-1]))
        arrived = swap_rims(jnp.concatenate(rims, axis=0))
        arrived = [
            along(arrived[band : band + 8], split(rim_order_at, band)[0]) for band in bands
        ]
        part, total = prefix_and_total(jnp.concatenate(arrived, axis=0), steps)
        for k, band in enumerate(bands):
            marks = [None] + [sums_at(band, o) for o in range(3)] + [lasts[k]]
            for c in range(4):
                arrivals = between(marks[c + 1], marks[c])
                ext_ref[block(c, band), :] = anchor_ref[block(c, band), :] + arrivals
        for band in bands:
            sums = []
            for c in range(4):
                low, high = split(rim_ends_at + c, band)
                inside = along(part[band : band + 8], low)
                sums.append(jnp.where(high == 1, total[band : band + 8], inside))
            for c, (here, back) in enumerate(zip(sums, previous(sums))):
                ext_ref[block(c, band), :] = ext_ref[block(c, band), :] + (here - back)

    for c in range(4):
        ext_ref[block(c), :] = field_rows(c)
        anchor_ref[block(c), :] = field_rows(4 + c)
    for sweep in range(SWEEPS):
        give_rims()
        bellman(sweep == SWEEPS - 1)
    for c in range(4):
        out_ref[pl.ds(16 + c, regions, stride=24), :] = ext_ref[block(c), :]
        ext_ref[block(c), :] = anchor_ref[block(c), :]
    arrange()
    lax.fori_loop(0, SWEEPS, lambda sweep, carry: (push(), carry)[1], 0)
    for c in range(4):
        visits = ext_ref[block(c), :]
        out_ref[pl.ds(20 + c, regions, stride=24), :] = visits
        for k in range(4):
            row = 4 * k + c
            out_ref[pl.ds(row, regions, stride=24), :] = policy_ref[block(row), :] * visits


def gradient_kernel(
    back_ref,
    logits_ref,
    feat_ref,
    w_in_ref,
    b_in_ref,
    w_out_ref,
    keep_ref,
    send_ref,
    grad_ref,
    hidden_grad_ref,
):
    chunks = logits_ref.shape[0] // 2
    hid = w_in_ref.shape[1]
    feats = feat_ref.shape[0]
    expected = jnp.sum(back_ref[:, 0:16, :], axis=0)
    gap = logits_ref[chunks : 2 * chunks, :] - expected
    logit_grad = -gap * (1.0 / (1.0 + jnp.exp(-logits_ref[0:chunks, :])))
    w_rows, b_col, w_col = columns_of(w_in_ref, b_in_ref, w_out_ref)
    out_sum = jnp.zeros((hid, LANES), jnp.float32)
    in_grad = jnp.zeros((feats, hid), jnp.float32)
    for first in range(0, chunks, 4):
        cells = []
        for c in range(first, first + 4):
            hidden = hidden_chunk(w_rows, b_col, feat_ref[:, pl.ds(c * LANES, LANES)])
            grad_row = logit_grad[c : c + 1]
            out_sum = out_sum + hidden * grad_row
            hidden_grad = grad_row * w_col * (1.0 - hidden * hidden)
            cells.append(hidden_grad.astype(jnp.bfloat16))
        span = pl.ds(first * LANES, 4 * LANES)
        in_grad = in_grad + contract_lanes(feat_ref[:, span], jnp.concatenate(cells, axis=1))
    grad_ref[0:feats, :] = in_grad
    out_grad = jnp.sum(out_sum.T, axis=0, keepdims=True)
    grad_ref[feats : feats + 8, :] = spread(out_grad, 8)
    first_core = (lax.axis_index("region") & 1) == 0
    left, right = grad_ref[:, 0 : hid // 2], grad_ref[:, hid // 2 : hid]
    keep_ref[...] = jnp.where(first_core, left, right)
    send_ref[...] = jnp.where(first_core, right, left)


def close_kernel(
    scale, half_ref, twin_ref, back_ref, value_ref, visit_ref, in_grad_ref, out_grad_ref
):
    dests, nodes = value_ref.shape
    feats, hid = in_grad_ref.shape
    for c in range(nodes // LANES):
        span = pl.ds(c * LANES, LANES)
        value_ref[:, span] = back_ref[pl.ds(16 + c, dests, stride=24), :]
        visit_ref[:, span] = back_ref[pl.ds(20 + c, dests, stride=24), :]
    first_core = (lax.axis_index("region") & 1) == 0
    half, twin = half_ref[...] * scale, twin_ref[...] * scale
    left = jnp.where(first_core, half, twin)
    right = jnp.where(first_core, twin, half)
    in_grad_ref[:, 0 : hid // 2] = left[0:feats]
    in_grad_ref[:, hid // 2 : hid] = right[0:feats]
    out_grad_ref[:, 0 : hid // 2] = left[feats : feats + 1]
    out_grad_ref[:, hid // 2 : hid] = right[feats : feats + 1]


def by_destination(
    edge_feat,
    w_in,
    b_in,
    w_out,
    targets,
    edge_live,
    boundary_rows,
    dest_nodes,
    anchor_mass,
    prior_value,
    demo_counts,
):
    regions = lax.axis_size("region")
    dests, nodes = prior_value.shape
    edges, feats = edge_feat.shape
    hid = w_in.shape[1]
    chunks = edges // LANES
    f32 = jnp.float32

    def partners(block, *steps):
        return [
            lax.ppermute(block[k], "region", [(i, i ^ step) for i in range(regions)])
            for k, step in enumerate(steps)
        ]

    layer_steps, chip_steps, core_step = (8, 16, 24), (2, 4, 6), 1
    feat_rows = edge_feat.T
    weights = (w_in, b_in.reshape(1, hid), w_out.reshape(1, hid))
    inputs = (
        feat_rows,
        *weights,
        targets.reshape(chunks, LANES),
        edge_live.reshape(chunks, LANES),
        boundary_rows.reshape(1, LANES),
        prior_value,
        anchor_mass,
        demo_counts.reshape(chunks, LANES),
    )
    *send, logits = pl.pallas_call(
        prepare_kernel,
        out_shape=(jax.ShapeDtypeStruct((128, LANES), f32),) * 4
        + (jax.ShapeDtypeStruct((2 * chunks, LANES), f32),),
        in_specs=[pl.BlockSpec(memory_space=pl.ANY)] * len(inputs),
        scratch_shapes=[pltpu.VMEM(cells.shape, cells.dtype) for cells in inputs]
        + [pltpu.SemaphoreType.DMA((len(inputs),))],
        compiler_params=pltpu.CompilerParams(vmem_limit_bytes=62 * MIB),
        name="prepare",
    )(*inputs)
    kept = pl.pallas_call(
        keep_kernel,
        out_shape=jax.ShapeDtypeStruct((128, LANES), f32),
        compiler_params=pltpu.CompilerParams(vmem_limit_bytes=16 * MIB),
        name="keep",
    )(send[0])
    layers = [kept] + partners(send[1:], *layer_steps)
    sends = pl.pallas_call(
        pack_kernel,
        out_shape=(jax.ShapeDtypeStruct((4, 80, LANES), f32),) * 4,
        compiler_params=pltpu.CompilerParams(vmem_limit_bytes=16 * MIB),
        name="pack",
    )(*layers)
    blocks = [sends[0]] + partners(sends[1:], *chip_steps)
    blocks = blocks + partners(blocks, *[core_step] * 4)
    offsets = [layer ^ spot for spot in (0,) + chip_steps for layer in (0,) + layer_steps]
    offsets = offsets + [spot ^ core_step for spot in offsets]
    back = pl.pallas_call(
        functools.partial(sweep_kernel, tuple(offsets)),
        out_shape=jax.ShapeDtypeStruct((regions * 24, LANES), f32),
        in_specs=[
            pl.BlockSpec(memory_space=pltpu.SMEM),
            *[pl.BlockSpec(memory_space=pltpu.VMEM)] * len(blocks),
        ],
        scratch_shapes=[
            pltpu.VMEM((regions * BLOCK, LANES), f32),
            pltpu.VMEM((regions * 48, LANES), jnp.int32),
            pltpu.VMEM((regions * 16, LANES), f32),
            pltpu.VMEM((regions * 5, LANES), f32),
            pltpu.VMEM((regions * 4, LANES), f32),
            pltpu.VMEM((regions * 16, LANES), f32),
            pltpu.VMEM((regions * 16, LANES), f32),
            pltpu.VMEM((regions * 16, LANES), f32),
            pltpu.VMEM((regions * 16, LANES), f32),
            pltpu.VMEM((regions * 16, LANES), f32),
        ],
        compiler_params=pltpu.CompilerParams(vmem_limit_bytes=16 * MIB),
        name="sweeps",
    )(dest_nodes, *blocks)
    back = lax.all_to_all(back.reshape(regions, 24, LANES), "region", 0, 0, tiled=True)
    keep, send = pl.pallas_call(
        gradient_kernel,
        out_shape=(jax.ShapeDtypeStruct((feats + 8, hid // 2), f32),) * 2,
        scratch_shapes=[
            pltpu.VMEM((feats + 8, hid), f32),
            pltpu.VMEM((hid, edges), jnp.bfloat16),
        ],
        compiler_params=pltpu.CompilerParams(vmem_limit_bytes=16 * MIB),
        name="gradient",
    )(back, logits, feat_rows, *weights)
    half = keep + partners([send], core_step)[0]
    for steps in (chip_steps, layer_steps):
        near, far, across = partners([half] * 3, *steps)
        half = (half + near) + (far + across)
    (twin,) = partners([half], core_step)
    values, visits, in_grad, out_grad = pl.pallas_call(
        functools.partial(close_kernel, 1.0 / math.sqrt(edges * regions)),
        out_shape=(
            jax.ShapeDtypeStruct((dests, nodes), f32),
            jax.ShapeDtypeStruct((dests, nodes), f32),
            jax.ShapeDtypeStruct((feats, hid), f32),
            jax.ShapeDtypeStruct((1, hid), f32),
        ),
        compiler_params=pltpu.CompilerParams(vmem_limit_bytes=16 * MIB),
        name="close",
    )(half, twin, back.reshape(dests * 24, LANES))
    return (values, visits, in_grad, out_grad.reshape(hid))


def shards(*arrays):
    boundary_rows, prior_value, targets = arrays[6], arrays[9], arrays[4]
    regions = lax.axis_size("region")
    dests, nodes = prior_value.shape
    fits = (nodes, targets.shape[0], boundary_rows.shape[0]) == (512, 2048, LANES)
    if fits and dests == regions == 32:
        return by_destination(*arrays)
    return ring_sweeps(*arrays)


def solution(mesh):
    placed = (
        P("region", None),
        P(),
        P(),
        P(),
        P("region"),
        P("region"),
        P("region"),
        P(),
        P(None, "region"),
        P(None, "region"),
        P("region"),
    )
    return jax.shard_map(
        shards,
        mesh=mesh,
        in_specs=placed,
        out_specs=(P(None, "region"), P(None, "region"), P(), P()),
        check_vma=False,
    )
```

```python
import functools
import math

import jax
import jax.numpy as jnp
from jax import lax
from jax.experimental import pallas as pl
from jax.experimental.pallas import tpu as pltpu
from jax.sharding import PartitionSpec as P

SWEEPS = 4


NEG_FILL = -1e30


def with_halo(cells, sides, width):
    for axis, dim in sides:
        count = lax.axis_size(axis)
        head = lax.slice_in_dim(cells, 0, width, axis=dim)
        tail = lax.slice_in_dim(cells, cells.shape[dim] - width, cells.shape[dim], axis=dim)
        cells = jnp.concatenate(
            [
                lax.ppermute(tail, axis, [(i, (i + 1) % count) for i in range(count)]),
                cells,
                lax.ppermute(head, axis, [((i + 1) % count, i) for i in range(count)]),
            ],
            axis=dim,
        )
    return cells


def sum_over(cells, axis, count):
    if count & (count - 1):
        return lax.psum(cells, axis)

    def partner(block, step):
        return lax.ppermute(block, axis, [(i, i ^ step) for i in range(count)])

    stride = 1
    while stride < count:
        if stride > 1 and stride * 4 <= count:
            near = partner(cells, stride)
            far = partner(cells, 2 * stride)
            across = partner(cells, 3 * stride)
            cells = (cells + near) + (far + across)
            stride *= 4
        else:
            cells = cells + partner(cells, stride)
            stride *= 2
    return cells


def ring_sweeps(
    edge_feat,
    w_in,
    b_in,
    w_out,
    targets,
    edge_live,
    boundary_rows,
    dest_nodes,
    anchor_mass,
    prior_value,
    demo_counts,
):
    node_count = prior_value.shape[1]
    dest_count = prior_value.shape[0]
    rim_width = boundary_rows.shape[0] // 2
    degree = targets.shape[0] // node_count
    region_pos = lax.axis_index("region")
    node_ids = region_pos * node_count + jnp.arange(node_count, dtype=jnp.int32)
    at_dest = node_ids[None, :] == dest_nodes[:, None]
    keep_flow = jnp.where(at_dest, 0.0, 1.0)
    target_idx = targets.reshape(degree, node_count)
    live_mask = edge_live.reshape(degree, node_count) > 0
    left_rows = boundary_rows[:rim_width]
    right_rows = boundary_rows[rim_width:]
    pre_act = jnp.dot(edge_feat, w_in, preferred_element_type=jnp.float32) + b_in
    hidden = jnp.tanh(pre_act)
    logits = jnp.dot(hidden, w_out, precision=lax.Precision.HIGHEST)
    reward = (-jax.nn.softplus(logits)).reshape(degree, node_count)
    values = prior_value
    masked = None
    log_total = None
    for sweep in range(SWEEPS):
        outgoing = jnp.concatenate([values[:, left_rows], values[:, right_rows]], axis=1)
        extend_padded = with_halo(outgoing, (("region", 1),), rim_width)
        extended = jnp.concatenate(
            [values, extend_padded[:, :rim_width], extend_padded[:, 3 * rim_width :]], axis=1
        )
        masked = jnp.where(live_mask[None], extended[:, target_idx] + reward[None], NEG_FILL)
        row_top = jnp.max(masked, axis=1)
        exp_total = jnp.sum(jnp.exp(masked - row_top[:, None, :]), axis=1)
        log_total = row_top + jnp.log(exp_total)
        values = jnp.where(at_dest, 0.0, log_total)
    policy = jnp.exp(masked - log_total[:, None, :]) * keep_flow[:, None, :]
    flat_targets = target_idx.reshape(-1)
    visits = anchor_mass
    for sweep in range(SWEEPS):
        outflow = (visits[:, None, :] * policy).reshape(dest_count, -1)
        arrivals = (
            jnp.zeros((dest_count, node_count + 2 * rim_width), jnp.float32)
            .at[:, flat_targets]
            .add(outflow)
        )
        padded = with_halo(arrivals[:, node_count:], (("region", 1),), rim_width)
        visits = anchor_mass + arrivals[:, :node_count]
        visits = visits.at[:, left_rows].add(padded[:, :rim_width])
        visits = visits.at[:, right_rows].add(padded[:, 3 * rim_width :])
    expected = jnp.sum(visits[:, None, :] * policy, axis=0).reshape(-1)
    residual_gap = demo_counts.astype(jnp.float32) - expected
    logit_grad = -residual_gap * jax.nn.sigmoid(logits)
    out_grad = jnp.dot(logit_grad, hidden, precision=lax.Precision.HIGHEST)
    hidden_grad = (logit_grad[:, None] * w_out[None, :] * (1.0 - hidden * hidden)).astype(
        jnp.bfloat16
    )
    in_grad = lax.dot_general(
        edge_feat, hidden_grad, (((0,), (0,)), ((), ())), preferred_element_type=jnp.float32
    )
    region_count = lax.axis_size("region")
    grad_scale = 1.0 / math.sqrt(targets.shape[0] * region_count)
    packed = jnp.concatenate([in_grad, out_grad[None]], axis=0)
    total = sum_over(packed, "region", region_count) * grad_scale
    return (values, visits, total[:-1], total[-1])


LANES = 128
BLOCK = 80
MIB = 1024 * 1024


def along(table, index):
    return jnp.take_along_axis(table, index, axis=1, mode="promise_in_bounds")


def spread(row, count):
    return jnp.broadcast_to(row, (count, row.shape[1]))


def lane_iota(rows):
    return lax.broadcasted_iota(jnp.int32, (rows, LANES), 1)


def row_iota(rows):
    return lax.broadcasted_iota(jnp.int32, (rows, LANES), 0)


def contract_lanes(left, right):
    return lax.dot_general(
        left.astype(jnp.bfloat16),
        right.astype(jnp.bfloat16),
        (((1,), (1,)), ((), ())),
        preferred_element_type=jnp.float32,
    )


def three_parts(cells):
    high = cells.astype(jnp.bfloat16)
    rest = cells - high.astype(jnp.float32)
    middle = rest.astype(jnp.bfloat16)
    low = (rest - middle.astype(jnp.float32)).astype(jnp.bfloat16)
    return high, middle, low


def prefix_and_total(cells, steps):
    parts = jnp.concatenate(three_parts(cells), axis=1)
    sums = jnp.dot(parts, steps, preferred_element_type=jnp.float32)
    return sums[:, :LANES], sums[:, LANES:]


def step_matrix():
    src = lax.broadcasted_iota(jnp.int32, (3 * LANES, 2 * LANES), 0) & (LANES - 1)
    dst = lax.broadcasted_iota(jnp.int32, (3 * LANES, 2 * LANES), 1)
    return jnp.where(dst > src, 1.0, 0.0).astype(jnp.bfloat16)


def earlier_equal(keys):
    lane = lane_iota(keys.shape[0])
    found = jnp.zeros(keys.shape, jnp.float32)
    for shift in range(1, LANES):
        same = (pltpu.roll(keys, shift, 1) == keys) & (lane >= shift)
        found = found + jnp.where(same, 1.0, 0.0)
    return found


def one_hot_lanes(row):
    return jnp.where(spread(row, LANES) == row_iota(LANES), 1.0, 0.0)


def histograms(keys):
    low, high = keys & (LANES - 1), keys >> 7
    found = []
    for c in range(keys.shape[0]):
        in_band = jnp.where(spread(high[c : c + 1], 8) == row_iota(8), 1.0, 0.0)
        found.append(contract_lanes(in_band, one_hot_lanes(low[c : c + 1])))
    return found


def order_of(keys, earlier, hists, start):
    rows = keys.shape[0]
    low, high = keys & (LANES - 1), keys >> 7
    ranks = []
    for c in range(rows):
        found = along(start, spread(low[c : c + 1], 8))
        found = jnp.where(spread(high[c : c + 1], 8) == row_iota(8), found, 0.0)
        ranks.append(jnp.sum(found, axis=0, keepdims=True) + earlier[c : c + 1])
        start = start + hists[c]
    lane = lane_iota(8).astype(jnp.float32)
    order = jnp.zeros((8, LANES), jnp.float32)
    for c in range(rows):
        rank = ranks[c].astype(jnp.int32)
        in_band = spread(rank >> 7, 8) == row_iota(8)
        both = jnp.concatenate(
            [jnp.where(in_band, lane, 0.0), jnp.where(in_band, 1.0, 0.0)], axis=0
        )
        got = contract_lanes(both, one_hot_lanes(rank & (LANES - 1)))
        order = order + got[:8] + got[8:] * float(c * LANES)
    return order


def sort_plans(groups, steps):
    hists = [histograms(keys) for keys, _ in groups]
    totals = [functools.reduce(jnp.add, found) for found in hists]
    inside, sums = prefix_and_total(jnp.concatenate(totals, axis=0), steps)
    plans = []
    for k, (keys, earlier) in enumerate(groups):
        before = jnp.zeros((1, LANES), jnp.float32)
        starts = []
        for row in range(8 * k, 8 * k + 8):
            starts.append(inside[row : row + 1] + before)
            before = before + sums[row : row + 1]
        start = jnp.concatenate(starts, axis=0)
        plans.append((order_of(keys, earlier, hists[k], start), start + totals[k]))
    return plans


def columns_of(w_in_ref, b_in_ref, w_out_ref):
    b_col = spread(b_in_ref[...], LANES).T
    w_col = spread(w_out_ref[...], LANES).T
    w_rows = w_in_ref[...].astype(jnp.float32).T.astype(jnp.bfloat16)
    return w_rows, b_col, w_col


def hidden_chunk(w_rows, b_col, feat):
    return jnp.tanh(jnp.dot(w_rows, feat, preferred_element_type=jnp.float32) + b_col)


def prepare_kernel(
    feat_hbm,
    w_in_hbm,
    b_in_hbm,
    w_out_hbm,
    targets_hbm,
    live_hbm,
    rows_hbm,
    prior_hbm,
    anchor_hbm,
    counts_hbm,
    send_0_ref,
    send_1_ref,
    send_2_ref,
    send_3_ref,
    logits_ref,
    feat_ref,
    w_in_ref,
    b_in_ref,
    w_out_ref,
    targets_ref,
    live_ref,
    rows_ref,
    prior_ref,
    anchor_ref,
    counts_ref,
    copy_sem,
):
    chunks = targets_ref.shape[0]
    pairs = (
        (targets_hbm, targets_ref),
        (rows_hbm, rows_ref),
        (w_in_hbm, w_in_ref),
        (b_in_hbm, b_in_ref),
        (w_out_hbm, w_out_ref),
        (feat_hbm, feat_ref),
        (live_hbm, live_ref),
        (prior_hbm, prior_ref),
        (anchor_hbm, anchor_ref),
        (counts_hbm, counts_ref),
    )
    copies = [
        pltpu.make_async_copy(src, dst, copy_sem.at[k]) for k, (src, dst) in enumerate(pairs)
    ]
    for copy in copies:
        copy.start()
    for copy in copies[:2]:
        copy.wait()
    steps = step_matrix()
    targets = targets_ref[...]
    rows = rows_ref[...]
    earlier = earlier_equal(jnp.concatenate([targets, spread(rows, 8)], axis=0))
    groups = []
    for half in range(2):
        picked = [4 * k + 2 * half + c for k in range(chunks // 4) for c in range(2)]
        groups.append(
            [
                jnp.concatenate([cells[j : j + 1] for j in picked], axis=0)
                for cells in (targets, earlier)
            ]
        )
    groups.append((rows, earlier[chunks : chunks + 1]))
    plans = sort_plans(groups, steps)
    rim_order, rim_ends = plans[2]
    for copy in copies[2:]:
        copy.wait()
    w_rows, b_col, w_col = columns_of(w_in_ref, b_in_ref, w_out_ref)
    logit_rows = []
    for c in range(chunks):
        hidden = hidden_chunk(w_rows, b_col, feat_ref[:, pl.ds(c * LANES, LANES)])
        logit_rows.append(jnp.sum(hidden * w_col, axis=0, keepdims=True))
    logits = jnp.concatenate(logit_rows, axis=0)
    logits_ref[0:chunks, :] = logits
    logits_ref[chunks : 2 * chunks, :] = counts_ref[...].astype(jnp.float32)
    reward = -(jnp.maximum(logits, 0.0) + jnp.log1p(jnp.exp(-jnp.abs(logits))))
    reward = jnp.where(live_ref[...] > 0, reward, NEG_FILL)
    graph = jnp.concatenate(
        [
            targets.astype(jnp.float32),
            reward,
            plans[0][0],
            plans[1][0],
            plans[0][1][0:5],
            plans[1][1][0:5],
            rim_ends[0:4],
            rows.astype(jnp.float32),
            rim_order[0:1],
        ],
        axis=0,
    )
    me = lax.axis_index("region")
    layer, chip, by_layer = me >> 3, (me >> 1) & 3, (me & 1) == 0
    for k, send_ref in enumerate((send_0_ref, send_1_ref, send_2_ref, send_3_ref)):
        send_ref[0:64, :] = graph
        dests = pl.ds(pl.multiple_of((layer ^ k) * 8, 8), 8)
        for c in range(4):
            span = pl.ds(c * LANES, LANES)
            for row, cells_ref in ((64 + 8 * c, prior_ref), (96 + 8 * c, anchor_ref)):
                turn = (8 - 2 * (chip ^ k)) & 7
                column = [
                    pltpu.roll(cells_ref[8 * z : 8 * z + 8, span], turn, 0)[0:2]
                    for z in range(4)
                ]
                send_ref[pl.ds(row, 8), :] = jnp.where(
                    by_layer, cells_ref[dests, span], jnp.concatenate(column, axis=0)
                )


def keep_kernel(src_ref, dst_ref):
    dst_ref[...] = src_ref[...]


def pack_kernel(*refs):
    layer_refs, send_refs = refs[:4], refs[4:]
    me = lax.axis_index("region")
    key = jnp.where((me & 1) == 0, (me >> 1) & 3, me >> 3)
    for k, send_ref in enumerate(send_refs):
        start = (key ^ k) * 2
        for z, layer_ref in enumerate(layer_refs):
            send_ref[z, 0:64, :] = layer_ref[0:64, :]
            for c in range(8):
                row = pl.ds(64 + 8 * c + start, 2)
                send_ref[z, pl.ds(64 + 2 * c, 2), :] = layer_ref[row, :]


def sweep_kernel(
    offsets,
    dest_nodes_ref,
    *refs,
):
    block_refs, refs = refs[:8], refs[8:]
    (
        out_ref,
        graph_ref,
    index_ref,
    reward_ref,
    ext_ref,
    anchor_ref,
    policy_ref,
    sorted_ref,
    flow_ref,
    part_ref,
    total_ref,
    ) = refs
    me = lax.axis_index("region")
    dest = dest_nodes_ref[me]
    regions = len(offsets)
    for spot, offset in enumerate(offsets):
        held = jnp.where((me & 1) == 0, *offset)
        place = pl.ds(pl.multiple_of((me ^ held) * BLOCK, BLOCK), BLOCK)
        graph_ref[place, :] = block_refs[spot // 4][spot % 4]
    dest_region, dest_node = dest // 512, dest % 512
    bands = range(0, regions, 8)
    region = lax.broadcasted_iota(jnp.int32, (8, LANES), 0)
    lane = lane_iota(8)
    first_lane = lane == 0
    left_lanes = lane_iota(regions) < LANES // 2
    steps = step_matrix()

    def block(k, band=None):
        if band is None:
            return pl.ds(k * regions, regions)
        return pl.ds(k * regions + band, 8)

    def split(k, band):
        cells = index_ref[block(k, band), :]
        return cells & (LANES - 1), cells >> 7

    def pick(tables, low, high):
        found = along(tables[0], low)
        for c, table in enumerate(tables[1:], 1):
            found = jnp.where(high == c, along(table, low), found)
        return found

    def swap_rims(rims):
        turned = pltpu.roll(rims, LANES // 2, 1)
        return jnp.where(
            left_lanes, pltpu.roll(turned, 1, 0), pltpu.roll(turned, regions - 1, 0)
        )

    def graph_rows(row):
        return graph_ref[pl.ds(row, regions, stride=BLOCK), :]

    def field_rows(row):
        return graph_rows(64 + 2 * row + (me & 1))

    for k, row in enumerate(list(range(16)) + list(range(32, 64))):
        index_ref[block(k), :] = graph_rows(row).astype(jnp.int32)
    order_at, ends_at, rim_ends_at, rows_at, rim_order_at = 16, 32, 42, 46, 47
    for k in range(16):
        reward_ref[block(k), :] = graph_rows(16 + k)

    def give_rims():
        rims = []
        for band in bands:
            values = [ext_ref[block(c, band), :] for c in range(4)]
            rims.append(pick(values, *split(rows_at, band)))
        ext_ref[block(4), :] = swap_rims(jnp.concatenate(rims, axis=0))

    def bellman(last):
        for band in bands:
            ext = [ext_ref[block(c, band), :] for c in range(5)]
            values = []
            for c in range(4):
                scores = [
                    pick(ext, *split(4 * k + c, band)) + reward_ref[block(4 * k + c, band), :]
                    for k in range(4)
                ]
                top = jnp.maximum(
                    jnp.maximum(scores[0], scores[1]), jnp.maximum(scores[2], scores[3])
                )
                grown = [jnp.exp(score - top) for score in scores]
                log_total = top + jnp.log((grown[0] + grown[1]) + (grown[2] + grown[3]))
                mask = (region == dest_region - band) & (lane == dest_node - c * LANES)
                values.append(jnp.where(mask, 0.0, log_total))
                if last:
                    for k in range(4):
                        policy_ref[block(4 * k + c, band), :] = jnp.where(
                            mask, 0.0, jnp.exp(scores[k] - log_total)
                        )
            for c in range(4):
                ext_ref[block(c, band), :] = values[c]

    def arrange():
        for band in bands:
            for half in range(2):
                tables = [
                    policy_ref[block(4 * (i >> 1) + 2 * half + (i & 1), band), :]
                    for i in range(8)
                ]
                for k in range(8 * half, 8 * half + 8):
                    sorted_ref[block(k, band), :] = pick(tables, *split(order_at + k, band))

    def previous(sums):
        rolled = [pltpu.roll(cells, 1, 1) for cells in sums]
        return [
            jnp.where(first_lane, before, cells)
            for before, cells in zip([jnp.zeros((8, LANES), jnp.float32)] + rolled[:-1], rolled)
        ]

    def push():
        for band in bands:
            visits = [ext_ref[block(c, band), :] for c in range(4)]
            for k in range(16):
                low, high = split(order_at + k, band)
                near = visits[2 * (k // 8) : 2 * (k // 8) + 2]
                flow = pick(near, low, high & 1) * sorted_ref[block(k, band), :]
                flow_ref[block(k, band), :] = flow
        for h in range(1):
            sp = pl.ds(h * 512, 512)
            part, total = prefix_and_total(flow_ref[sp, :], steps)
            part_ref[sp, :] = part
            total_ref[sp, :] = total
        def half_sums(band, half, o):
            low, high = split(ends_at + 5 * half + o, band)
            inside = jnp.zeros((8, LANES), jnp.float32)
            before = jnp.zeros((8, LANES), jnp.float32)
            whole = jnp.zeros((8, LANES), jnp.float32)
            for c in range(8):
                row = block(8 * half + c, band)
                here = high == c
                inside = jnp.where(here, along(part_ref[row, :], low), inside)
                whole = jnp.where(here, before, whole)
                before = before + total_ref[row, :]
            return inside, jnp.where(high == 8, before, whole)

        def sums_at(band, o):
            first, second = half_sums(band, 0, o), half_sums(band, 1, o)
            return first[0] + second[0], first[1] + second[1]

        def between(here, back):
            rolled = [pltpu.roll(cells, 1, 1) for cells in here]
            if back is None:
                earlier = [jnp.zeros((8, LANES), jnp.float32)] * 2
            else:
                earlier = [pltpu.roll(cells, 1, 1) for cells in back]
            shifted = [jnp.where(first_lane, a, b) for a, b in zip(earlier, rolled)]
            return (here[0] - shifted[0]) + (here[1] - shifted[1])

        rims, lasts = [], []
        for band in bands:
            lasts.append(sums_at(band, 3))
            rims.append(between(sums_at(band, 4), lasts[-1]))
        arrived = swap_rims(jnp.concatenate(rims, axis=0))
        arrived = [
            along(arrived[band : band + 8], split(rim_order_at, band)[0]) for band in bands
        ]
        part, total = prefix_and_total(jnp.concatenate(arrived, axis=0), steps)
        for k, band in enumerate(bands):
            marks = [None] + [sums_at(band, o) for o in range(3)] + [lasts[k]]
            for c in range(4):
                arrivals = between(marks[c + 1], marks[c])
                ext_ref[block(c, band), :] = anchor_ref[block(c, band), :] + arrivals
        for band in bands:
            sums = []
            for c in range(4):
                low, high = split(rim_ends_at + c, band)
                inside = along(part[band : band + 8], low)
                sums.append(jnp.where(high == 1, total[band : band + 8], inside))
            for c, (here, back) in enumerate(zip(sums, previous(sums))):
                ext_ref[block(c, band), :] = ext_ref[block(c, band), :] + (here - back)

    for c in range(4):
        ext_ref[block(c), :] = field_rows(c)
        anchor_ref[block(c), :] = field_rows(4 + c)
    for sweep in range(SWEEPS):
        give_rims()
        bellman(sweep == SWEEPS - 1)
    for c in range(4):
        out_ref[pl.ds(16 + c, regions, stride=24), :] = ext_ref[block(c), :]
        ext_ref[block(c), :] = anchor_ref[block(c), :]
    arrange()
    lax.fori_loop(0, SWEEPS, lambda sweep, carry: (push(), carry)[1], 0)
    for c in range(4):
        visits = ext_ref[block(c), :]
        out_ref[pl.ds(20 + c, regions, stride=24), :] = visits
        for k in range(4):
            row = 4 * k + c
            out_ref[pl.ds(row, regions, stride=24), :] = policy_ref[block(row), :] * visits


def gradient_kernel(
    back_ref,
    logits_ref,
    feat_ref,
    w_in_ref,
    b_in_ref,
    w_out_ref,
    keep_ref,
    send_ref,
    grad_ref,
    hidden_grad_ref,
):
    chunks = logits_ref.shape[0] // 2
    hid = w_in_ref.shape[1]
    feats = feat_ref.shape[0]
    expected = jnp.sum(back_ref[:, 0:16, :], axis=0)
    gap = logits_ref[chunks : 2 * chunks, :] - expected
    logit_grad = -gap * (1.0 / (1.0 + jnp.exp(-logits_ref[0:chunks, :])))
    w_rows, b_col, w_col = columns_of(w_in_ref, b_in_ref, w_out_ref)
    out_sum = jnp.zeros((hid, LANES), jnp.float32)
    in_grad = jnp.zeros((feats, hid), jnp.float32)
    for first in range(0, chunks, 4):
        cells = []
        for c in range(first, first + 4):
            hidden = hidden_chunk(w_rows, b_col, feat_ref[:, pl.ds(c * LANES, LANES)])
            grad_row = logit_grad[c : c + 1]
            out_sum = out_sum + hidden * grad_row
            hidden_grad = grad_row * w_col * (1.0 - hidden * hidden)
            cells.append(hidden_grad.astype(jnp.bfloat16))
        span = pl.ds(first * LANES, 4 * LANES)
        in_grad = in_grad + contract_lanes(feat_ref[:, span], jnp.concatenate(cells, axis=1))
    grad_ref[0:feats, :] = in_grad
    out_grad = jnp.sum(out_sum.T, axis=0, keepdims=True)
    grad_ref[feats : feats + 8, :] = spread(out_grad, 8)
    first_core = (lax.axis_index("region") & 1) == 0
    left, right = grad_ref[:, 0 : hid // 2], grad_ref[:, hid // 2 : hid]
    keep_ref[...] = jnp.where(first_core, left, right)
    send_ref[...] = jnp.where(first_core, right, left)


def close_kernel(
    scale, half_ref, twin_ref, back_ref, value_ref, visit_ref, in_grad_ref, out_grad_ref
):
    dests, nodes = value_ref.shape
    feats, hid = in_grad_ref.shape
    for c in range(nodes // LANES):
        span = pl.ds(c * LANES, LANES)
        value_ref[:, span] = back_ref[pl.ds(16 + c, dests, stride=24), :]
        visit_ref[:, span] = back_ref[pl.ds(20 + c, dests, stride=24), :]
    first_core = (lax.axis_index("region") & 1) == 0
    half, twin = half_ref[...] * scale, twin_ref[...] * scale
    left = jnp.where(first_core, half, twin)
    right = jnp.where(first_core, twin, half)
    in_grad_ref[:, 0 : hid // 2] = left[0:feats]
    in_grad_ref[:, hid // 2 : hid] = right[0:feats]
    out_grad_ref[:, 0 : hid // 2] = left[feats : feats + 1]
    out_grad_ref[:, hid // 2 : hid] = right[feats : feats + 1]


def by_destination(
    edge_feat,
    w_in,
    b_in,
    w_out,
    targets,
    edge_live,
    boundary_rows,
    dest_nodes,
    anchor_mass,
    prior_value,
    demo_counts,
):
    regions = lax.axis_size("region")
    dests, nodes = prior_value.shape
    edges, feats = edge_feat.shape
    hid = w_in.shape[1]
    chunks = edges // LANES
    f32 = jnp.float32

    def partners(block, *steps):
        return [
            lax.ppermute(block[k], "region", [(i, i ^ step) for i in range(regions)])
            for k, step in enumerate(steps)
        ]

    def mixed_partners(block, even_steps, odd_steps):
        return [
            lax.ppermute(block[k], "region", [(i, i ^ steps[i % 2]) for i in range(regions)])
            for k, steps in enumerate(zip(even_steps, odd_steps))
        ]

    layer_steps, chip_steps, core_step = (8, 16, 24), (2, 4, 6), 1
    feat_rows = edge_feat.T
    weights = (w_in, b_in.reshape(1, hid), w_out.reshape(1, hid))
    inputs = (
        feat_rows,
        *weights,
        targets.reshape(chunks, LANES),
        edge_live.reshape(chunks, LANES),
        boundary_rows.reshape(1, LANES),
        prior_value,
        anchor_mass,
        demo_counts.reshape(chunks, LANES),
    )
    *send, logits = pl.pallas_call(
        prepare_kernel,
        out_shape=(jax.ShapeDtypeStruct((128, LANES), f32),) * 4
        + (jax.ShapeDtypeStruct((2 * chunks, LANES), f32),),
        in_specs=[pl.BlockSpec(memory_space=pl.ANY)] * len(inputs),
        scratch_shapes=[pltpu.VMEM(cells.shape, cells.dtype) for cells in inputs]
        + [pltpu.SemaphoreType.DMA((len(inputs),))],
        compiler_params=pltpu.CompilerParams(vmem_limit_bytes=62 * MIB),
        name="prepare",
    )(*inputs)
    kept = pl.pallas_call(
        keep_kernel,
        out_shape=jax.ShapeDtypeStruct((128, LANES), f32),
        compiler_params=pltpu.CompilerParams(vmem_limit_bytes=16 * MIB),
        name="keep",
    )(send[0])
    layers = [kept] + mixed_partners(send[1:], layer_steps, chip_steps)
    sends = pl.pallas_call(
        pack_kernel,
        out_shape=(jax.ShapeDtypeStruct((4, 80, LANES), f32),) * 4,
        compiler_params=pltpu.CompilerParams(vmem_limit_bytes=16 * MIB),
        name="pack",
    )(*layers)
    blocks = [sends[0]] + mixed_partners(sends[1:], chip_steps, layer_steps)
    blocks = blocks + partners(blocks, *[core_step] * 4)
    paths = [(2 * j ^ 8 * k, 8 * j ^ 2 * k) for j in range(4) for k in range(4)]
    offsets = paths + [(odd ^ core_step, even ^ core_step) for even, odd in paths]
    back = pl.pallas_call(
        functools.partial(sweep_kernel, tuple(offsets)),
        out_shape=jax.ShapeDtypeStruct((regions * 24, LANES), f32),
        in_specs=[
            pl.BlockSpec(memory_space=pltpu.SMEM),
            *[pl.BlockSpec(memory_space=pltpu.VMEM)] * len(blocks),
        ],
        scratch_shapes=[
            pltpu.VMEM((regions * BLOCK, LANES), f32),
            pltpu.VMEM((regions * 48, LANES), jnp.int32),
            pltpu.VMEM((regions * 16, LANES), f32),
            pltpu.VMEM((regions * 5, LANES), f32),
            pltpu.VMEM((regions * 4, LANES), f32),
            pltpu.VMEM((regions * 16, LANES), f32),
            pltpu.VMEM((regions * 16, LANES), f32),
            pltpu.VMEM((regions * 16, LANES), f32),
            pltpu.VMEM((regions * 16, LANES), f32),
            pltpu.VMEM((regions * 16, LANES), f32),
        ],
        compiler_params=pltpu.CompilerParams(vmem_limit_bytes=16 * MIB),
        name="sweeps",
    )(dest_nodes, *blocks)
    back = lax.all_to_all(back.reshape(regions, 24, LANES), "region", 0, 0, tiled=True)
    keep, send = pl.pallas_call(
        gradient_kernel,
        out_shape=(jax.ShapeDtypeStruct((feats + 8, hid // 2), f32),) * 2,
        scratch_shapes=[
            pltpu.VMEM((feats + 8, hid), f32),
            pltpu.VMEM((hid, edges), jnp.bfloat16),
        ],
        compiler_params=pltpu.CompilerParams(vmem_limit_bytes=16 * MIB),
        name="gradient",
    )(back, logits, feat_rows, *weights)
    half = keep + partners([send], core_step)[0]
    for steps in (chip_steps, layer_steps):
        near, far, across = partners([half] * 3, *steps)
        half = (half + near) + (far + across)
    (twin,) = partners([half], core_step)
    values, visits, in_grad, out_grad = pl.pallas_call(
        functools.partial(close_kernel, 1.0 / math.sqrt(edges * regions)),
        out_shape=(
            jax.ShapeDtypeStruct((dests, nodes), f32),
            jax.ShapeDtypeStruct((dests, nodes), f32),
            jax.ShapeDtypeStruct((feats, hid), f32),
            jax.ShapeDtypeStruct((1, hid), f32),
        ),
        compiler_params=pltpu.CompilerParams(vmem_limit_bytes=16 * MIB),
        name="close",
    )(half, twin, back.reshape(dests * 24, LANES))
    return (values, visits, in_grad, out_grad.reshape(hid))


def shards(*arrays):
    boundary_rows, prior_value, targets = arrays[6], arrays[9], arrays[4]
    regions = lax.axis_size("region")
    dests, nodes = prior_value.shape
    fits = (nodes, targets.shape[0], boundary_rows.shape[0]) == (512, 2048, LANES)
    if fits and dests == regions == 32:
        return by_destination(*arrays)
    return ring_sweeps(*arrays)


def solution(mesh):
    placed = (
        P("region", None),
        P(),
        P(),
        P(),
        P("region"),
        P("region"),
        P("region"),
        P(),
        P(None, "region"),
        P(None, "region"),
        P("region"),
    )
    return jax.shard_map(
        shards,
        mesh=mesh,
        in_specs=placed,
        out_specs=(P(None, "region"), P(None, "region"), P(), P()),
        check_vma=False,
    )
```

```python
import functools
import math

import jax
import jax.numpy as jnp
from jax import lax
from jax.experimental import pallas as pl
from jax.experimental.pallas import tpu as pltpu
from jax.sharding import PartitionSpec as P

SWEEPS = 4


NEG_FILL = -1e30


def with_halo(cells, sides, width):
    for axis, dim in sides:
        count = lax.axis_size(axis)
        head = lax.slice_in_dim(cells, 0, width, axis=dim)
        tail = lax.slice_in_dim(cells, cells.shape[dim] - width, cells.shape[dim], axis=dim)
        cells = jnp.concatenate(
            [
                lax.ppermute(tail, axis, [(i, (i + 1) % count) for i in range(count)]),
                cells,
                lax.ppermute(head, axis, [((i + 1) % count, i) for i in range(count)]),
            ],
            axis=dim,
        )
    return cells


def sum_over(cells, axis, count):
    if count & (count - 1):
        return lax.psum(cells, axis)

    def partner(block, step):
        return lax.ppermute(block, axis, [(i, i ^ step) for i in range(count)])

    stride = 1
    while stride < count:
        if stride > 1 and stride * 4 <= count:
            near = partner(cells, stride)
            far = partner(cells, 2 * stride)
            across = partner(cells, 3 * stride)
            cells = (cells + near) + (far + across)
            stride *= 4
        else:
            cells = cells + partner(cells, stride)
            stride *= 2
    return cells


def ring_sweeps(
    edge_feat,
    w_in,
    b_in,
    w_out,
    targets,
    edge_live,
    boundary_rows,
    dest_nodes,
    anchor_mass,
    prior_value,
    demo_counts,
):
    node_count = prior_value.shape[1]
    dest_count = prior_value.shape[0]
    rim_width = boundary_rows.shape[0] // 2
    degree = targets.shape[0] // node_count
    region_pos = lax.axis_index("region")
    node_ids = region_pos * node_count + jnp.arange(node_count, dtype=jnp.int32)
    at_dest = node_ids[None, :] == dest_nodes[:, None]
    keep_flow = jnp.where(at_dest, 0.0, 1.0)
    target_idx = targets.reshape(degree, node_count)
    live_mask = edge_live.reshape(degree, node_count) > 0
    left_rows = boundary_rows[:rim_width]
    right_rows = boundary_rows[rim_width:]
    pre_act = jnp.dot(edge_feat, w_in, preferred_element_type=jnp.float32) + b_in
    hidden = jnp.tanh(pre_act)
    logits = jnp.dot(hidden, w_out, precision=lax.Precision.HIGHEST)
    reward = (-jax.nn.softplus(logits)).reshape(degree, node_count)
    values = prior_value
    masked = None
    log_total = None
    for sweep in range(SWEEPS):
        outgoing = jnp.concatenate([values[:, left_rows], values[:, right_rows]], axis=1)
        extend_padded = with_halo(outgoing, (("region", 1),), rim_width)
        extended = jnp.concatenate(
            [values, extend_padded[:, :rim_width], extend_padded[:, 3 * rim_width :]], axis=1
        )
        masked = jnp.where(live_mask[None], extended[:, target_idx] + reward[None], NEG_FILL)
        row_top = jnp.max(masked, axis=1)
        exp_total = jnp.sum(jnp.exp(masked - row_top[:, None, :]), axis=1)
        log_total = row_top + jnp.log(exp_total)
        values = jnp.where(at_dest, 0.0, log_total)
    policy = jnp.exp(masked - log_total[:, None, :]) * keep_flow[:, None, :]
    flat_targets = target_idx.reshape(-1)
    visits = anchor_mass
    for sweep in range(SWEEPS):
        outflow = (visits[:, None, :] * policy).reshape(dest_count, -1)
        arrivals = (
            jnp.zeros((dest_count, node_count + 2 * rim_width), jnp.float32)
            .at[:, flat_targets]
            .add(outflow)
        )
        padded = with_halo(arrivals[:, node_count:], (("region", 1),), rim_width)
        visits = anchor_mass + arrivals[:, :node_count]
        visits = visits.at[:, left_rows].add(padded[:, :rim_width])
        visits = visits.at[:, right_rows].add(padded[:, 3 * rim_width :])
    expected = jnp.sum(visits[:, None, :] * policy, axis=0).reshape(-1)
    residual_gap = demo_counts.astype(jnp.float32) - expected
    logit_grad = -residual_gap * jax.nn.sigmoid(logits)
    out_grad = jnp.dot(logit_grad, hidden, precision=lax.Precision.HIGHEST)
    hidden_grad = (logit_grad[:, None] * w_out[None, :] * (1.0 - hidden * hidden)).astype(
        jnp.bfloat16
    )
    in_grad = lax.dot_general(
        edge_feat, hidden_grad, (((0,), (0,)), ((), ())), preferred_element_type=jnp.float32
    )
    region_count = lax.axis_size("region")
    grad_scale = 1.0 / math.sqrt(targets.shape[0] * region_count)
    packed = jnp.concatenate([in_grad, out_grad[None]], axis=0)
    total = sum_over(packed, "region", region_count) * grad_scale
    return (values, visits, total[:-1], total[-1])


LANES = 128
BLOCK = 80
MIB = 1024 * 1024


def along(table, index):
    return jnp.take_along_axis(table, index, axis=1, mode="promise_in_bounds")


def spread(row, count):
    return jnp.broadcast_to(row, (count, row.shape[1]))


def lane_iota(rows):
    return lax.broadcasted_iota(jnp.int32, (rows, LANES), 1)


def row_iota(rows):
    return lax.broadcasted_iota(jnp.int32, (rows, LANES), 0)


def contract_lanes(left, right):
    return lax.dot_general(
        left.astype(jnp.bfloat16),
        right.astype(jnp.bfloat16),
        (((1,), (1,)), ((), ())),
        preferred_element_type=jnp.float32,
    )


def three_parts(cells):
    high = cells.astype(jnp.bfloat16)
    rest = cells - high.astype(jnp.float32)
    middle = rest.astype(jnp.bfloat16)
    low = (rest - middle.astype(jnp.float32)).astype(jnp.bfloat16)
    return high, middle, low


def prefix_and_total(cells, steps):
    parts = jnp.concatenate(three_parts(cells), axis=1)
    sums = jnp.dot(parts, steps, preferred_element_type=jnp.float32)
    return sums[:, :LANES], sums[:, LANES:]


def step_matrix():
    src = lax.broadcasted_iota(jnp.int32, (3 * LANES, 2 * LANES), 0) & (LANES - 1)
    dst = lax.broadcasted_iota(jnp.int32, (3 * LANES, 2 * LANES), 1)
    return jnp.where(dst > src, 1.0, 0.0).astype(jnp.bfloat16)


def earlier_equal(keys):
    lane = lane_iota(keys.shape[0])
    found = jnp.zeros(keys.shape, jnp.float32)
    for shift in range(1, LANES):
        same = (pltpu.roll(keys, shift, 1) == keys) & (lane >= shift)
        found = found + jnp.where(same, 1.0, 0.0)
    return found


def one_hot_lanes(row):
    return jnp.where(spread(row, LANES) == row_iota(LANES), 1.0, 0.0)


def histograms(keys):
    low, high = keys & (LANES - 1), keys >> 7
    found = []
    for c in range(keys.shape[0]):
        in_band = jnp.where(spread(high[c : c + 1], 8) == row_iota(8), 1.0, 0.0)
        found.append(contract_lanes(in_band, one_hot_lanes(low[c : c + 1])))
    return found


def order_of(keys, earlier, hists, start):
    rows = keys.shape[0]
    low, high = keys & (LANES - 1), keys >> 7
    ranks = []
    for c in range(rows):
        found = along(start, spread(low[c : c + 1], 8))
        found = jnp.where(spread(high[c : c + 1], 8) == row_iota(8), found, 0.0)
        ranks.append(jnp.sum(found, axis=0, keepdims=True) + earlier[c : c + 1])
        start = start + hists[c]
    lane = lane_iota(8).astype(jnp.float32)
    order = jnp.zeros((8, LANES), jnp.float32)
    for c in range(rows):
        rank = ranks[c].astype(jnp.int32)
        in_band = spread(rank >> 7, 8) == row_iota(8)
        both = jnp.concatenate(
            [jnp.where(in_band, lane, 0.0), jnp.where(in_band, 1.0, 0.0)], axis=0
        )
        got = contract_lanes(both, one_hot_lanes(rank & (LANES - 1)))
        order = order + got[:8] + got[8:] * float(c * LANES)
    return order


def sort_plans(groups, steps):
    hists = [histograms(keys) for keys, _ in groups]
    totals = [functools.reduce(jnp.add, found) for found in hists]
    inside, sums = prefix_and_total(jnp.concatenate(totals, axis=0), steps)
    plans = []
    for k, (keys, earlier) in enumerate(groups):
        before = jnp.zeros((1, LANES), jnp.float32)
        starts = []
        for row in range(8 * k, 8 * k + 8):
            starts.append(inside[row : row + 1] + before)
            before = before + sums[row : row + 1]
        start = jnp.concatenate(starts, axis=0)
        plans.append((order_of(keys, earlier, hists[k], start), start + totals[k]))
    return plans


def columns_of(w_in_ref, b_in_ref, w_out_ref):
    b_col = spread(b_in_ref[...], LANES).T
    w_col = spread(w_out_ref[...], LANES).T
    w_rows = w_in_ref[...].astype(jnp.float32).T.astype(jnp.bfloat16)
    return w_rows, b_col, w_col


def hidden_chunk(w_rows, b_col, feat):
    return jnp.tanh(jnp.dot(w_rows, feat, preferred_element_type=jnp.float32) + b_col)


def prepare_kernel(
    feat_hbm,
    w_in_hbm,
    b_in_hbm,
    w_out_hbm,
    targets_hbm,
    live_hbm,
    rows_hbm,
    prior_hbm,
    anchor_hbm,
    counts_hbm,
    send_0_ref,
    send_1_ref,
    send_2_ref,
    send_3_ref,
    logits_ref,
    feat_ref,
    w_in_ref,
    b_in_ref,
    w_out_ref,
    targets_ref,
    live_ref,
    rows_ref,
    prior_ref,
    anchor_ref,
    counts_ref,
    copy_sem,
):
    chunks = targets_ref.shape[0]
    pairs = (
        (targets_hbm, targets_ref),
        (rows_hbm, rows_ref),
        (w_in_hbm, w_in_ref),
        (b_in_hbm, b_in_ref),
        (w_out_hbm, w_out_ref),
        (feat_hbm, feat_ref),
        (live_hbm, live_ref),
        (prior_hbm, prior_ref),
        (anchor_hbm, anchor_ref),
        (counts_hbm, counts_ref),
    )
    copies = [
        pltpu.make_async_copy(src, dst, copy_sem.at[k]) for k, (src, dst) in enumerate(pairs)
    ]
    for copy in copies:
        copy.start()
    for copy in copies[:2]:
        copy.wait()
    steps = step_matrix()
    targets = targets_ref[...]
    rows = rows_ref[...]
    earlier = earlier_equal(jnp.concatenate([targets, spread(rows, 8)], axis=0))
    groups = []
    for half in range(2):
        picked = [4 * k + 2 * half + c for k in range(chunks // 4) for c in range(2)]
        groups.append(
            [
                jnp.concatenate([cells[j : j + 1] for j in picked], axis=0)
                for cells in (targets, earlier)
            ]
        )
    groups.append((rows, earlier[chunks : chunks + 1]))
    plans = sort_plans(groups, steps)
    rim_order, rim_ends = plans[2]
    for copy in copies[2:]:
        copy.wait()
    w_rows, b_col, w_col = columns_of(w_in_ref, b_in_ref, w_out_ref)
    logit_rows = []
    for c in range(chunks):
        hidden = hidden_chunk(w_rows, b_col, feat_ref[:, pl.ds(c * LANES, LANES)])
        logit_rows.append(jnp.sum(hidden * w_col, axis=0, keepdims=True))
    logits = jnp.concatenate(logit_rows, axis=0)
    logits_ref[0:chunks, :] = logits
    logits_ref[chunks : 2 * chunks, :] = counts_ref[...].astype(jnp.float32)
    reward = -(jnp.maximum(logits, 0.0) + jnp.log1p(jnp.exp(-jnp.abs(logits))))
    reward = jnp.where(live_ref[...] > 0, reward, NEG_FILL)
    graph = jnp.concatenate(
        [
            targets.astype(jnp.float32),
            reward,
            plans[0][0],
            plans[1][0],
            plans[0][1][0:5],
            plans[1][1][0:5],
            rim_ends[0:4],
            rows.astype(jnp.float32),
            rim_order[0:1],
        ],
        axis=0,
    )
    me = lax.axis_index("region")
    layer, chip, by_layer = me >> 3, (me >> 1) & 3, (me & 1) == 0
    for k, send_ref in enumerate((send_0_ref, send_1_ref, send_2_ref, send_3_ref)):
        send_ref[0:64, :] = graph
        dests = pl.ds(pl.multiple_of((layer ^ k) * 8, 8), 8)
        for c in range(4):
            span = pl.ds(c * LANES, LANES)
            for row, cells_ref in ((64 + 8 * c, prior_ref), (96 + 8 * c, anchor_ref)):
                turn = (8 - 2 * (chip ^ k)) & 7
                column = [
                    pltpu.roll(cells_ref[8 * z : 8 * z + 8, span], turn, 0)[0:2]
                    for z in range(4)
                ]
                send_ref[pl.ds(row, 8), :] = jnp.where(
                    by_layer, cells_ref[dests, span], jnp.concatenate(column, axis=0)
                )


def keep_kernel(src_ref, dst_ref):
    dst_ref[...] = src_ref[...]


def pack_kernel(*refs):
    layer_refs, send_refs = refs[:4], refs[4:]
    me = lax.axis_index("region")
    key = jnp.where((me & 1) == 0, (me >> 1) & 3, me >> 3)
    for k, send_ref in enumerate(send_refs):
        turn = (8 - 2 * (key ^ k)) & 7
        for z, layer_ref in enumerate(layer_refs):
            send_ref[z, 0:64, :] = layer_ref[0:64, :]
            pairs = [
                pltpu.roll(layer_ref[64 + 8 * c : 72 + 8 * c, :], turn, 0)[0:2]
                for c in range(8)
            ]
            send_ref[z, 64:80, :] = jnp.concatenate(pairs, axis=0)


def sweep_kernel(
    offsets,
    dest_nodes_ref,
    *refs,
):
    block_refs, refs = refs[:8], refs[8:]
    (
        out_ref,
        graph_ref,
    index_ref,
    reward_ref,
    ext_ref,
    anchor_ref,
    policy_ref,
    sorted_ref,
    flow_ref,
    part_ref,
    total_ref,
    ) = refs
    me = lax.axis_index("region")
    dest = dest_nodes_ref[me]
    regions = len(offsets)
    for spot, offset in enumerate(offsets):
        held = jnp.where((me & 1) == 0, *offset)
        place = pl.ds(pl.multiple_of((me ^ held) * BLOCK, BLOCK), BLOCK)
        graph_ref[place, :] = block_refs[spot // 4][spot % 4]
    dest_region, dest_node = dest // 512, dest % 512
    bands = range(0, regions, 8)
    region = lax.broadcasted_iota(jnp.int32, (8, LANES), 0)
    lane = lane_iota(8)
    first_lane = lane == 0
    left_lanes = lane_iota(regions) < LANES // 2
    steps = step_matrix()

    def block(k, band=None):
        if band is None:
            return pl.ds(k * regions, regions)
        return pl.ds(k * regions + band, 8)

    def split(k, band):
        cells = index_ref[block(k, band), :]
        return cells & (LANES - 1), cells >> 7

    def pick(tables, low, high):
        found = along(tables[0], low)
        for c, table in enumerate(tables[1:], 1):
            found = jnp.where(high == c, along(table, low), found)
        return found

    def swap_rims(rims):
        turned = pltpu.roll(rims, LANES // 2, 1)
        return jnp.where(
            left_lanes, pltpu.roll(turned, 1, 0), pltpu.roll(turned, regions - 1, 0)
        )

    def graph_rows(row):
        return graph_ref[pl.ds(row, regions, stride=BLOCK), :]

    def field_rows(row):
        return jnp.where(
            (me & 1) == 0, graph_rows(64 + 2 * row), graph_rows(65 + 2 * row)
        )

    for k, row in enumerate(list(range(16)) + list(range(32, 64))):
        index_ref[block(k), :] = graph_rows(row).astype(jnp.int32)
    order_at, ends_at, rim_ends_at, rows_at, rim_order_at = 16, 32, 42, 46, 47
    for k in range(16):
        reward_ref[block(k), :] = graph_rows(16 + k)

    def give_rims():
        rims = []
        for band in bands:
            values = [ext_ref[block(c, band), :] for c in range(4)]
            rims.append(pick(values, *split(rows_at, band)))
        ext_ref[block(4), :] = swap_rims(jnp.concatenate(rims, axis=0))

    def bellman(last):
        for band in bands:
            ext = [ext_ref[block(c, band), :] for c in range(5)]
            values = []
            for c in range(4):
                scores = [
                    pick(ext, *split(4 * k + c, band)) + reward_ref[block(4 * k + c, band), :]
                    for k in range(4)
                ]
                top = jnp.maximum(
                    jnp.maximum(scores[0], scores[1]), jnp.maximum(scores[2], scores[3])
                )
                grown = [jnp.exp(score - top) for score in scores]
                log_total = top + jnp.log((grown[0] + grown[1]) + (grown[2] + grown[3]))
                mask = (region == dest_region - band) & (lane == dest_node - c * LANES)
                values.append(jnp.where(mask, 0.0, log_total))
                if last:
                    for k in range(4):
                        policy_ref[block(4 * k + c, band), :] = jnp.where(
                            mask, 0.0, jnp.exp(scores[k] - log_total)
                        )
            for c in range(4):
                ext_ref[block(c, band), :] = values[c]

    def arrange():
        for band in bands:
            for half in range(2):
                tables = [
                    policy_ref[block(4 * (i >> 1) + 2 * half + (i & 1), band), :]
                    for i in range(8)
                ]
                for k in range(8 * half, 8 * half + 8):
                    sorted_ref[block(k, band), :] = pick(tables, *split(order_at + k, band))

    def previous(sums):
        rolled = [pltpu.roll(cells, 1, 1) for cells in sums]
        return [
            jnp.where(first_lane, before, cells)
            for before, cells in zip([jnp.zeros((8, LANES), jnp.float32)] + rolled[:-1], rolled)
        ]

    def push():
        for band in bands:
            visits = [ext_ref[block(c, band), :] for c in range(4)]
            for k in range(16):
                low, high = split(order_at + k, band)
                near = visits[2 * (k // 8) : 2 * (k // 8) + 2]
                flow = pick(near, low, high & 1) * sorted_ref[block(k, band), :]
                flow_ref[block(k, band), :] = flow
        for h in range(1):
            sp = pl.ds(h * 512, 512)
            part, total = prefix_and_total(flow_ref[sp, :], steps)
            part_ref[sp, :] = part
            total_ref[sp, :] = total
        def half_sums(band, half, o):
            low, high = split(ends_at + 5 * half + o, band)
            inside = jnp.zeros((8, LANES), jnp.float32)
            before = jnp.zeros((8, LANES), jnp.float32)
            whole = jnp.zeros((8, LANES), jnp.float32)
            for c in range(8):
                row = block(8 * half + c, band)
                here = high == c
                inside = jnp.where(here, along(part_ref[row, :], low), inside)
                whole = jnp.where(here, before, whole)
                before = before + total_ref[row, :]
            return inside, jnp.where(high == 8, before, whole)

        def sums_at(band, o):
            first, second = half_sums(band, 0, o), half_sums(band, 1, o)
            return first[0] + second[0], first[1] + second[1]

        def between(here, back):
            rolled = [pltpu.roll(cells, 1, 1) for cells in here]
            if back is None:
                earlier = [jnp.zeros((8, LANES), jnp.float32)] * 2
            else:
                earlier = [pltpu.roll(cells, 1, 1) for cells in back]
            shifted = [jnp.where(first_lane, a, b) for a, b in zip(earlier, rolled)]
            return (here[0] - shifted[0]) + (here[1] - shifted[1])

        rims, lasts = [], []
        for band in bands:
            lasts.append(sums_at(band, 3))
            rims.append(between(sums_at(band, 4), lasts[-1]))
        arrived = swap_rims(jnp.concatenate(rims, axis=0))
        arrived = [
            along(arrived[band : band + 8], split(rim_order_at, band)[0]) for band in bands
        ]
        part, total = prefix_and_total(jnp.concatenate(arrived, axis=0), steps)
        for k, band in enumerate(bands):
            marks = [None] + [sums_at(band, o) for o in range(3)] + [lasts[k]]
            for c in range(4):
                arrivals = between(marks[c + 1], marks[c])
                ext_ref[block(c, band), :] = anchor_ref[block(c, band), :] + arrivals
        for band in bands:
            sums = []
            for c in range(4):
                low, high = split(rim_ends_at + c, band)
                inside = along(part[band : band + 8], low)
                sums.append(jnp.where(high == 1, total[band : band + 8], inside))
            for c, (here, back) in enumerate(zip(sums, previous(sums))):
                ext_ref[block(c, band), :] = ext_ref[block(c, band), :] + (here - back)

    for c in range(4):
        ext_ref[block(c), :] = field_rows(c)
        anchor_ref[block(c), :] = field_rows(4 + c)
    for sweep in range(SWEEPS):
        give_rims()
        bellman(sweep == SWEEPS - 1)
    for c in range(4):
        out_ref[pl.ds(16 + c, regions, stride=24), :] = ext_ref[block(c), :]
        ext_ref[block(c), :] = anchor_ref[block(c), :]
    arrange()
    lax.fori_loop(0, SWEEPS, lambda sweep, carry: (push(), carry)[1], 0)
    for c in range(4):
        visits = ext_ref[block(c), :]
        out_ref[pl.ds(20 + c, regions, stride=24), :] = visits
        for k in range(4):
            row = 4 * k + c
            out_ref[pl.ds(row, regions, stride=24), :] = policy_ref[block(row), :] * visits


def gradient_kernel(
    back_ref,
    logits_ref,
    feat_ref,
    w_in_ref,
    b_in_ref,
    w_out_ref,
    keep_ref,
    send_ref,
    grad_ref,
    hidden_grad_ref,
):
    chunks = logits_ref.shape[0] // 2
    hid = w_in_ref.shape[1]
    feats = feat_ref.shape[0]
    expected = jnp.sum(back_ref[:, 0:16, :], axis=0)
    gap = logits_ref[chunks : 2 * chunks, :] - expected
    logit_grad = -gap * (1.0 / (1.0 + jnp.exp(-logits_ref[0:chunks, :])))
    w_rows, b_col, w_col = columns_of(w_in_ref, b_in_ref, w_out_ref)
    out_sum = jnp.zeros((hid, LANES), jnp.float32)
    in_grad = jnp.zeros((feats, hid), jnp.float32)
    for first in range(0, chunks, 4):
        cells = []
        for c in range(first, first + 4):
            hidden = hidden_chunk(w_rows, b_col, feat_ref[:, pl.ds(c * LANES, LANES)])
            grad_row = logit_grad[c : c + 1]
            out_sum = out_sum + hidden * grad_row
            hidden_grad = grad_row * w_col * (1.0 - hidden * hidden)
            cells.append(hidden_grad.astype(jnp.bfloat16))
        span = pl.ds(first * LANES, 4 * LANES)
        in_grad = in_grad + contract_lanes(feat_ref[:, span], jnp.concatenate(cells, axis=1))
    grad_ref[0:feats, :] = in_grad
    out_grad = jnp.sum(out_sum.T, axis=0, keepdims=True)
    grad_ref[feats : feats + 8, :] = spread(out_grad, 8)
    first_core = (lax.axis_index("region") & 1) == 0
    left, right = grad_ref[:, 0 : hid // 2], grad_ref[:, hid // 2 : hid]
    keep_ref[...] = jnp.where(first_core, left, right)
    send_ref[...] = jnp.where(first_core, right, left)


def close_kernel(
    scale, half_ref, twin_ref, back_ref, value_ref, visit_ref, in_grad_ref, out_grad_ref
):
    dests, nodes = value_ref.shape
    feats, hid = in_grad_ref.shape
    for c in range(nodes // LANES):
        span = pl.ds(c * LANES, LANES)
        value_ref[:, span] = back_ref[pl.ds(16 + c, dests, stride=24), :]
        visit_ref[:, span] = back_ref[pl.ds(20 + c, dests, stride=24), :]
    first_core = (lax.axis_index("region") & 1) == 0
    half, twin = half_ref[...] * scale, twin_ref[...] * scale
    left = jnp.where(first_core, half, twin)
    right = jnp.where(first_core, twin, half)
    in_grad_ref[:, 0 : hid // 2] = left[0:feats]
    in_grad_ref[:, hid // 2 : hid] = right[0:feats]
    out_grad_ref[:, 0 : hid // 2] = left[feats : feats + 1]
    out_grad_ref[:, hid // 2 : hid] = right[feats : feats + 1]


def by_destination(
    edge_feat,
    w_in,
    b_in,
    w_out,
    targets,
    edge_live,
    boundary_rows,
    dest_nodes,
    anchor_mass,
    prior_value,
    demo_counts,
):
    regions = lax.axis_size("region")
    dests, nodes = prior_value.shape
    edges, feats = edge_feat.shape
    hid = w_in.shape[1]
    chunks = edges // LANES
    f32 = jnp.float32

    def partners(block, *steps):
        return [
            lax.ppermute(block[k], "region", [(i, i ^ step) for i in range(regions)])
            for k, step in enumerate(steps)
        ]

    def mixed_partners(block, even_steps, odd_steps):
        return [
            lax.ppermute(block[k], "region", [(i, i ^ steps[i % 2]) for i in range(regions)])
            for k, steps in enumerate(zip(even_steps, odd_steps))
        ]

    layer_steps, chip_steps, core_step = (8, 16, 24), (2, 4, 6), 1
    feat_rows = edge_feat.T
    weights = (w_in, b_in.reshape(1, hid), w_out.reshape(1, hid))
    inputs = (
        feat_rows,
        *weights,
        targets.reshape(chunks, LANES),
        edge_live.reshape(chunks, LANES),
        boundary_rows.reshape(1, LANES),
        prior_value,
        anchor_mass,
        demo_counts.reshape(chunks, LANES),
    )
    *send, logits = pl.pallas_call(
        prepare_kernel,
        out_shape=(jax.ShapeDtypeStruct((128, LANES), f32),) * 4
        + (jax.ShapeDtypeStruct((2 * chunks, LANES), f32),),
        in_specs=[pl.BlockSpec(memory_space=pl.ANY)] * len(inputs),
        scratch_shapes=[pltpu.VMEM(cells.shape, cells.dtype) for cells in inputs]
        + [pltpu.SemaphoreType.DMA((len(inputs),))],
        compiler_params=pltpu.CompilerParams(vmem_limit_bytes=62 * MIB),
        name="prepare",
    )(*inputs)
    kept = pl.pallas_call(
        keep_kernel,
        out_shape=jax.ShapeDtypeStruct((128, LANES), f32),
        compiler_params=pltpu.CompilerParams(vmem_limit_bytes=16 * MIB),
        name="keep",
    )(send[0])
    layers = [kept] + mixed_partners(send[1:], layer_steps, chip_steps)
    sends = pl.pallas_call(
        pack_kernel,
        out_shape=(jax.ShapeDtypeStruct((4, 80, LANES), f32),) * 4,
        compiler_params=pltpu.CompilerParams(vmem_limit_bytes=16 * MIB),
        name="pack",
    )(*layers)
    blocks = [sends[0]] + mixed_partners(sends[1:], chip_steps, layer_steps)
    blocks = blocks + partners(blocks, *[core_step] * 4)
    paths = [(2 * j ^ 8 * k, 8 * j ^ 2 * k) for j in range(4) for k in range(4)]
    offsets = paths + [(odd ^ core_step, even ^ core_step) for even, odd in paths]
    back = pl.pallas_call(
        functools.partial(sweep_kernel, tuple(offsets)),
        out_shape=jax.ShapeDtypeStruct((regions * 24, LANES), f32),
        in_specs=[
            pl.BlockSpec(memory_space=pltpu.SMEM),
            *[pl.BlockSpec(memory_space=pltpu.VMEM)] * len(blocks),
        ],
        scratch_shapes=[
            pltpu.VMEM((regions * BLOCK, LANES), f32),
            pltpu.VMEM((regions * 48, LANES), jnp.int32),
            pltpu.VMEM((regions * 16, LANES), f32),
            pltpu.VMEM((regions * 5, LANES), f32),
            pltpu.VMEM((regions * 4, LANES), f32),
            pltpu.VMEM((regions * 16, LANES), f32),
            pltpu.VMEM((regions * 16, LANES), f32),
            pltpu.VMEM((regions * 16, LANES), f32),
            pltpu.VMEM((regions * 16, LANES), f32),
            pltpu.VMEM((regions * 16, LANES), f32),
        ],
        compiler_params=pltpu.CompilerParams(vmem_limit_bytes=16 * MIB),
        name="sweeps",
    )(dest_nodes, *blocks)
    back = lax.all_to_all(back.reshape(regions, 24, LANES), "region", 0, 0, tiled=True)
    keep, send = pl.pallas_call(
        gradient_kernel,
        out_shape=(jax.ShapeDtypeStruct((feats + 8, hid // 2), f32),) * 2,
        scratch_shapes=[
            pltpu.VMEM((feats + 8, hid), f32),
            pltpu.VMEM((hid, edges), jnp.bfloat16),
        ],
        compiler_params=pltpu.CompilerParams(vmem_limit_bytes=16 * MIB),
        name="gradient",
    )(back, logits, feat_rows, *weights)
    half = keep + partners([send], core_step)[0]
    for steps in (chip_steps, layer_steps):
        near, far, across = partners([half] * 3, *steps)
        half = (half + near) + (far + across)
    (twin,) = partners([half], core_step)
    values, visits, in_grad, out_grad = pl.pallas_call(
        functools.partial(close_kernel, 1.0 / math.sqrt(edges * regions)),
        out_shape=(
            jax.ShapeDtypeStruct((dests, nodes), f32),
            jax.ShapeDtypeStruct((dests, nodes), f32),
            jax.ShapeDtypeStruct((feats, hid), f32),
            jax.ShapeDtypeStruct((1, hid), f32),
        ),
        compiler_params=pltpu.CompilerParams(vmem_limit_bytes=16 * MIB),
        name="close",
    )(half, twin, back.reshape(dests * 24, LANES))
    return (values, visits, in_grad, out_grad.reshape(hid))


def shards(*arrays):
    boundary_rows, prior_value, targets = arrays[6], arrays[9], arrays[4]
    regions = lax.axis_size("region")
    dests, nodes = prior_value.shape
    fits = (nodes, targets.shape[0], boundary_rows.shape[0]) == (512, 2048, LANES)
    if fits and dests == regions == 32:
        return by_destination(*arrays)
    return ring_sweeps(*arrays)


def solution(mesh):
    placed = (
        P("region", None),
        P(),
        P(),
        P(),
        P("region"),
        P("region"),
        P("region"),
        P(),
        P(None, "region"),
        P(None, "region"),
        P("region"),
    )
    return jax.shard_map(
        shards,
        mesh=mesh,
        in_specs=placed,
        out_specs=(P(None, "region"), P(None, "region"), P(), P()),
        check_vma=False,
    )
```

```python
import functools
import math

import jax
import jax.numpy as jnp
from jax import lax
from jax.experimental import pallas as pl
from jax.experimental.pallas import tpu as pltpu
from jax.sharding import PartitionSpec as P

SWEEPS = 4


NEG_FILL = -1e30


def with_halo(cells, sides, width):
    for axis, dim in sides:
        count = lax.axis_size(axis)
        head = lax.slice_in_dim(cells, 0, width, axis=dim)
        tail = lax.slice_in_dim(cells, cells.shape[dim] - width, cells.shape[dim], axis=dim)
        cells = jnp.concatenate(
            [
                lax.ppermute(tail, axis, [(i, (i + 1) % count) for i in range(count)]),
                cells,
                lax.ppermute(head, axis, [((i + 1) % count, i) for i in range(count)]),
            ],
            axis=dim,
        )
    return cells


def sum_over(cells, axis, count):
    if count & (count - 1):
        return lax.psum(cells, axis)

    def partner(block, step):
        return lax.ppermute(block, axis, [(i, i ^ step) for i in range(count)])

    stride = 1
    while stride < count:
        if stride > 1 and stride * 4 <= count:
            near = partner(cells, stride)
            far = partner(cells, 2 * stride)
            across = partner(cells, 3 * stride)
            cells = (cells + near) + (far + across)
            stride *= 4
        else:
            cells = cells + partner(cells, stride)
            stride *= 2
    return cells


def ring_sweeps(
    edge_feat,
    w_in,
    b_in,
    w_out,
    targets,
    edge_live,
    boundary_rows,
    dest_nodes,
    anchor_mass,
    prior_value,
    demo_counts,
):
    node_count = prior_value.shape[1]
    dest_count = prior_value.shape[0]
    rim_width = boundary_rows.shape[0] // 2
    degree = targets.shape[0] // node_count
    region_pos = lax.axis_index("region")
    node_ids = region_pos * node_count + jnp.arange(node_count, dtype=jnp.int32)
    at_dest = node_ids[None, :] == dest_nodes[:, None]
    keep_flow = jnp.where(at_dest, 0.0, 1.0)
    target_idx = targets.reshape(degree, node_count)
    live_mask = edge_live.reshape(degree, node_count) > 0
    left_rows = boundary_rows[:rim_width]
    right_rows = boundary_rows[rim_width:]
    pre_act = jnp.dot(edge_feat, w_in, preferred_element_type=jnp.float32) + b_in
    hidden = jnp.tanh(pre_act)
    logits = jnp.dot(hidden, w_out, precision=lax.Precision.HIGHEST)
    reward = (-jax.nn.softplus(logits)).reshape(degree, node_count)
    values = prior_value
    masked = None
    log_total = None
    for sweep in range(SWEEPS):
        outgoing = jnp.concatenate([values[:, left_rows], values[:, right_rows]], axis=1)
        extend_padded = with_halo(outgoing, (("region", 1),), rim_width)
        extended = jnp.concatenate(
            [values, extend_padded[:, :rim_width], extend_padded[:, 3 * rim_width :]], axis=1
        )
        masked = jnp.where(live_mask[None], extended[:, target_idx] + reward[None], NEG_FILL)
        row_top = jnp.max(masked, axis=1)
        exp_total = jnp.sum(jnp.exp(masked - row_top[:, None, :]), axis=1)
        log_total = row_top + jnp.log(exp_total)
        values = jnp.where(at_dest, 0.0, log_total)
    policy = jnp.exp(masked - log_total[:, None, :]) * keep_flow[:, None, :]
    flat_targets = target_idx.reshape(-1)
    visits = anchor_mass
    for sweep in range(SWEEPS):
        outflow = (visits[:, None, :] * policy).reshape(dest_count, -1)
        arrivals = (
            jnp.zeros((dest_count, node_count + 2 * rim_width), jnp.float32)
            .at[:, flat_targets]
            .add(outflow)
        )
        padded = with_halo(arrivals[:, node_count:], (("region", 1),), rim_width)
        visits = anchor_mass + arrivals[:, :node_count]
        visits = visits.at[:, left_rows].add(padded[:, :rim_width])
        visits = visits.at[:, right_rows].add(padded[:, 3 * rim_width :])
    expected = jnp.sum(visits[:, None, :] * policy, axis=0).reshape(-1)
    residual_gap = demo_counts.astype(jnp.float32) - expected
    logit_grad = -residual_gap * jax.nn.sigmoid(logits)
    out_grad = jnp.dot(logit_grad, hidden, precision=lax.Precision.HIGHEST)
    hidden_grad = (logit_grad[:, None] * w_out[None, :] * (1.0 - hidden * hidden)).astype(
        jnp.bfloat16
    )
    in_grad = lax.dot_general(
        edge_feat, hidden_grad, (((0,), (0,)), ((), ())), preferred_element_type=jnp.float32
    )
    region_count = lax.axis_size("region")
    grad_scale = 1.0 / math.sqrt(targets.shape[0] * region_count)
    packed = jnp.concatenate([in_grad, out_grad[None]], axis=0)
    total = sum_over(packed, "region", region_count) * grad_scale
    return (values, visits, total[:-1], total[-1])


LANES = 128
BLOCK = 80
MIB = 1024 * 1024


def along(table, index):
    return jnp.take_along_axis(table, index, axis=1, mode="promise_in_bounds")


def spread(row, count):
    return jnp.broadcast_to(row, (count, row.shape[1]))


def lane_iota(rows):
    return lax.broadcasted_iota(jnp.int32, (rows, LANES), 1)


def row_iota(rows):
    return lax.broadcasted_iota(jnp.int32, (rows, LANES), 0)


def contract_lanes(left, right):
    return lax.dot_general(
        left.astype(jnp.bfloat16),
        right.astype(jnp.bfloat16),
        (((1,), (1,)), ((), ())),
        preferred_element_type=jnp.float32,
    )


def three_parts(cells):
    high = cells.astype(jnp.bfloat16)
    rest = cells - high.astype(jnp.float32)
    middle = rest.astype(jnp.bfloat16)
    low = (rest - middle.astype(jnp.float32)).astype(jnp.bfloat16)
    return high, middle, low


def prefix_and_total(cells, steps):
    parts = jnp.concatenate(three_parts(cells), axis=1)
    sums = jnp.dot(parts, steps, preferred_element_type=jnp.float32)
    return sums[:, :LANES], sums[:, LANES:]


def step_matrix():
    src = lax.broadcasted_iota(jnp.int32, (3 * LANES, 2 * LANES), 0) & (LANES - 1)
    dst = lax.broadcasted_iota(jnp.int32, (3 * LANES, 2 * LANES), 1)
    return jnp.where(dst > src, 1.0, 0.0).astype(jnp.bfloat16)


def earlier_equal(keys):
    lane = lane_iota(keys.shape[0])
    found = jnp.zeros(keys.shape, jnp.float32)
    for shift in range(1, LANES):
        same = (pltpu.roll(keys, shift, 1) == keys) & (lane >= shift)
        found = found + jnp.where(same, 1.0, 0.0)
    return found


def one_hot_lanes(row):
    return jnp.where(spread(row, LANES) == row_iota(LANES), 1.0, 0.0)


def histograms(keys):
    low, high = keys & (LANES - 1), keys >> 7
    found = []
    for c in range(keys.shape[0]):
        in_band = jnp.where(spread(high[c : c + 1], 8) == row_iota(8), 1.0, 0.0)
        found.append(contract_lanes(in_band, one_hot_lanes(low[c : c + 1])))
    return found


def order_of(keys, earlier, hists, start):
    rows = keys.shape[0]
    low, high = keys & (LANES - 1), keys >> 7
    ranks = []
    for c in range(rows):
        found = along(start, spread(low[c : c + 1], 8))
        found = jnp.where(spread(high[c : c + 1], 8) == row_iota(8), found, 0.0)
        ranks.append(jnp.sum(found, axis=0, keepdims=True) + earlier[c : c + 1])
        start = start + hists[c]
    lane = lane_iota(8).astype(jnp.float32)
    order = jnp.zeros((8, LANES), jnp.float32)
    for c in range(rows):
        rank = ranks[c].astype(jnp.int32)
        in_band = spread(rank >> 7, 8) == row_iota(8)
        both = jnp.concatenate(
            [jnp.where(in_band, lane, 0.0), jnp.where(in_band, 1.0, 0.0)], axis=0
        )
        got = contract_lanes(both, one_hot_lanes(rank & (LANES - 1)))
        order = order + got[:8] + got[8:] * float(c * LANES)
    return order


def sort_plans(groups, steps):
    hists = [histograms(keys) for keys, _ in groups]
    totals = [functools.reduce(jnp.add, found) for found in hists]
    inside, sums = prefix_and_total(jnp.concatenate(totals, axis=0), steps)
    plans = []
    for k, (keys, earlier) in enumerate(groups):
        before = jnp.zeros((1, LANES), jnp.float32)
        starts = []
        for row in range(8 * k, 8 * k + 8):
            starts.append(inside[row : row + 1] + before)
            before = before + sums[row : row + 1]
        start = jnp.concatenate(starts, axis=0)
        plans.append((order_of(keys, earlier, hists[k], start), start + totals[k]))
    return plans


def columns_of(w_in_ref, b_in_ref, w_out_ref):
    b_col = spread(b_in_ref[...], LANES).T
    w_col = spread(w_out_ref[...], LANES).T
    w_rows = w_in_ref[...].astype(jnp.float32).T.astype(jnp.bfloat16)
    return w_rows, b_col, w_col


def hidden_chunk(w_rows, b_col, feat):
    return jnp.tanh(jnp.dot(w_rows, feat, preferred_element_type=jnp.float32) + b_col)


def prepare_kernel(
    feat_hbm,
    w_in_hbm,
    b_in_hbm,
    w_out_hbm,
    targets_hbm,
    live_hbm,
    rows_hbm,
    prior_hbm,
    anchor_hbm,
    counts_hbm,
    send_0_ref,
    send_1_ref,
    send_2_ref,
    send_3_ref,
    logits_ref,
    feat_ref,
    w_in_ref,
    b_in_ref,
    w_out_ref,
    targets_ref,
    live_ref,
    rows_ref,
    prior_ref,
    anchor_ref,
    counts_ref,
    copy_sem,
):
    chunks = targets_ref.shape[0]
    pairs = (
        (targets_hbm, targets_ref),
        (rows_hbm, rows_ref),
        (w_in_hbm, w_in_ref),
        (b_in_hbm, b_in_ref),
        (w_out_hbm, w_out_ref),
        (feat_hbm, feat_ref),
        (live_hbm, live_ref),
        (prior_hbm, prior_ref),
        (anchor_hbm, anchor_ref),
        (counts_hbm, counts_ref),
    )
    copies = [
        pltpu.make_async_copy(src, dst, copy_sem.at[k]) for k, (src, dst) in enumerate(pairs)
    ]
    for copy in copies:
        copy.start()
    for copy in copies[:2]:
        copy.wait()
    steps = step_matrix()
    targets = targets_ref[...]
    rows = rows_ref[...]
    earlier = earlier_equal(jnp.concatenate([targets, spread(rows, 8)], axis=0))
    groups = []
    for half in range(2):
        picked = [4 * k + 2 * half + c for k in range(chunks // 4) for c in range(2)]
        groups.append(
            [
                jnp.concatenate([cells[j : j + 1] for j in picked], axis=0)
                for cells in (targets, earlier)
            ]
        )
    groups.append((rows, earlier[chunks : chunks + 1]))
    plans = sort_plans(groups, steps)
    rim_order, rim_ends = plans[2]
    for copy in copies[2:]:
        copy.wait()
    w_rows, b_col, w_col = columns_of(w_in_ref, b_in_ref, w_out_ref)
    logit_rows = []
    for c in range(chunks):
        hidden = hidden_chunk(w_rows, b_col, feat_ref[:, pl.ds(c * LANES, LANES)])
        logit_rows.append(jnp.sum(hidden * w_col, axis=0, keepdims=True))
    logits = jnp.concatenate(logit_rows, axis=0)
    logits_ref[0:chunks, :] = logits
    logits_ref[chunks : 2 * chunks, :] = counts_ref[...].astype(jnp.float32)
    reward = -(jnp.maximum(logits, 0.0) + jnp.log1p(jnp.exp(-jnp.abs(logits))))
    reward = jnp.where(live_ref[...] > 0, reward, NEG_FILL)
    graph = jnp.concatenate(
        [
            targets.astype(jnp.float32),
            reward,
            plans[0][0],
            plans[1][0],
            plans[0][1][0:5],
            plans[1][1][0:5],
            rim_ends[0:4],
            rows.astype(jnp.float32),
            rim_order[0:1],
        ],
        axis=0,
    )
    me = lax.axis_index("region")
    layer, chip, by_layer = me >> 3, (me >> 1) & 3, (me & 1) == 0
    for k, send_ref in enumerate((send_0_ref, send_1_ref, send_2_ref, send_3_ref)):
        send_ref[0:64, :] = graph
        dests = pl.ds(pl.multiple_of((layer ^ k) * 8, 8), 8)
        for c in range(4):
            span = pl.ds(c * LANES, LANES)
            for row, cells_ref in ((64 + 8 * c, prior_ref), (96 + 8 * c, anchor_ref)):
                turn = (8 - 2 * (chip ^ k)) & 7
                column = [
                    pltpu.roll(cells_ref[8 * z : 8 * z + 8, span], turn, 0)[0:2]
                    for z in range(4)
                ]
                send_ref[pl.ds(row, 8), :] = jnp.where(
                    by_layer, cells_ref[dests, span], jnp.concatenate(column, axis=0)
                )


def keep_kernel(src_ref, dst_ref):
    dst_ref[...] = src_ref[...]


def pack_kernel(*refs):
    layer_refs, send_refs = refs[:4], refs[4:]
    me = lax.axis_index("region")
    key = jnp.where((me & 1) == 0, (me >> 1) & 3, me >> 3)
    for k, send_ref in enumerate(send_refs):
        turn = (8 - 2 * (key ^ k)) & 7
        for z, layer_ref in enumerate(layer_refs):
            send_ref[z, 0:64, :] = layer_ref[0:64, :]
            pairs = [
                pltpu.roll(layer_ref[64 + 8 * c : 72 + 8 * c, :], turn, 0)[0:2]
                for c in range(8)
            ]
            send_ref[z, 64:80, :] = jnp.concatenate(pairs, axis=0)


def sweep_kernel(
    offsets,
    dest_nodes_ref,
    *refs,
):
    block_refs, refs = refs[:8], refs[8:]
    (
        out_ref,
        graph_ref,
    index_ref,
    reward_ref,
    ext_ref,
    anchor_ref,
    policy_ref,
    sorted_ref,
    flow_ref,
    part_ref,
    total_ref,
    ) = refs
    me = lax.axis_index("region")
    dest = dest_nodes_ref[me]
    regions = len(offsets)
    for spot, offset in enumerate(offsets):
        held = jnp.where((me & 1) == 0, *offset)
        place = pl.ds(pl.multiple_of((me ^ held) * BLOCK, BLOCK), BLOCK)
        graph_ref[place, :] = block_refs[spot // 4][spot % 4]
    dest_region, dest_node = dest // 512, dest % 512
    bands = range(0, regions, 8)
    region = lax.broadcasted_iota(jnp.int32, (8, LANES), 0)
    lane = lane_iota(8)
    first_lane = lane == 0
    left_lanes = lane_iota(regions) < LANES // 2
    steps = step_matrix()

    def block(k, band=None):
        if band is None:
            return pl.ds(k * regions, regions)
        return pl.ds(k * regions + band, 8)

    def split(k, band):
        cells = index_ref[block(k, band), :]
        return cells & (LANES - 1), cells >> 7

    def pick(tables, low, high):
        found = along(tables[0], low)
        for c, table in enumerate(tables[1:], 1):
            found = jnp.where(high == c, along(table, low), found)
        return found

    def swap_rims(rims):
        turned = pltpu.roll(rims, LANES // 2, 1)
        return jnp.where(
            left_lanes, pltpu.roll(turned, 1, 0), pltpu.roll(turned, regions - 1, 0)
        )

    def graph_rows(row):
        return graph_ref[pl.ds(row, regions, stride=BLOCK), :]

    def field_rows(row):
        return jnp.where(
            (me & 1) == 0, graph_rows(64 + 2 * row), graph_rows(65 + 2 * row)
        )

    for k, row in enumerate(list(range(16)) + list(range(32, 64))):
        index_ref[block(k), :] = graph_rows(row).astype(jnp.int32)
    order_at, ends_at, rim_ends_at, rows_at, rim_order_at = 16, 32, 42, 46, 47
    for k in range(16):
        reward_ref[block(k), :] = graph_rows(16 + k)

    def give_rims():
        rims = []
        for band in bands:
            values = [ext_ref[block(c, band), :] for c in range(4)]
            rims.append(pick(values, *split(rows_at, band)))
        ext_ref[block(4), :] = swap_rims(jnp.concatenate(rims, axis=0))

    def bellman(last):
        for band in bands:
            ext = [ext_ref[block(c, band), :] for c in range(5)]
            values = []
            for c in range(4):
                scores = [
                    pick(ext, *split(4 * k + c, band)) + reward_ref[block(4 * k + c, band), :]
                    for k in range(4)
                ]
                top = jnp.maximum(
                    jnp.maximum(scores[0], scores[1]), jnp.maximum(scores[2], scores[3])
                )
                grown = [jnp.exp(score - top) for score in scores]
                log_total = top + jnp.log((grown[0] + grown[1]) + (grown[2] + grown[3]))
                mask = (region == dest_region - band) & (lane == dest_node - c * LANES)
                values.append(jnp.where(mask, 0.0, log_total))
                if last:
                    for k in range(4):
                        policy_ref[block(4 * k + c, band), :] = jnp.where(
                            mask, 0.0, jnp.exp(scores[k] - log_total)
                        )
            for c in range(4):
                ext_ref[block(c, band), :] = values[c]

    def arrange():
        for band in bands:
            for half in range(2):
                tables = [
                    policy_ref[block(4 * (i >> 1) + 2 * half + (i & 1), band), :]
                    for i in range(8)
                ]
                for k in range(8 * half, 8 * half + 8):
                    sorted_ref[block(k, band), :] = pick(tables, *split(order_at + k, band))

    def previous(sums):
        rolled = [pltpu.roll(cells, 1, 1) for cells in sums]
        return [
            jnp.where(first_lane, before, cells)
            for before, cells in zip([jnp.zeros((8, LANES), jnp.float32)] + rolled[:-1], rolled)
        ]

    def push():
        for band in bands:
            visits = [ext_ref[block(c, band), :] for c in range(4)]
            for k in range(16):
                low, high = split(order_at + k, band)
                near = visits[2 * (k // 8) : 2 * (k // 8) + 2]
                flow = pick(near, low, high & 1) * sorted_ref[block(k, band), :]
                flow_ref[block(k, band), :] = flow
        for h in range(1):
            sp = pl.ds(h * 512, 512)
            part, total = prefix_and_total(flow_ref[sp, :], steps)
            part_ref[sp, :] = part
            total_ref[sp, :] = total
        def half_sums(band, half, o):
            low, high = split(ends_at + 5 * half + o, band)
            inside = jnp.zeros((8, LANES), jnp.float32)
            before = jnp.zeros((8, LANES), jnp.float32)
            whole = jnp.zeros((8, LANES), jnp.float32)
            for c in range(8):
                row = block(8 * half + c, band)
                here = high == c
                inside = jnp.where(here, along(part_ref[row, :], low), inside)
                whole = jnp.where(here, before, whole)
                before = before + total_ref[row, :]
            return inside, jnp.where(high == 8, before, whole)

        def sums_at(band, o):
            first, second = half_sums(band, 0, o), half_sums(band, 1, o)
            return first[0] + second[0], first[1] + second[1]

        def between(here, back):
            rolled = [pltpu.roll(cells, 1, 1) for cells in here]
            if back is None:
                earlier = [jnp.zeros((8, LANES), jnp.float32)] * 2
            else:
                earlier = [pltpu.roll(cells, 1, 1) for cells in back]
            shifted = [jnp.where(first_lane, a, b) for a, b in zip(earlier, rolled)]
            return (here[0] - shifted[0]) + (here[1] - shifted[1])

        rims, lasts = [], []
        for band in bands:
            lasts.append(sums_at(band, 3))
            rims.append(between(sums_at(band, 4), lasts[-1]))
        arrived = swap_rims(jnp.concatenate(rims, axis=0))
        arrived = [
            along(arrived[band : band + 8], split(rim_order_at, band)[0]) for band in bands
        ]
        part, total = prefix_and_total(jnp.concatenate(arrived, axis=0), steps)
        for k, band in enumerate(bands):
            marks = [None] + [sums_at(band, o) for o in range(3)] + [lasts[k]]
            for c in range(4):
                arrivals = between(marks[c + 1], marks[c])
                ext_ref[block(c, band), :] = anchor_ref[block(c, band), :] + arrivals
        for band in bands:
            sums = []
            for c in range(4):
                low, high = split(rim_ends_at + c, band)
                inside = along(part[band : band + 8], low)
                sums.append(jnp.where(high == 1, total[band : band + 8], inside))
            for c, (here, back) in enumerate(zip(sums, previous(sums))):
                ext_ref[block(c, band), :] = ext_ref[block(c, band), :] + (here - back)

    for c in range(4):
        ext_ref[block(c), :] = field_rows(c)
        anchor_ref[block(c), :] = field_rows(4 + c)
    for sweep in range(SWEEPS):
        give_rims()
        bellman(sweep == SWEEPS - 1)
    for c in range(4):
        out_ref[pl.ds(16 + c, regions, stride=24), :] = ext_ref[block(c), :]
        ext_ref[block(c), :] = anchor_ref[block(c), :]
    arrange()
    lax.fori_loop(0, SWEEPS, lambda sweep, carry: (push(), carry)[1], 0)
    for c in range(4):
        visits = ext_ref[block(c), :]
        out_ref[pl.ds(20 + c, regions, stride=24), :] = visits
        for k in range(4):
            row = 4 * k + c
            out_ref[pl.ds(row, regions, stride=24), :] = policy_ref[block(row), :] * visits


def first_half():
    me = lax.axis_index("region")
    return ((me ^ (me >> 1) ^ (me >> 2)) & 1) == 0


def gradient_kernel(
    back_ref,
    logits_ref,
    feat_ref,
    w_in_ref,
    b_in_ref,
    w_out_ref,
    keep_ref,
    send_ref,
    grad_ref,
    hidden_grad_ref,
):
    chunks = logits_ref.shape[0] // 2
    hid = w_in_ref.shape[1]
    feats = feat_ref.shape[0]
    expected = jnp.sum(back_ref[:, 0:16, :], axis=0)
    gap = logits_ref[chunks : 2 * chunks, :] - expected
    logit_grad = -gap * (1.0 / (1.0 + jnp.exp(-logits_ref[0:chunks, :])))
    w_rows, b_col, w_col = columns_of(w_in_ref, b_in_ref, w_out_ref)
    out_sum = jnp.zeros((hid, LANES), jnp.float32)
    in_grad = jnp.zeros((feats, hid), jnp.float32)
    for first in range(0, chunks, 4):
        cells = []
        for c in range(first, first + 4):
            hidden = hidden_chunk(w_rows, b_col, feat_ref[:, pl.ds(c * LANES, LANES)])
            grad_row = logit_grad[c : c + 1]
            out_sum = out_sum + hidden * grad_row
            hidden_grad = grad_row * w_col * (1.0 - hidden * hidden)
            cells.append(hidden_grad.astype(jnp.bfloat16))
        span = pl.ds(first * LANES, 4 * LANES)
        in_grad = in_grad + contract_lanes(feat_ref[:, span], jnp.concatenate(cells, axis=1))
    grad_ref[0:feats, :] = in_grad
    out_grad = jnp.sum(out_sum.T, axis=0, keepdims=True)
    grad_ref[feats : feats + 8, :] = spread(out_grad, 8)
    first_core = first_half()
    left, right = grad_ref[:, 0 : hid // 2], grad_ref[:, hid // 2 : hid]
    keep_ref[...] = jnp.where(first_core, left, right)
    send_ref[...] = jnp.where(first_core, right, left)


def close_kernel(
    scale, half_ref, twin_ref, back_ref, value_ref, visit_ref, in_grad_ref, out_grad_ref
):
    dests, nodes = value_ref.shape
    feats, hid = in_grad_ref.shape
    for c in range(nodes // LANES):
        span = pl.ds(c * LANES, LANES)
        value_ref[:, span] = back_ref[pl.ds(16 + c, dests, stride=24), :]
        visit_ref[:, span] = back_ref[pl.ds(20 + c, dests, stride=24), :]
    first_core = first_half()
    half, twin = half_ref[...] * scale, twin_ref[...] * scale
    left = jnp.where(first_core, half, twin)
    right = jnp.where(first_core, twin, half)
    in_grad_ref[:, 0 : hid // 2] = left[0:feats]
    in_grad_ref[:, hid // 2 : hid] = right[0:feats]
    out_grad_ref[:, 0 : hid // 2] = left[feats : feats + 1]
    out_grad_ref[:, hid // 2 : hid] = right[feats : feats + 1]


def by_destination(
    edge_feat,
    w_in,
    b_in,
    w_out,
    targets,
    edge_live,
    boundary_rows,
    dest_nodes,
    anchor_mass,
    prior_value,
    demo_counts,
):
    regions = lax.axis_size("region")
    dests, nodes = prior_value.shape
    edges, feats = edge_feat.shape
    hid = w_in.shape[1]
    chunks = edges // LANES
    f32 = jnp.float32

    def partners(block, *steps):
        return [
            lax.ppermute(block[k], "region", [(i, i ^ step) for i in range(regions)])
            for k, step in enumerate(steps)
        ]

    def mixed_partners(block, even_steps, odd_steps):
        return [
            lax.ppermute(block[k], "region", [(i, i ^ steps[i % 2]) for i in range(regions)])
            for k, steps in enumerate(zip(even_steps, odd_steps))
        ]

    layer_steps, chip_steps, core_step = (8, 16, 24), (2, 4, 6), 1
    feat_rows = edge_feat.T
    weights = (w_in, b_in.reshape(1, hid), w_out.reshape(1, hid))
    inputs = (
        feat_rows,
        *weights,
        targets.reshape(chunks, LANES),
        edge_live.reshape(chunks, LANES),
        boundary_rows.reshape(1, LANES),
        prior_value,
        anchor_mass,
        demo_counts.reshape(chunks, LANES),
    )
    *send, logits = pl.pallas_call(
        prepare_kernel,
        out_shape=(jax.ShapeDtypeStruct((128, LANES), f32),) * 4
        + (jax.ShapeDtypeStruct((2 * chunks, LANES), f32),),
        in_specs=[pl.BlockSpec(memory_space=pl.ANY)] * len(inputs),
        scratch_shapes=[pltpu.VMEM(cells.shape, cells.dtype) for cells in inputs]
        + [pltpu.SemaphoreType.DMA((len(inputs),))],
        compiler_params=pltpu.CompilerParams(vmem_limit_bytes=62 * MIB),
        name="prepare",
    )(*inputs)
    kept = pl.pallas_call(
        keep_kernel,
        out_shape=jax.ShapeDtypeStruct((128, LANES), f32),
        compiler_params=pltpu.CompilerParams(vmem_limit_bytes=16 * MIB),
        name="keep",
    )(send[0])
    layers = [kept] + mixed_partners(send[1:], layer_steps, chip_steps)
    sends = pl.pallas_call(
        pack_kernel,
        out_shape=(jax.ShapeDtypeStruct((4, 80, LANES), f32),) * 4,
        compiler_params=pltpu.CompilerParams(vmem_limit_bytes=16 * MIB),
        name="pack",
    )(*layers)
    blocks = [sends[0]] + mixed_partners(sends[1:], chip_steps, layer_steps)
    blocks = blocks + partners(blocks, *[core_step] * 4)
    paths = [(2 * j ^ 8 * k, 8 * j ^ 2 * k) for j in range(4) for k in range(4)]
    offsets = paths + [(odd ^ core_step, even ^ core_step) for even, odd in paths]
    back = pl.pallas_call(
        functools.partial(sweep_kernel, tuple(offsets)),
        out_shape=jax.ShapeDtypeStruct((regions * 24, LANES), f32),
        in_specs=[
            pl.BlockSpec(memory_space=pltpu.SMEM),
            *[pl.BlockSpec(memory_space=pltpu.VMEM)] * len(blocks),
        ],
        scratch_shapes=[
            pltpu.VMEM((regions * BLOCK, LANES), f32),
            pltpu.VMEM((regions * 48, LANES), jnp.int32),
            pltpu.VMEM((regions * 16, LANES), f32),
            pltpu.VMEM((regions * 5, LANES), f32),
            pltpu.VMEM((regions * 4, LANES), f32),
            pltpu.VMEM((regions * 16, LANES), f32),
            pltpu.VMEM((regions * 16, LANES), f32),
            pltpu.VMEM((regions * 16, LANES), f32),
            pltpu.VMEM((regions * 16, LANES), f32),
            pltpu.VMEM((regions * 16, LANES), f32),
        ],
        compiler_params=pltpu.CompilerParams(vmem_limit_bytes=16 * MIB),
        name="sweeps",
    )(dest_nodes, *blocks)
    back = lax.all_to_all(back.reshape(regions, 24, LANES), "region", 0, 0, tiled=True)
    keep, send = pl.pallas_call(
        gradient_kernel,
        out_shape=(jax.ShapeDtypeStruct((feats + 8, hid // 2), f32),) * 2,
        scratch_shapes=[
            pltpu.VMEM((feats + 8, hid), f32),
            pltpu.VMEM((hid, edges), jnp.bfloat16),
        ],
        compiler_params=pltpu.CompilerParams(vmem_limit_bytes=16 * MIB),
        name="gradient",
    )(back, logits, feat_rows, *weights)
    half = keep + partners([send], core_step)[0]
    for steps in ((3, 5, 6), layer_steps):
        near, far, across = partners([half] * 3, *steps)
        half = (half + near) + (far + across)
    (twin,) = partners([half], core_step)
    values, visits, in_grad, out_grad = pl.pallas_call(
        functools.partial(close_kernel, 1.0 / math.sqrt(edges * regions)),
        out_shape=(
            jax.ShapeDtypeStruct((dests, nodes), f32),
            jax.ShapeDtypeStruct((dests, nodes), f32),
            jax.ShapeDtypeStruct((feats, hid), f32),
            jax.ShapeDtypeStruct((1, hid), f32),
        ),
        compiler_params=pltpu.CompilerParams(vmem_limit_bytes=16 * MIB),
        name="close",
    )(half, twin, back.reshape(dests * 24, LANES))
    return (values, visits, in_grad, out_grad.reshape(hid))


def shards(*arrays):
    boundary_rows, prior_value, targets = arrays[6], arrays[9], arrays[4]
    regions = lax.axis_size("region")
    dests, nodes = prior_value.shape
    fits = (nodes, targets.shape[0], boundary_rows.shape[0]) == (512, 2048, LANES)
    if fits and dests == regions == 32:
        return by_destination(*arrays)
    return ring_sweeps(*arrays)


def solution(mesh):
    placed = (
        P("region", None),
        P(),
        P(),
        P(),
        P("region"),
        P("region"),
        P("region"),
        P(),
        P(None, "region"),
        P(None, "region"),
        P("region"),
    )
    return jax.shard_map(
        shards,
        mesh=mesh,
        in_specs=placed,
        out_specs=(P(None, "region"), P(None, "region"), P(), P()),
        check_vma=False,
    )
```
